32 devices in a mesh: dp: 8 (over z, x), tensor: 4 (over y, core).
Axes of the slice: x: 2, y: 2, z: 4, core: 2. Of those that a mesh axis runs over, the one named last changes fastest.
Arguments:
- image: bfloat16 [16, 1024, 1536], P('dp', 'tensor'), may hold values from -6 to 6
- text: bfloat16 [16, 152, 1536], P('dp', 'tensor'), may hold values from -6 to 6
- cond: bfloat16 [16, 1536], P('dp'), may hold values from -6 to 6
- teacher_image: bfloat16 [16, 1024, 1536], P('dp', 'tensor'), may hold values from -8 to 8
- teacher_text: bfloat16 [16, 152, 1536], P('dp', 'tensor'), may hold values from -8 to 8
- grad_image: bfloat16 [16, 1024, 1536], P('dp', 'tensor'), may hold values from -8 to 8
- grad_text: bfloat16 [16, 152, 1536], P('dp', 'tensor'), may hold values from -8 to 8
- live: int32 [16], P('dp'), may hold values from 0 to 1, as said below
- w_mod: bfloat16 [2, 1536, 9216], P(None, 'dp', 'tensor'), may hold values from -0.15625 to 0.15625
- w_qkv: bfloat16 [2, 3, 24, 64, 1536], P(None, None, 'tensor', 'dp'), may hold values from -0.15625 to 0.15625
- w_out: bfloat16 [2, 24, 64, 1536], P(None, 'tensor', 'dp'), may hold values from -3 to 3
- w_up: bfloat16 [2, 1536, 6144], P(None, 'dp', 'tensor'), may hold values from -0.15625 to 0.15625
- w_down: bfloat16 [2, 1536, 6144], P(None, 'dp', 'tensor'), may hold values from -0.078125 to 0.078125
Outputs:
- loss: float32 [], replicated
- grad_mod: float32 [2, 1536, 9216], P(None, 'dp', 'tensor')
- grad_qkv: float32 [2, 3, 24, 64, 1536], P(None, None, 'tensor', 'dp')
- grad_out: float32 [2, 24, 64, 1536], P(None, 'tensor', 'dp')
- grad_up: float32 [2, 1536, 6144], P(None, 'dp', 'tensor')
- grad_down: float32 [2, 1536, 6144], P(None, 'dp', 'tensor')
- grad_image_in: float32 [16, 1024, 1536], P('dp', 'tensor')
- grad_text_in: float32 [16, 152, 1536], P('dp', 'tensor')
- grad_cond: float32 [16, 1536], P('dp')
The draws below stay inside these ranges and needn't reach their ends.
Inputs may be any that keep to these rules, and one draw needn't show every extreme that they name: Slot 2 * r + j lies on data rank r. On each rank the live slots are the first ones, 1 to 2 of them. Rank r and rank r + 8 / 2 together hold 3 live slots, so some rank has all 2 live.
All inputs are finite; a program needn't handle non-finite values.
Results may differ from the reference program's by a relative error of at most 0.0085.
The reference program's roundings to bfloat16 on the way count: a program that leaves them out, or rounds other values in their place, can miss the bound.
Values may be sent and summed in bfloat16 or wider, within the bound.
A program may use at most 384 MiB of HBM per device.

```python
import jax
import jax.numpy as jnp
from jax import lax

D = 1536
HEADS = 24
HD = 64
FF = 6144
LI = 1024
LT = 152
SLOTS = 2
SEQS = 16


def draw_live(key, part):
    key = jax.random.fold_in(key, 5)
    ranks = SEQS // SLOTS
    half = ranks // 2
    first = jax.random.randint(key, (half,), 1, SLOTS + 1)
    second = SLOTS + 1 - first
    counts = jnp.concatenate([first, second], 0)
    places = jnp.arange(SLOTS)
    return (places[None, :] < counts[:, None]).astype(jnp.int32).reshape(SEQS)


def layered(common, weight, noise):
    return jnp.clip(weight[:, None, None] * common[None, None, :] + noise, -8.0, 8.0)


def feature_field(key, rows):
    key_common, key_weight, key_noise = jax.random.split(key, 3)
    common = jax.random.normal(key_common, (D,), jnp.float32)
    weight = jax.random.uniform(key_weight, (SEQS,), jnp.float32, 0.75, 1.25)
    noise = jnp.clip(jax.random.normal(key_noise, (SEQS, rows, D), jnp.float32), -4.0, 4.0)
    return layered(common, weight, noise)


def draw_teacher_image(key, part):
    key = jax.random.fold_in(key, 21)
    return feature_field(key, LI).astype(jnp.bfloat16)


def draw_teacher_text(key, part):
    key = jax.random.fold_in(key, 22)
    return feature_field(key, LT).astype(jnp.bfloat16)


def draw_grad_image(key, part):
    key = jax.random.fold_in(key, 23)
    return feature_field(key, LI).astype(jnp.bfloat16)


def draw_grad_text(key, part):
    key = jax.random.fold_in(key, 24)
    return feature_field(key, LT).astype(jnp.bfloat16)


def shard_levels(own_key, extent, cuts, least, high):
    def one(dim, blocks):
        draws = jax.random.uniform(jax.random.fold_in(jax.random.fold_in(own_key, 6), dim), (blocks,), jnp.float32, least / len(cuts), high / len(cuts))
        return jnp.repeat(jnp.exp(draws), extent[dim] // blocks).reshape((-1,) + (1,) * (len(extent) - dim - 1))

    factor_of = one(*cuts[0])
    for cut in cuts[1:]:
        factor_of = factor_of * one(*cut)
    return factor_of


def normal_values(key, dims, deviation, limit, cuts=(), kind=jnp.bfloat16):
    values = jax.random.normal(key, dims, jnp.float32) * deviation
    if len(cuts) > 0:
        values = shard_levels(key, dims, cuts, -0.22, 0.18) * values
    return jnp.clip(values, min=-limit, max=limit).astype(kind)


def setup_inputs(seed: int = 0) -> dict:
    streams_of = jax.random.split(jax.random.key(seed), 14)
    image = normal_values(streams_of[0], (SEQS, LI, D), 1.0, 6.0, ((0, 8), (1, 4)))
    text = normal_values(streams_of[1], (SEQS, LT, D), 1.0, 6.0, ((0, 8), (1, 4)))
    cond = normal_values(streams_of[2], (SEQS, D), 1.0, 6.0, ((0, 8),))
    teacher_image = draw_teacher_image(jax.random.fold_in(streams_of[13], 71), 0)
    teacher_text = draw_teacher_text(jax.random.fold_in(streams_of[13], 71), 0)
    grad_image = draw_grad_image(jax.random.fold_in(streams_of[13], 71), 0)
    grad_text = draw_grad_text(jax.random.fold_in(streams_of[13], 71), 0)
    live = draw_live(jax.random.fold_in(streams_of[13], 71), 0)
    w_mod = normal_values(streams_of[8], (2, D, 6 * D), D ** -0.5, 0.15625, ((1, 8), (2, 4)))
    w_qkv = normal_values(streams_of[9], (2, 3, HEADS, HD, D), D ** -0.5, 0.15625, ((2, 4), (3, 8)))
    w_out = normal_values(streams_of[10], (2, HEADS, HD, D), 4 ** -0.5, 3.0, ((1, 4), (2, 8)))
    w_up = normal_values(streams_of[11], (2, D, FF), D ** -0.5, 0.15625, ((1, 8), (2, 4)))
    w_down = normal_values(streams_of[12], (2, D, FF), FF ** -0.5, 0.078125, ((1, 8), (2, 4)))
    return dict(image=image, text=text, cond=cond, teacher_image=teacher_image, teacher_text=teacher_text, grad_image=grad_image, grad_text=grad_text, live=live, w_mod=w_mod, w_qkv=w_qkv, w_out=w_out, w_up=w_up, w_down=w_down)


@jax.custom_vjp
def low(v):
    return lax.optimization_barrier(v.astype(jnp.bfloat16)).astype(jnp.float32)

@jax.custom_vjp
def low_back(v):
    return v

def low_keep(v):
    return (low(v), None)

def low_pass(kept, grad):
    return (grad,)

def back_keep(v):
    return (v, None)

def back_low(kept, grad):
    return (low(grad),)
low.defvjp(low_keep, low_pass)
low_back.defvjp(back_keep, back_low)
norm_eps = 1e-06

def layer_norm(values):
    center = lax.optimization_barrier(jnp.mean(values, -1, keepdims=True))
    spread = lax.optimization_barrier(jnp.mean(jnp.square(values - center), -1, keepdims=True))
    return (values - center) * lax.rsqrt(spread + norm_eps)

def matmul(left, right):
    return jnp.dot(left, right, precision=lax.Precision.HIGHEST, preferred_element_type=jnp.float32)

def one_sequence(weights, pieces):
    w_mod, w_qkv, w_out, w_up, w_down = weights
    x_text, x_image, cond_vec = pieces
    act = low(jax.nn.silu(cond_vec))
    streams = (x_text, x_image)
    mods = []
    joined = []
    for s in range(2):
        mod = low_back(matmul(act, w_mod[s])).reshape(6, D)
        normed = low(layer_norm(streams[s]) * (1.0 + mod[1]) + mod[0])
        joined.append(low_back(low(matmul(normed, w_qkv[s].reshape(3 * D, D).T))))
        mods.append(mod)
    packed = jnp.concatenate(joined, 0).reshape(LT + LI, 3, HEADS, HD)
    query, key, value = (packed[:, 0], packed[:, 1], packed[:, 2])
    scores = low_back(jnp.einsum('qhe,khe->hqk', query, key, precision=lax.Precision.HIGHEST) * HD ** (-0.5))
    probs = low(jax.nn.softmax(scores, -1))
    attended = jnp.einsum('hqk,khe->qhe', probs, value, precision=lax.Precision.HIGHEST).reshape(LT + LI, D)
    attended = low_back(low(attended))
    parts = (attended[:LT], attended[LT:])
    results = []
    for s in range(2):
        mod = mods[s]
        middle = streams[s] + mod[2] * low_back(matmul(parts[s], w_out[s].reshape(D, D)))
        normed = low(layer_norm(middle) * (1.0 + mod[4]) + mod[3])
        before = low_back(matmul(normed, w_up[s]))
        hidden = low(jax.nn.gelu(before, approximate=True))
        results.append(middle + mod[5] * low_back(matmul(hidden, w_down[s].T)))
    return (results[0], results[1])

def reference(image, text, cond, teacher_image, teacher_text, grad_image, grad_text, live, w_mod, w_qkv, w_out, w_up, w_down):
    weights = (w_mod.astype(jnp.float32), w_qkv.astype(jnp.float32), w_out.astype(jnp.float32), w_up.astype(jnp.float32), w_down.astype(jnp.float32))
    stepper = jax.checkpoint(one_sequence)

    def forward(params, x_text, x_image, cond_f):
        return lax.map(lambda pieces: stepper(params, pieces), (x_text, x_image, cond_f))
    outputs, pull = jax.vjp(forward, weights, text.astype(jnp.float32), image.astype(jnp.float32), cond.astype(jnp.float32))
    out_text, out_image = outputs
    mask = live.astype(jnp.float32)[:, None, None]
    err_text = out_text - teacher_text.astype(jnp.float32)
    err_image = out_image - teacher_image.astype(jnp.float32)
    count = jnp.sum(live).astype(jnp.float32) * (LI + LT)
    loss = (jnp.sum(mask * err_text * err_text) + jnp.sum(mask * err_image * err_image)) / (count * D)
    cot_text = mask * (grad_text.astype(jnp.float32) + 2.0 * err_text)
    cot_image = mask * (grad_image.astype(jnp.float32) + 2.0 * err_image)
    grads, g_text, g_image, g_cond = pull((cot_text, cot_image))
    return (loss, grads[0], grads[1], grads[2], grads[3], grads[4], g_image, g_text, g_cond)
```

```python
import math
from functools import partial

import jax
import jax.numpy as jnp
from jax import lax
from jax.experimental import pallas as pl
from jax.experimental.pallas import tpu as pltpu
from jax.sharding import PartitionSpec as P

norm_eps = 1e-06

LOG2E = math.log2(math.e)
HEAD = 64


def nt(a, b):
    return lax.dot_general(a, b, (((1,), (1,)), ((), ())), preferred_element_type=jnp.float32)


def nn(a, b):
    return jnp.dot(a, b, preferred_element_type=jnp.float32)


def query_blocks(rows_img, rows_txt):
    step = 256 if rows_img % 256 == 0 else rows_img
    return [(0, s, step) for s in range(0, rows_img, step)] + [(1, 0, rows_txt)]


def pad_bias(rows, block, valid):
    place = lax.broadcasted_iota(jnp.int32, (rows, 1), 0)
    return jnp.where(lax.rem(place, block) < valid, 0.0, -1e30).astype(jnp.float32)


def attend_kernel(block, valid, qi, ki, vi, qt, kt, vt, oi, ot, lse):
    factor = HEAD**-0.5
    low = lax.broadcasted_iota(jnp.int32, (1, 2 * HEAD), 1) < HEAD
    zero = jnp.zeros((), jnp.bfloat16)
    bias = pad_bias(qt.shape[0], block, valid)
    vit, vtt = vi[...].T, vt[...].T
    keys = []
    for h in range(2):
        mask = low if h == 0 else ~low
        keys.append((jnp.where(mask, ki[...], zero), jnp.where(mask, kt[...], zero)))
    at = 0
    for which, start, size in query_blocks(qi.shape[0], qt.shape[0]):
        src, dst = (qi, oi) if which == 0 else (qt, ot)
        q = src[start : start + size, :]
        parts = []
        for h in range(2):
            s_i = nt(keys[h][0], q)
            s_t = nt(keys[h][1], q) + bias
            top = jnp.maximum(
                jnp.max(s_i, 0, keepdims=True), jnp.max(s_t, 0, keepdims=True)
            )
            e_i = jnp.exp2((s_i - top) * (factor * LOG2E))
            e_t = jnp.exp2((s_t - top) * (factor * LOG2E))
            total = jnp.sum(e_i, 0, keepdims=True) + jnp.sum(e_t, 0, keepdims=True)
            inv = 1.0 / total
            p_i = (e_i * inv).astype(jnp.bfloat16)
            p_t = (e_t * inv).astype(jnp.bfloat16)
            rows = slice(h * HEAD, (h + 1) * HEAD)
            parts.append(nn(vit[rows], p_i) + nn(vtt[rows], p_t))
            lse[0, h : h + 1, at : at + size] = top * (factor * LOG2E) + jnp.log2(total)
        dst[start : start + size, :] = jnp.concatenate(parts, 0).T.astype(jnp.bfloat16)
        at += size


def back_kernel(block, valid, qi, ki, vi, qt, kt, vt, gi, gt, lse,
                dqi, dki, dvi, dqt, dkt, dvt, aki, avi, akt, avt):
    factor = HEAD**-0.5
    low = lax.broadcasted_iota(jnp.int32, (1, 2 * HEAD), 1) < HEAD
    zero = jnp.zeros((), jnp.bfloat16)
    bias = pad_bias(qt.shape[0], block, valid)
    kit, ktt = ki[...].T, kt[...].T
    masks = [low, ~low]
    at = 0
    first = True
    for which, start, size in query_blocks(qi.shape[0], qt.shape[0]):
        q_ref, g_ref, d_ref = (qi, gi, dqi) if which == 0 else (qt, gt, dqt)
        q, g = q_ref[start : start + size, :], g_ref[start : start + size, :]
        parts = []
        for h in range(2):
            q_h, g_h = jnp.where(masks[h], q, zero), jnp.where(masks[h], g, zero)
            stat = lse[0, h : h + 1, at : at + size]
            p_i = jnp.exp2(nt(ki[...], q_h) * (factor * LOG2E) - stat)
            p_t = jnp.exp2((nt(kt[...], q_h) + bias) * (factor * LOG2E) - stat)
            d_i, d_t = nt(vi[...], g_h), nt(vt[...], g_h)
            delta = jnp.sum(d_i * p_i, 0, keepdims=True) + jnp.sum(d_t * p_t, 0, keepdims=True)
            s_i = (p_i * (d_i - delta)).astype(jnp.bfloat16)
            s_t = (p_t * (d_t - delta)).astype(jnp.bfloat16)
            v_i = nn(p_i.astype(jnp.bfloat16), g_h)
            v_t = nn(p_t.astype(jnp.bfloat16), g_h)
            k_i = nn(s_i, q_h)
            k_t = nn(s_t, q_h)
            if first:
                avi[...], avt[...], aki[...], akt[...] = v_i, v_t, k_i, k_t
                first = False
            else:
                avi[...] += v_i
                avt[...] += v_t
                aki[...] += k_i
                akt[...] += k_t
            rows = slice(h * HEAD, (h + 1) * HEAD)
            parts.append(nn(kit[rows], s_i) + nn(ktt[rows], s_t))
        d_ref[start : start + size, :] = (jnp.concatenate(parts, 0).T * factor).astype(jnp.bfloat16)
        at += size
    dki[...] = (aki[...] * factor).astype(jnp.bfloat16)
    dkt[...] = (akt[...] * factor).astype(jnp.bfloat16)
    dvi[...] = avi[...].astype(jnp.bfloat16)
    dvt[...] = avt[...].astype(jnp.bfloat16)


def kind_specs(rows, pairs, heads_first):
    return [pl.BlockSpec((rows, 2 * HEAD), partial(lambda k, p: (0, k * pairs + p), k)) for k in range(3)]


def attend(qkv_img, qkv_txt, block, valid):
    n_i, n_t = qkv_img.shape[0], qkv_txt.shape[0]
    inner = qkv_img.shape[1] // 3
    pairs = inner // (2 * HEAD)
    col = lambda rows: pl.BlockSpec((rows, 2 * HEAD), lambda p: (0, p))
    return pl.pallas_call(
        partial(attend_kernel, block, valid),
        grid=(pairs,),
        in_specs=kind_specs(n_i, pairs, 0) + kind_specs(n_t, pairs, 0),
        out_specs=[col(n_i), col(n_t), pl.BlockSpec((1, 2, n_i + n_t), lambda p: (p, 0, 0))],
        out_shape=[
            jax.ShapeDtypeStruct((n_i, inner), jnp.bfloat16),
            jax.ShapeDtypeStruct((n_t, inner), jnp.bfloat16),
            jax.ShapeDtypeStruct((pairs, 2, n_i + n_t), jnp.float32),
        ],
        compiler_params=pltpu.CompilerParams(vmem_limit_bytes=40 << 20),
        cost_estimate=pl.CostEstimate(flops=4 * (n_i + n_t) ** 2 * inner * 4, bytes_accessed=8 * (n_i + n_t) * inner, transcendentals=0),
    )(*([qkv_img] * 3 + [qkv_txt] * 3))


def attend_back(qkv_img, qkv_txt, g_img, g_txt, lse, block, valid):
    n_i, n_t = qkv_img.shape[0], qkv_txt.shape[0]
    inner = qkv_img.shape[1] // 3
    pairs = inner // (2 * HEAD)
    col = lambda rows: pl.BlockSpec((rows, 2 * HEAD), lambda p: (0, p))
    outs = [jax.ShapeDtypeStruct((n_i, inner), jnp.bfloat16)] * 3 + [jax.ShapeDtypeStruct((n_t, inner), jnp.bfloat16)] * 3
    res = pl.pallas_call(
        partial(back_kernel, block, valid),
        grid=(pairs,),
        in_specs=kind_specs(n_i, pairs, 0) + kind_specs(n_t, pairs, 0) + [col(n_i), col(n_t), pl.BlockSpec((1, 2, n_i + n_t), lambda p: (p, 0, 0))],
        out_specs=[col(n_i)] * 3 + [col(n_t)] * 3,
        out_shape=outs,
        scratch_shapes=[pltpu.VMEM((n, 2 * HEAD), jnp.float32) for n in (n_i, n_i, n_t, n_t)],
        compiler_params=pltpu.CompilerParams(vmem_limit_bytes=40 << 20),
        cost_estimate=pl.CostEstimate(flops=10 * (n_i + n_t) ** 2 * inner * 4, bytes_accessed=16 * (n_i + n_t) * inner, transcendentals=0),
    )(*([qkv_img] * 3 + [qkv_txt] * 3 + [g_img, g_txt, lse]))
    return res[:3], res[3:]


def tn(a, b):
    return lax.dot_general(a, b, (((0,), (0,)), ((), ())), preferred_element_type=jnp.float32)


def norm_forward(values):
    center = jnp.mean(values, -1, keepdims=True)
    spread = jnp.mean(jnp.square(values - center), -1, keepdims=True)
    rstd = lax.rsqrt(spread + norm_eps)
    return ((values - center) * rstd, rstd)


def norm_backward(grads, hats, rstd):
    first = jnp.mean(grads, -1, keepdims=True)
    second = jnp.mean(grads * hats, -1, keepdims=True)
    return rstd * (grads - first - hats * second)


class Group:
    def __init__(self, size):
        self.size = size
        self.evens = [2 * k for k in range(size // 2)]
        self.odds = [2 * k + 1 for k in range(size // 2)]
        self.order = self.evens + self.odds

    def send(self, value, flip):
        return lax.ppermute(value, "tensor", [(t, t ^ flip) for t in range(self.size)])

    def gather(self, own):
        evens = [own] + [self.send(own, flip) for flip in self.evens[1:]]
        return evens + [self.send(value, 1) for value in evens]


def on_device(
    n_dp,
    group,
    image,
    text,
    cond,
    teacher_image,
    teacher_text,
    grad_image,
    grad_text,
    live,
    w_mod,
    w_qkv,
    w_out,
    w_up,
    w_down,
):
    slots, width = cond.shape
    rows_i, rows_t = image.shape[1], text.shape[1]
    pad_t = -(-rows_t // 8) * 8
    size = group.size
    f_qkv, f_out, f_up, f_down = (
        lax.all_gather(w_qkv, "dp", axis=3, tiled=True),
        lax.all_gather(w_out, "dp", axis=2, tiled=True),
        lax.all_gather(w_up, "dp", axis=1, tiled=True),
        lax.all_gather(w_down, "dp", axis=1, tiled=True),
    )
    heads = f_qkv.shape[2]
    inner = heads * HEAD
    odd = heads % 2
    if odd:
        f_qkv = jnp.pad(f_qkv, ((0, 0), (0, 0), (0, 1), (0, 0), (0, 0)))
        f_out = jnp.pad(f_out, ((0, 0), (0, 1), (0, 0), (0, 0)))
    inner_p = inner + odd * HEAD
    f_qkv = f_qkv.reshape(2, 3 * inner_p, width)
    f_out = f_out.reshape(2, inner_p, width)
    here = lax.axis_index("dp")
    cond_f = cond.astype(jnp.float32)

    part = w_mod.shape[1]
    cond_all = lax.all_gather(cond, "dp", axis=0, tiled=True).astype(jnp.float32)
    act_all = jax.nn.silu(cond_all).astype(jnp.bfloat16)
    act_own = lax.dynamic_slice_in_dim(act_all, here * part, part, 1)
    mod_part = jnp.stack([nn(act_own, w_mod[s]) for s in range(2)], 1)
    mod_sum = lax.psum_scatter(mod_part, "dp", scatter_dimension=0, tiled=True)
    mod_full = lax.all_gather(mod_sum, "tensor", axis=2, tiled=True)
    mods = mod_full.reshape(slots, 2, 6, width)

    is_image = (lax.broadcasted_iota(jnp.int32, (rows_i + pad_t, 1), 0) < rows_i)
    is_real = (lax.broadcasted_iota(jnp.int32, (rows_i + pad_t, 1), 0) < rows_i + rows_t)

    def merged(img, txt, j):
        return jnp.concatenate([img[j], jnp.pad(txt[j], ((0, pad_t - rows_t), (0, 0)))], 0)

    def pick(j, span):
        return jnp.where(is_image, mods[j, 1, span][None], mods[j, 0, span][None])

    def token_sums(values):
        return jnp.stack([jnp.sum(values[rows_i:], 0), jnp.sum(values[:rows_i], 0)])

    def spread(blocks):
        return (
            jnp.concatenate([b[:rows_i] for b in blocks], 0),
            jnp.concatenate([b[rows_i:] for b in blocks], 0),
        )

    half_i, half_t = size // 2 * rows_i, size // 2 * pad_t

    def scatter(make_img, make_txt):
        top_i, top_t = slice(half_i, 2 * half_i), slice(half_t, 2 * half_t)
        sent_i = group.send(make_img(top_i).astype(jnp.bfloat16), 1)
        sent_t = group.send(make_txt(top_t).astype(jnp.bfloat16), 1)
        own_i = make_img(slice(0, half_i))
        own_t = make_txt(slice(0, half_t))
        blocks = []
        for k in range(size // 2):
            cut_i, cut_t = slice(k * rows_i, (k + 1) * rows_i), slice(k * pad_t, (k + 1) * pad_t)
            blocks.append(
                jnp.concatenate(
                    [
                        own_i[cut_i] + sent_i[cut_i].astype(jnp.float32),
                        own_t[cut_t] + sent_t[cut_t].astype(jnp.float32),
                    ],
                    0,
                )
            )
        total = blocks[0]
        for k in range(1, size // 2):
            total = total + group.send(blocks[k].astype(jnp.bfloat16), 2 * k).astype(jnp.float32)
        return total

    count = 3.0 * (n_dp // 2) * size * (rows_i + rows_t)

    slot = [dict() for j in range(slots)]
    for j in range(slots):
        v = slot[j]
        v["x"] = merged(image, text, j).astype(jnp.float32)
        v["hat1"], v["rstd1"] = norm_forward(v["x"])
        h1 = (v["hat1"] * (1.0 + pick(j, 1)) + pick(j, 0)).astype(jnp.bfloat16)
        v["h1_i"], v["h1_t"] = spread(group.gather(h1))
    for j in range(slots):
        v = slot[j]
        v["qkv_i"] = nt(v["h1_i"], f_qkv[1]).astype(jnp.bfloat16)
        v["qkv_t"] = nt(v["h1_t"], f_qkv[0]).astype(jnp.bfloat16)
        v["att_i"], v["att_t"], v["lse"] = attend(v["qkv_i"], v["qkv_t"], pad_t, rows_t)
        v["y"] = scatter(lambda r: nn(v["att_i"][r], f_out[1]), lambda r: nn(v["att_t"][r], f_out[0]))
        v["mid"] = v["x"] + pick(j, 2) * v["y"]
        v["hat2"], v["rstd2"] = norm_forward(v["mid"])
        h2 = (v["hat2"] * (1.0 + pick(j, 4)) + pick(j, 3)).astype(jnp.bfloat16)
        v["h2_i"], v["h2_t"] = spread(group.gather(h2))
    for j in range(slots):
        v = slot[j]
        v["pre_i"], v["pre_t"] = nn(v["h2_i"], f_up[1]), nn(v["h2_t"], f_up[0])
        v["hid_i"] = jax.nn.gelu(v["pre_i"], approximate=True).astype(jnp.bfloat16)
        v["hid_t"] = jax.nn.gelu(v["pre_t"], approximate=True).astype(jnp.bfloat16)
        v["m"] = scatter(lambda r: nt(v["hid_i"][r], f_down[1]), lambda r: nt(v["hid_t"][r], f_down[0]))
        out = v["mid"] + pick(j, 5) * v["m"]
        mask = jnp.where(is_real, live[j].astype(jnp.float32), 0.0)
        err = mask * (out - merged(teacher_image, teacher_text, j).astype(jnp.float32))
        v["loss"] = jnp.sum(err * err)
        v["cot"] = mask * merged(grad_image, grad_text, j).astype(jnp.float32) + 2.0 * err
        v["dgate2"] = token_sums(v["cot"] * v["m"])
        dm = (v["cot"] * pick(j, 5)).astype(jnp.bfloat16)
        v["dm_i"], v["dm_t"] = spread(group.gather(dm))
    loss = lax.psum(sum(v["loss"] for v in slot), ("dp", "tensor")) / (count * width)

    def reduced(make, axis, shape=None):
        g = jnp.stack([make("_t"), make("_i")]).astype(jnp.bfloat16)
        if shape is not None:
            g = g.reshape(shape)
        return lax.psum_scatter(g, "dp", scatter_dimension=axis, tiled=True).astype(jnp.float32)

    done_down = reduced(lambda e: sum(tn(v["dm" + e], v["hid" + e]) for v in slot), 1)
    for j in range(slots):
        v = slot[j]
        for s, e in enumerate(("_t", "_i")):
            dhid = nn(v["dm" + e], f_down[s])
            unused, pull = jax.vjp(partial(jax.nn.gelu, approximate=True), v["pre" + e])
            v["dpre" + e] = pull(dhid)[0].astype(jnp.bfloat16)
        v["dh2"] = scatter(lambda r: nt(v["dpre_i"][r], f_up[1]), lambda r: nt(v["dpre_t"][r], f_up[0]))
    done_up = reduced(lambda e: sum(tn(v["h2" + e], v["dpre" + e]) for v in slot), 1)
    for j in range(slots):
        v = slot[j]
        v["dshift2"] = token_sums(v["dh2"])
        v["dscale2"] = token_sums(v["dh2"] * v["hat2"])
        v["dmid"] = v["cot"] + norm_backward(v["dh2"] * (1.0 + pick(j, 4)), v["hat2"], v["rstd2"])
        v["dgate1"] = token_sums(v["dmid"] * v["y"])
        dy = (v["dmid"] * pick(j, 2)).astype(jnp.bfloat16)
        v["dy_i"], v["dy_t"] = spread(group.gather(dy))
    out_shape = (2, heads + odd, HEAD, width)
    done_out = reduced(lambda e: sum(tn(v["att" + e], v["dy" + e]) for v in slot), 2, out_shape)
    for j in range(slots):
        v = slot[j]
        g_i = nt(v["dy_i"], f_out[1]).astype(jnp.bfloat16)
        g_t = nt(v["dy_t"], f_out[0]).astype(jnp.bfloat16)
        back_i, back_t = attend_back(v["qkv_i"], v["qkv_t"], g_i, g_t, v["lse"], pad_t, rows_t)
        v["dqkv_i"], v["dqkv_t"] = jnp.concatenate(back_i, 1), jnp.concatenate(back_t, 1)
        v["dh1"] = scatter(lambda r: nn(v["dqkv_i"][r], f_qkv[1]), lambda r: nn(v["dqkv_t"][r], f_qkv[0]))
    qkv_shape = (2, 3, heads + odd, HEAD, width)
    done_qkv = reduced(lambda e: sum(tn(v["dqkv" + e], v["h1" + e]) for v in slot), 3, qkv_shape)
    grad_i, grad_t, terms = [], [], []
    for j in range(slots):
        v = slot[j]
        dshift1 = token_sums(v["dh1"])
        dscale1 = token_sums(v["dh1"] * v["hat1"])
        back = v["dmid"] + norm_backward(v["dh1"] * (1.0 + pick(j, 1)), v["hat1"], v["rstd1"])
        grad_i.append(back[:rows_i])
        grad_t.append(back[rows_i : rows_i + rows_t])
        terms.append(
            jnp.stack([dshift1, dscale1, v["dgate1"], v["dshift2"], v["dscale2"], v["dgate2"]], 1)
        )
    dmod = jnp.stack(terms).reshape(slots, 2, size, -1)
    dmod = lax.psum_scatter(dmod, "tensor", scatter_dimension=2, tiled=False).astype(jnp.bfloat16)
    dmod_all = lax.all_gather(dmod, "dp", axis=0, tiled=True)
    done_mod = jnp.stack([tn(act_own, dmod_all[:, s]) for s in range(2)])
    cond_part = nt(dmod_all[:, 0], w_mod[0]) + nt(dmod_all[:, 1], w_mod[1])
    cond_sum = lax.psum(cond_part, "tensor")
    cond_rows = lax.all_gather(cond_sum, "dp", axis=1, tiled=True)
    cond_total = lax.dynamic_slice_in_dim(cond_rows, here * slots, slots, 0)
    unused_value, silu_pull = jax.vjp(jax.nn.silu, cond_f)
    grad_cond = silu_pull(cond_total)[0]
    if odd:
        done_qkv, done_out = done_qkv[:, :, :heads], done_out[:, :heads]
    return (
        loss,
        done_mod,
        done_qkv,
        done_out,
        done_up,
        done_down,
        jnp.stack(grad_i),
        jnp.stack(grad_t),
        grad_cond,
    )


def solution(mesh):
    return jax.shard_map(
        partial(on_device, mesh.shape["dp"], Group(mesh.shape["tensor"])),
        mesh=mesh,
        in_specs=(
            P("dp", "tensor", None),
            P("dp", "tensor", None),
            P("dp", None),
            P("dp", "tensor", None),
            P("dp", "tensor", None),
            P("dp", "tensor", None),
            P("dp", "tensor", None),
            P("dp"),
            P(None, "dp", "tensor"),
            P(None, None, "tensor", "dp", None),
            P(None, "tensor", "dp", None),
            P(None, "dp", "tensor"),
            P(None, "dp", "tensor"),
        ),
        out_specs=(
            P(),
            P(None, "dp", "tensor"),
            P(None, None, "tensor", "dp", None),
            P(None, "tensor", "dp", None),
            P(None, "dp", "tensor"),
            P(None, "dp", "tensor"),
            P("dp", "tensor", None),
            P("dp", "tensor", None),
            P("dp", None),
        ),
        check_vma=False,
    )
```

```python
import math
from functools import partial

import jax
import jax.numpy as jnp
from jax import lax
from jax.experimental import pallas as pl
from jax.experimental.pallas import tpu as pltpu
from jax.sharding import PartitionSpec as P

norm_eps = 1e-06

LOG2E = math.log2(math.e)
HEAD = 64


def nt(a, b):
    return lax.dot_general(a, b, (((1,), (1,)), ((), ())), preferred_element_type=jnp.float32)


def nn(a, b):
    return jnp.dot(a, b, preferred_element_type=jnp.float32)


def query_blocks(rows_img, rows_txt):
    step = 256 if rows_img % 256 == 0 else rows_img
    return [(0, s, step) for s in range(0, rows_img, step)] + [(1, 0, rows_txt)]


def pad_bias(rows, block, valid):
    place = lax.broadcasted_iota(jnp.int32, (rows, 1), 0)
    return jnp.where(lax.rem(place, block) < valid, 0.0, -1e30).astype(jnp.float32)


def attend_kernel(block, valid, qi, ki, vi, qt, kt, vt, oi, ot, lse):
    factor = HEAD**-0.5
    low = lax.broadcasted_iota(jnp.int32, (1, 2 * HEAD), 1) < HEAD
    zero = jnp.zeros((), jnp.bfloat16)
    bias = pad_bias(qt.shape[0], block, valid)
    vit, vtt = vi[...].T, vt[...].T
    keys = []
    for h in range(2):
        mask = low if h == 0 else ~low
        keys.append((jnp.where(mask, ki[...], zero), jnp.where(mask, kt[...], zero)))
    at = 0
    for which, start, size in query_blocks(qi.shape[0], qt.shape[0]):
        src, dst = (qi, oi) if which == 0 else (qt, ot)
        q = src[start : start + size, :]
        parts = []
        for h in range(2):
            s_i = nt(keys[h][0], q)
            s_t = nt(keys[h][1], q) + bias
            top = jnp.maximum(
                jnp.max(s_i, 0, keepdims=True), jnp.max(s_t, 0, keepdims=True)
            )
            e_i = jnp.exp2((s_i - top) * (factor * LOG2E))
            e_t = jnp.exp2((s_t - top) * (factor * LOG2E))
            total = jnp.sum(e_i, 0, keepdims=True) + jnp.sum(e_t, 0, keepdims=True)
            inv = 1.0 / total
            p_i = (e_i * inv).astype(jnp.bfloat16)
            p_t = (e_t * inv).astype(jnp.bfloat16)
            rows = slice(h * HEAD, (h + 1) * HEAD)
            parts.append(nn(vit[rows], p_i) + nn(vtt[rows], p_t))
            lse[0, h : h + 1, at : at + size] = top * (factor * LOG2E) + jnp.log2(total)
        dst[start : start + size, :] = jnp.concatenate(parts, 0).T.astype(jnp.bfloat16)
        at += size


def back_kernel(block, valid, qi, ki, vi, qt, kt, vt, gi, gt, lse,
                dqi, dki, dvi, dqt, dkt, dvt, aki, avi, akt, avt):
    factor = HEAD**-0.5
    low = lax.broadcasted_iota(jnp.int32, (1, 2 * HEAD), 1) < HEAD
    zero = jnp.zeros((), jnp.bfloat16)
    bias = pad_bias(qt.shape[0], block, valid)
    kit, ktt = ki[...].T, kt[...].T
    masks = [low, ~low]
    at = 0
    first = True
    for which, start, size in query_blocks(qi.shape[0], qt.shape[0]):
        q_ref, g_ref, d_ref = (qi, gi, dqi) if which == 0 else (qt, gt, dqt)
        q, g = q_ref[start : start + size, :], g_ref[start : start + size, :]
        parts = []
        for h in range(2):
            q_h, g_h = jnp.where(masks[h], q, zero), jnp.where(masks[h], g, zero)
            stat = lse[0, h : h + 1, at : at + size]
            p_i = jnp.exp2(nt(ki[...], q_h) * (factor * LOG2E) - stat)
            p_t = jnp.exp2((nt(kt[...], q_h) + bias) * (factor * LOG2E) - stat)
            d_i, d_t = nt(vi[...], g_h), nt(vt[...], g_h)
            delta = jnp.sum(d_i * p_i, 0, keepdims=True) + jnp.sum(d_t * p_t, 0, keepdims=True)
            s_i = (p_i * (d_i - delta)).astype(jnp.bfloat16)
            s_t = (p_t * (d_t - delta)).astype(jnp.bfloat16)
            v_i = nn(p_i.astype(jnp.bfloat16), g_h)
            v_t = nn(p_t.astype(jnp.bfloat16), g_h)
            k_i = nn(s_i, q_h)
            k_t = nn(s_t, q_h)
            if first:
                avi[...], avt[...], aki[...], akt[...] = v_i, v_t, k_i, k_t
                first = False
            else:
                avi[...] += v_i
                avt[...] += v_t
                aki[...] += k_i
                akt[...] += k_t
            rows = slice(h * HEAD, (h + 1) * HEAD)
            parts.append(nn(kit[rows], s_i) + nn(ktt[rows], s_t))
        d_ref[start : start + size, :] = (jnp.concatenate(parts, 0).T * factor).astype(jnp.bfloat16)
        at += size
    dki[...] = (aki[...] * factor).astype(jnp.bfloat16)
    dkt[...] = (akt[...] * factor).astype(jnp.bfloat16)
    dvi[...] = avi[...].astype(jnp.bfloat16)
    dvt[...] = avt[...].astype(jnp.bfloat16)


def kind_specs(rows, pairs, heads_first):
    return [pl.BlockSpec((rows, 2 * HEAD), partial(lambda k, p: (0, k * pairs + p), k)) for k in range(3)]


def attend(qkv_img, qkv_txt, block, valid):
    n_i, n_t = qkv_img.shape[0], qkv_txt.shape[0]
    inner = qkv_img.shape[1] // 3
    pairs = inner // (2 * HEAD)
    col = lambda rows: pl.BlockSpec((rows, 2 * HEAD), lambda p: (0, p))
    return pl.pallas_call(
        partial(attend_kernel, block, valid),
        grid=(pairs,),
        in_specs=kind_specs(n_i, pairs, 0) + kind_specs(n_t, pairs, 0),
        out_specs=[col(n_i), col(n_t), pl.BlockSpec((1, 2, n_i + n_t), lambda p: (p, 0, 0))],
        out_shape=[
            jax.ShapeDtypeStruct((n_i, inner), jnp.bfloat16),
            jax.ShapeDtypeStruct((n_t, inner), jnp.bfloat16),
            jax.ShapeDtypeStruct((pairs, 2, n_i + n_t), jnp.float32),
        ],
        compiler_params=pltpu.CompilerParams(vmem_limit_bytes=40 << 20),
        cost_estimate=pl.CostEstimate(flops=4 * (n_i + n_t) ** 2 * inner * 4, bytes_accessed=8 * (n_i + n_t) * inner, transcendentals=0),
    )(*([qkv_img] * 3 + [qkv_txt] * 3))


def attend_back(qkv_img, qkv_txt, g_img, g_txt, lse, block, valid):
    n_i, n_t = qkv_img.shape[0], qkv_txt.shape[0]
    inner = qkv_img.shape[1] // 3
    pairs = inner // (2 * HEAD)
    col = lambda rows: pl.BlockSpec((rows, 2 * HEAD), lambda p: (0, p))
    outs = [jax.ShapeDtypeStruct((n_i, inner), jnp.bfloat16)] * 3 + [jax.ShapeDtypeStruct((n_t, inner), jnp.bfloat16)] * 3
    res = pl.pallas_call(
        partial(back_kernel, block, valid),
        grid=(pairs,),
        in_specs=kind_specs(n_i, pairs, 0) + kind_specs(n_t, pairs, 0) + [col(n_i), col(n_t), pl.BlockSpec((1, 2, n_i + n_t), lambda p: (p, 0, 0))],
        out_specs=[col(n_i)] * 3 + [col(n_t)] * 3,
        out_shape=outs,
        scratch_shapes=[pltpu.VMEM((n, 2 * HEAD), jnp.float32) for n in (n_i, n_i, n_t, n_t)],
        compiler_params=pltpu.CompilerParams(vmem_limit_bytes=40 << 20),
        cost_estimate=pl.CostEstimate(flops=10 * (n_i + n_t) ** 2 * inner * 4, bytes_accessed=16 * (n_i + n_t) * inner, transcendentals=0),
    )(*([qkv_img] * 3 + [qkv_txt] * 3 + [g_img, g_txt, lse]))
    return res[:3], res[3:]


def tn(a, b):
    return lax.dot_general(a, b, (((0,), (0,)), ((), ())), preferred_element_type=jnp.float32)


def norm_forward(values):
    center = jnp.mean(values, -1, keepdims=True)
    spread = jnp.mean(jnp.square(values - center), -1, keepdims=True)
    rstd = lax.rsqrt(spread + norm_eps)
    return ((values - center) * rstd, rstd)


def norm_backward(grads, hats, rstd):
    first = jnp.mean(grads, -1, keepdims=True)
    second = jnp.mean(grads * hats, -1, keepdims=True)
    return rstd * (grads - first - hats * second)


class Group:
    def __init__(self, size):
        self.size = size
        self.evens = [2 * k for k in range(size // 2)]
        self.odds = [2 * k + 1 for k in range(size // 2)]
        self.order = self.evens + self.odds

    def send(self, value, flip):
        return lax.ppermute(value, "tensor", [(t, t ^ flip) for t in range(self.size)])

    def gather(self, own):
        evens = [own] + [self.send(own, flip) for flip in self.evens[1:]]
        return evens + [self.send(value, 1) for value in evens]


MESH = pl.DeviceIdType.MESH


def flip_bits(index, flip, size):
    total, bit = 0, 1
    while bit < size:
        digit = lax.rem(lax.div(index, bit), 2)
        total = total + bit * ((1 - digit) if flip & bit else digit)
        bit *= 2
    return total


class Data:
    def __init__(self, size):
        self.size = size
        self.nx = math.isqrt(size // 2)
        self.nz = size // self.nx

    def send(self, value, flip):
        return lax.ppermute(value, "dp", [(p, p ^ flip) for p in range(self.size)])

    def gather(self, own):
        blocks = {}
        for zk in range(self.nz):
            blocks[zk * self.nx] = self.send(own, zk * self.nx) if zk else own
        for zk in range(self.nz):
            for xk in range(1, self.nx):
                blocks[zk * self.nx + xk] = self.send(blocks[zk * self.nx], xk)
        return [blocks[k] for k in range(self.size)]


def place_kernel(size, *refs):
    blocks, out, sems = refs[:size], refs[size], refs[size + 1]
    here = lax.axis_index("dp")
    part = blocks[0].shape[1]
    copies = []
    for k in range(size):
        start = pl.multiple_of(flip_bits(here, k, size) * part, 16)
        copies.append(
            pltpu.make_async_copy(blocks[k], out.at[:, pl.ds(start, part), :], sems.at[k])
        )
        copies[-1].start()
    for copy in copies:
        copy.wait()


def place(blocks):
    size = len(blocks)
    two, part, columns = blocks[0].shape
    return pl.pallas_call(
        partial(place_kernel, size),
        in_specs=[pl.BlockSpec(memory_space=pl.ANY)] * size,
        out_specs=pl.BlockSpec(memory_space=pl.ANY),
        out_shape=jax.ShapeDtypeStruct((two, size * part, columns), blocks[0].dtype),
        scratch_shapes=[pltpu.SemaphoreType.DMA((size,))],
        cost_estimate=pl.CostEstimate(flops=0, bytes_accessed=4 * two * size * part * columns, transcendentals=0),
    )(*blocks)


def greet(n_dp, size):
    me_d, me_t = lax.axis_index("dp"), lax.axis_index("tensor")
    barrier = pltpu.get_barrier_semaphore()
    for k in range(1, n_dp):
        pl.semaphore_signal(barrier, inc=1, device_id=(flip_bits(me_d, k, n_dp), me_t), device_id_type=MESH)
    for k in range(1, size):
        pl.semaphore_signal(barrier, inc=1, device_id=(me_d, flip_bits(me_t, k, size)), device_id_type=MESH)
    pl.semaphore_wait(barrier, n_dp + size - 2)


def to_data(n_dp, source, target, send, recv):
    me_d, me_t = lax.axis_index("dp"), lax.axis_index("tensor")
    copies = []
    for k in range(1, n_dp):
        peer = flip_bits(me_d, k, n_dp)
        copy = pltpu.make_async_remote_copy(
            src_ref=source(peer),
            dst_ref=target.at[me_d],
            send_sem=send.at[k - 1],
            recv_sem=recv.at[k - 1],
            device_id=(peer, me_t),
            device_id_type=MESH,
        )
        copy.start()
        copies.append(copy)
    return copies


def to_tensor(size, source, target, send, recv):
    me_d, me_t = lax.axis_index("dp"), lax.axis_index("tensor")
    copies = []
    for k in range(1, size):
        peer = flip_bits(me_t, k, size)
        copy = pltpu.make_async_remote_copy(
            src_ref=source(peer),
            dst_ref=target.at[me_t],
            send_sem=send.at[k - 1],
            recv_sem=recv.at[k - 1],
            device_id=(me_d, peer),
            device_id_type=MESH,
        )
        copy.start()
        copies.append(copy)
    return copies


def finish(copies):
    for copy in copies:
        copy.wait()


def mod_kernel(n_dp, size, cond, w, mod_out, act_out, conds, parts, got, own, sd1, rd1, sd2, rd2, st, rt):
    me_d, me_t = lax.axis_index("dp"), lax.axis_index("tensor")
    rows, part, columns = conds.shape[1], w.shape[1], w.shape[2]
    greet(n_dp, size)
    copies = to_data(n_dp, lambda peer: cond.at[peer], conds, sd1, rd1)
    conds[me_d] = cond[me_d]
    finish(copies)
    value = conds[...].reshape(n_dp * rows, conds.shape[2])[:, :part]
    act = (value * jax.nn.sigmoid(value)).astype(jnp.bfloat16)
    act_out[...] = act
    place = lax.rem(lax.broadcasted_iota(jnp.int32, (n_dp * rows, 1), 0), rows)
    mixed = jnp.where(place < rows // 4, nn(act, w[0]), nn(act, w[1]))
    parts[...] = mixed.reshape(n_dp, rows, columns)
    copies = to_data(n_dp, lambda peer: parts.at[peer], got, sd2, rd2)
    got[me_d] = parts[me_d]
    finish(copies)
    total = got[0]
    for p in range(1, n_dp):
        total = total + got[p]
    own[...] = total
    copies = to_tensor(size, lambda peer: own, mod_out, st, rt)
    mod_out[me_t] = total
    finish(copies)


def mod_forward(n_dp, size, cond, w_mod):
    slots, width = cond.shape
    part, columns = w_mod.shape[1:]
    rows, lanes = 4 * slots, -(-part // 128) * 128
    laid = cond.astype(jnp.float32).reshape(slots, n_dp, part).transpose(1, 0, 2)
    laid = jnp.concatenate([laid, laid, jnp.zeros_like(laid), jnp.zeros_like(laid)], 1)
    laid = jnp.pad(laid, ((0, 0), (0, 0), (0, lanes - part)))
    dma = pltpu.SemaphoreType.DMA
    return pl.pallas_call(
        partial(mod_kernel, n_dp, size),
        in_specs=[pl.BlockSpec(memory_space=pltpu.VMEM)] * 2,
        out_specs=[pl.BlockSpec(memory_space=pltpu.VMEM)] * 2,
        out_shape=[
            jax.ShapeDtypeStruct((size, rows, columns), jnp.float32),
            jax.ShapeDtypeStruct((n_dp * rows, part), jnp.bfloat16),
        ],
        scratch_shapes=[
            pltpu.VMEM((n_dp, rows, lanes), jnp.float32),
            pltpu.VMEM((n_dp, rows, columns), jnp.float32),
            pltpu.VMEM((n_dp, rows, columns), jnp.float32),
            pltpu.VMEM((rows, columns), jnp.float32),
            dma((n_dp - 1,)), dma((n_dp - 1,)), dma((n_dp - 1,)), dma((n_dp - 1,)),
            dma((size - 1,)), dma((size - 1,)),
        ],
        compiler_params=pltpu.CompilerParams(
            collective_id=0, has_side_effects=True, vmem_limit_bytes=40 << 20
        ),
        cost_estimate=pl.CostEstimate(flops=1 << 33, bytes_accessed=1 << 21, transcendentals=0),
    )(laid, w_mod)


def mod_back_kernel(n_dp, size, terms, act, w, grad, cond_out, loss_out, halves, sums, every, cparts, cgot, cfull,
                    st1, rt1, sd1, rd1, sd2, rd2, st2, rt2):
    me_d, me_t = lax.axis_index("dp"), lax.axis_index("tensor")
    rows, columns = terms.shape[1:]
    part = w.shape[1]
    greet(n_dp, size)
    copies = to_tensor(size, lambda peer: terms.at[peer], halves, st1, rt1)
    halves[me_t] = terms[me_t]
    finish(copies)
    total = halves[0]
    for t in range(1, size):
        total = total + halves[t]
    sums[...] = total
    copies = to_data(n_dp, lambda peer: sums, every, sd1, rd1)
    every[me_d] = total
    finish(copies)
    loss = every[0, rows // 2 : rows // 2 + 1, :128]
    for p in range(1, n_dp):
        loss = loss + every[p, rows // 2 : rows // 2 + 1, :128]
    loss_out[...] = jnp.broadcast_to(loss, loss_out.shape)
    dmod = every[...].reshape(n_dp * rows, columns).astype(jnp.bfloat16)
    place = lax.rem(lax.broadcasted_iota(jnp.int32, (n_dp * rows, 1), 0), rows)
    quarter = rows // 4
    back = [nt(dmod, w[s]) for s in range(2)]
    mixed = jnp.where(place < quarter, back[0], jnp.where(place < 2 * quarter, back[1], 0.0))
    cparts[:, :, :part] = mixed.reshape(n_dp, rows, part)
    copies = to_data(n_dp, lambda peer: cparts.at[peer], cgot, sd2, rd2)
    cgot[me_d] = cparts[me_d]
    for s in range(2):
        mask = (place >= s * quarter) & (place < (s + 1) * quarter)
        picked = jnp.where(mask, act[...], jnp.zeros((), jnp.bfloat16))
        grad[s] = tn(picked, dmod)
    finish(copies)
    copies = to_tensor(size, lambda peer: cgot, cfull, st2, rt2)
    cfull[me_t] = cgot[...]
    finish(copies)
    full = cfull[0]
    for t in range(1, size):
        full = full + cfull[t]
    cond_out[...] = full


def mod_backward(n_dp, size, terms, act, w_mod):
    rows, columns = terms.shape[1:]
    part = w_mod.shape[1]
    lanes = -(-part // 128) * 128
    dma = pltpu.SemaphoreType.DMA
    f32 = jnp.float32
    return pl.pallas_call(
        partial(mod_back_kernel, n_dp, size),
        in_specs=[pl.BlockSpec(memory_space=pltpu.VMEM)] * 3,
        out_specs=[pl.BlockSpec(memory_space=pltpu.VMEM)] * 3,
        out_shape=[
            jax.ShapeDtypeStruct(w_mod.shape, f32),
            jax.ShapeDtypeStruct((n_dp, rows, lanes), f32),
            jax.ShapeDtypeStruct((8, 128), f32),
        ],
        scratch_shapes=[
            pltpu.VMEM((size, rows, columns), f32),
            pltpu.VMEM((rows, columns), f32),
            pltpu.VMEM((n_dp, rows, columns), f32),
            pltpu.VMEM((n_dp, rows, lanes), f32),
            pltpu.VMEM((n_dp, rows, lanes), f32),
            pltpu.VMEM((size, n_dp, rows, lanes), f32),
            dma((size - 1,)), dma((size - 1,)),
            dma((n_dp - 1,)), dma((n_dp - 1,)), dma((n_dp - 1,)), dma((n_dp - 1,)),
            dma((size - 1,)), dma((size - 1,)),
        ],
        compiler_params=pltpu.CompilerParams(
            collective_id=1, has_side_effects=True, vmem_limit_bytes=40 << 20
        ),
        cost_estimate=pl.CostEstimate(flops=1 << 33, bytes_accessed=1 << 21, transcendentals=0),
    )(terms, act, w_mod)


def on_device(
    data,
    group,
    image,
    text,
    cond,
    teacher_image,
    teacher_text,
    grad_image,
    grad_text,
    live,
    w_mod,
    w_qkv,
    w_out,
    w_up,
    w_down,
):
    slots, width = cond.shape
    rows_i, rows_t = image.shape[1], text.shape[1]
    pad_t = -(-rows_t // 8) * 8
    size = group.size
    n_dp = data.size
    mod_all, act_all = mod_forward(n_dp, size, cond, w_mod)
    mods = jnp.stack(
        [
            jnp.stack([mod_all[:, s * slots + j].reshape(6, width) for s in range(2)])
            for j in range(slots)
        ]
    )

    heads = w_qkv.shape[2]
    odd = heads % 2

    def by_head(blocks, pad):
        joined = jnp.stack(blocks, -3)
        if odd:
            joined = jnp.pad(joined, pad)
        return joined.reshape(2, -1, width)

    f_qkv = by_head(data.gather(w_qkv), ((0, 0), (0, 0), (0, odd), (0, 0), (0, 0), (0, 0)))
    f_out = by_head(data.gather(w_out), ((0, 0), (0, odd), (0, 0), (0, 0), (0, 0)))
    f_up = place(data.gather(w_up))
    f_down = place(data.gather(w_down))

    is_image = (lax.broadcasted_iota(jnp.int32, (rows_i + pad_t, 1), 0) < rows_i)
    is_real = (lax.broadcasted_iota(jnp.int32, (rows_i + pad_t, 1), 0) < rows_i + rows_t)

    def merged(img, txt, j):
        return jnp.concatenate([img[j], jnp.pad(txt[j], ((0, pad_t - rows_t), (0, 0)))], 0)

    def pick(j, span):
        return jnp.where(is_image, mods[j, 1, span][None], mods[j, 0, span][None])

    def token_sums(values):
        return jnp.stack([jnp.sum(values[rows_i:], 0), jnp.sum(values[:rows_i], 0)])

    def spread(blocks):
        return (
            jnp.concatenate([b[:rows_i] for b in blocks], 0),
            jnp.concatenate([b[rows_i:] for b in blocks], 0),
        )

    half_i, half_t = size // 2 * rows_i, size // 2 * pad_t

    def scatter(make_img, make_txt):
        top_i, top_t = slice(half_i, 2 * half_i), slice(half_t, 2 * half_t)
        sent_i = group.send(make_img(top_i).astype(jnp.bfloat16), 1)
        sent_t = group.send(make_txt(top_t).astype(jnp.bfloat16), 1)
        own_i = make_img(slice(0, half_i))
        own_t = make_txt(slice(0, half_t))
        blocks = []
        for k in range(size // 2):
            cut_i, cut_t = slice(k * rows_i, (k + 1) * rows_i), slice(k * pad_t, (k + 1) * pad_t)
            blocks.append(
                jnp.concatenate(
                    [
                        own_i[cut_i] + sent_i[cut_i].astype(jnp.float32),
                        own_t[cut_t] + sent_t[cut_t].astype(jnp.float32),
                    ],
                    0,
                )
            )
        total = blocks[0]
        for k in range(1, size // 2):
            total = total + group.send(blocks[k].astype(jnp.bfloat16), 2 * k).astype(jnp.float32)
        return total

    count = 3.0 * (n_dp // 2) * size * (rows_i + rows_t)

    slot = [dict() for j in range(slots)]
    for j in range(slots):
        v = slot[j]
        v["x"] = merged(image, text, j).astype(jnp.float32)
        v["hat1"], v["rstd1"] = norm_forward(v["x"])
        h1 = (v["hat1"] * (1.0 + pick(j, 1)) + pick(j, 0)).astype(jnp.bfloat16)
        v["h1_i"], v["h1_t"] = spread(group.gather(h1))
    for j in range(slots):
        v = slot[j]
        v["qkv_i"] = nt(v["h1_i"], f_qkv[1]).astype(jnp.bfloat16)
        v["qkv_t"] = nt(v["h1_t"], f_qkv[0]).astype(jnp.bfloat16)
        v["att_i"], v["att_t"], v["lse"] = attend(v["qkv_i"], v["qkv_t"], pad_t, rows_t)
        v["y"] = scatter(lambda r: nn(v["att_i"][r], f_out[1]), lambda r: nn(v["att_t"][r], f_out[0]))
        v["mid"] = v["x"] + pick(j, 2) * v["y"]
        v["hat2"], v["rstd2"] = norm_forward(v["mid"])
        h2 = (v["hat2"] * (1.0 + pick(j, 4)) + pick(j, 3)).astype(jnp.bfloat16)
        v["h2_i"], v["h2_t"] = spread(group.gather(h2))
    for j in range(slots):
        v = slot[j]
        v["pre_i"], v["pre_t"] = nn(v["h2_i"], f_up[1]), nn(v["h2_t"], f_up[0])
        v["hid_i"] = jax.nn.gelu(v["pre_i"], approximate=True).astype(jnp.bfloat16)
        v["hid_t"] = jax.nn.gelu(v["pre_t"], approximate=True).astype(jnp.bfloat16)
        v["m"] = scatter(lambda r: nt(v["hid_i"][r], f_down[1]), lambda r: nt(v["hid_t"][r], f_down[0]))
        out = v["mid"] + pick(j, 5) * v["m"]
        mask = jnp.where(is_real, live[j].astype(jnp.float32), 0.0)
        err = mask * (out - merged(teacher_image, teacher_text, j).astype(jnp.float32))
        v["loss"] = jnp.sum(err * err)
        v["cot"] = mask * merged(grad_image, grad_text, j).astype(jnp.float32) + 2.0 * err
        v["dgate2"] = token_sums(v["cot"] * v["m"])
        dm = (v["cot"] * pick(j, 5)).astype(jnp.bfloat16)
        v["dm_i"], v["dm_t"] = spread(group.gather(dm))

    here = lax.axis_index("dp")
    here_z, here_x = lax.div(here, data.nx), lax.rem(here, data.nx)

    def exchange(own, for_x, for_z):
        got = [data.send(for_x(xk), xk) for xk in range(1, data.nx)]
        total = None
        sent = []
        for zk in range(1, data.nz):
            part = own(zk)
            for g in got:
                part = part + for_z(g, zk).astype(jnp.float32)
            sent.append(data.send(part.astype(jnp.bfloat16), zk * data.nx))
        total = own(0)
        for g in got:
            total = total + for_z(g, 0).astype(jnp.float32)
        for g in sent:
            total = total + g.astype(jnp.float32)
        return total

    def reduced_rows(make):
        g = [make(e).astype(jnp.bfloat16) for e in ("_t", "_i")]
        g = [v.reshape(data.nz, data.nx, -1, v.shape[-1]) for v in g]
        column = lambda v, xk: lax.dynamic_index_in_dim(v, flip_bits(here_x, xk, data.nx), 1, keepdims=False)
        line = lambda v, zk, axis: lax.dynamic_index_in_dim(v, flip_bits(here_z, zk, data.nz), axis, keepdims=False)
        return exchange(
            lambda zk: jnp.stack([line(column(v, 0), zk, 0) for v in g]).astype(jnp.float32),
            lambda xk: jnp.stack([column(v, xk) for v in g]),
            lambda v, zk: line(v, zk, 1),
        )

    def reduced_heads(make, lead):
        g = [make(e).astype(jnp.bfloat16).reshape(lead, data.nz, data.nx, -1, width) for e in ("_t", "_i")]
        return exchange(
            lambda zk: jnp.stack([v[:, zk, 0] for v in g]).astype(jnp.float32),
            lambda xk: jnp.stack([v[:, :, xk] for v in g]),
            lambda v, zk: v[:, :, zk],
        )

    done_down = reduced_rows(lambda e: sum(tn(v["dm" + e], v["hid" + e]) for v in slot))
    for j in range(slots):
        v = slot[j]
        for s, e in enumerate(("_t", "_i")):
            dhid = nn(v["dm" + e], f_down[s])
            unused, pull = jax.vjp(partial(jax.nn.gelu, approximate=True), v["pre" + e])
            v["dpre" + e] = pull(dhid)[0].astype(jnp.bfloat16)
        v["dh2"] = scatter(lambda r: nt(v["dpre_i"][r], f_up[1]), lambda r: nt(v["dpre_t"][r], f_up[0]))
    done_up = reduced_rows(lambda e: sum(tn(v["h2" + e], v["dpre" + e]) for v in slot))
    for j in range(slots):
        v = slot[j]
        v["dshift2"] = token_sums(v["dh2"])
        v["dscale2"] = token_sums(v["dh2"] * v["hat2"])
        v["dmid"] = v["cot"] + norm_backward(v["dh2"] * (1.0 + pick(j, 4)), v["hat2"], v["rstd2"])
        v["dgate1"] = token_sums(v["dmid"] * v["y"])
        dy = (v["dmid"] * pick(j, 2)).astype(jnp.bfloat16)
        v["dy_i"], v["dy_t"] = spread(group.gather(dy))
    done_out = reduced_heads(lambda e: sum(tn(v["att" + e], v["dy" + e]) for v in slot), heads + odd)
    for j in range(slots):
        v = slot[j]
        g_i = nt(v["dy_i"], f_out[1]).astype(jnp.bfloat16)
        g_t = nt(v["dy_t"], f_out[0]).astype(jnp.bfloat16)
        back_i, back_t = attend_back(v["qkv_i"], v["qkv_t"], g_i, g_t, v["lse"], pad_t, rows_t)
        v["dqkv_i"], v["dqkv_t"] = jnp.concatenate(back_i, 1), jnp.concatenate(back_t, 1)
        v["dh1"] = scatter(lambda r: nn(v["dqkv_i"][r], f_qkv[1]), lambda r: nn(v["dqkv_t"][r], f_qkv[0]))
    done_qkv = reduced_heads(lambda e: sum(tn(v["dqkv" + e], v["h1" + e]) for v in slot), 3 * (heads + odd))
    done_qkv = done_qkv.reshape(2, 3, heads + odd, -1, width)
    grad_i, grad_t, terms = [], [], []
    for j in range(slots):
        v = slot[j]
        dshift1 = token_sums(v["dh1"])
        dscale1 = token_sums(v["dh1"] * v["hat1"])
        back = v["dmid"] + norm_backward(v["dh1"] * (1.0 + pick(j, 1)), v["hat1"], v["rstd1"])
        grad_i.append(back[:rows_i])
        grad_t.append(back[rows_i : rows_i + rows_t])
        terms.append(
            jnp.stack([dshift1, dscale1, v["dgate1"], v["dshift2"], v["dscale2"], v["dgate2"]], 1)
        )
    lost = sum(v["loss"] for v in slot)
    laid = jnp.stack(terms, 1).reshape(2 * slots, size, -1).transpose(1, 0, 2)
    laid = jnp.concatenate([laid, jnp.full((size, 1, laid.shape[2]), lost), jnp.zeros((size, 2 * slots - 1, laid.shape[2]), jnp.float32)], 1)
    done_mod, cond_rows, loss_rows = mod_backward(n_dp, size, laid, act_all, w_mod)
    loss = loss_rows[0, 0] / (count * width)
    cond_rows = cond_rows[:, :, : w_mod.shape[1]]
    cond_total = (cond_rows[:, :slots] + cond_rows[:, slots : 2 * slots]).transpose(1, 0, 2).reshape(slots, width)
    unused_value, silu_pull = jax.vjp(jax.nn.silu, cond.astype(jnp.float32))
    grad_cond = silu_pull(cond_total)[0]
    if odd:
        done_qkv, done_out = done_qkv[:, :, :heads], done_out[:, :heads]
    return (
        loss,
        done_mod,
        done_qkv,
        done_out,
        done_up,
        done_down,
        jnp.stack(grad_i),
        jnp.stack(grad_t),
        grad_cond,
    )


def solution(mesh):
    return jax.shard_map(
        partial(on_device, Data(mesh.shape["dp"]), Group(mesh.shape["tensor"])),
        mesh=mesh,
        in_specs=(
            P("dp", "tensor", None),
            P("dp", "tensor", None),
            P("dp", None),
            P("dp", "tensor", None),
            P("dp", "tensor", None),
            P("dp", "tensor", None),
            P("dp", "tensor", None),
            P("dp"),
            P(None, "dp", "tensor"),
            P(None, None, "tensor", "dp", None),
            P(None, "tensor", "dp", None),
            P(None, "dp", "tensor"),
            P(None, "dp", "tensor"),
        ),
        out_specs=(
            P(),
            P(None, "dp", "tensor"),
            P(None, None, "tensor", "dp", None),
            P(None, "tensor", "dp", None),
            P(None, "dp", "tensor"),
            P(None, "dp", "tensor"),
            P("dp", "tensor", None),
            P("dp", "tensor", None),
            P("dp", None),
        ),
        check_vma=False,
    )
```

```python
import math
from functools import partial

import jax
import jax.numpy as jnp
from jax import lax
from jax.experimental import pallas as pl
from jax.experimental.pallas import tpu as pltpu
from jax.sharding import PartitionSpec as P

norm_eps = 1e-06

LOG2E = math.log2(math.e)
HEAD = 64


def nt(a, b):
    return lax.dot_general(a, b, (((1,), (1,)), ((), ())), preferred_element_type=jnp.float32)


def nn(a, b):
    return jnp.dot(a, b, preferred_element_type=jnp.float32)


def query_blocks(rows_img, rows_txt):
    step = 256 if rows_img % 256 == 0 else rows_img
    return [(0, s, step) for s in range(0, rows_img, step)] + [(1, 0, rows_txt)]


def pad_bias(rows, block, valid):
    place = lax.broadcasted_iota(jnp.int32, (rows, 1), 0)
    return jnp.where(lax.rem(place, block) < valid, 0.0, -1e30).astype(jnp.float32)


def attend_kernel(block, valid, qi, ki, vi, qt, kt, vt, oi, ot, lse):
    factor = HEAD**-0.5
    low = lax.broadcasted_iota(jnp.int32, (1, 2 * HEAD), 1) < HEAD
    zero = jnp.zeros((), jnp.bfloat16)
    bias = pad_bias(qt.shape[0], block, valid)
    vit, vtt = vi[...].T, vt[...].T
    keys = []
    for h in range(2):
        mask = low if h == 0 else ~low
        keys.append((jnp.where(mask, ki[...], zero), jnp.where(mask, kt[...], zero)))
    at = 0
    for which, start, size in query_blocks(qi.shape[0], qt.shape[0]):
        src, dst = (qi, oi) if which == 0 else (qt, ot)
        q = src[start : start + size, :]
        parts = []
        for h in range(2):
            s_i = nt(keys[h][0], q)
            s_t = nt(keys[h][1], q) + bias
            top = jnp.maximum(
                jnp.max(s_i, 0, keepdims=True), jnp.max(s_t, 0, keepdims=True)
            )
            e_i = jnp.exp2((s_i - top) * (factor * LOG2E))
            e_t = jnp.exp2((s_t - top) * (factor * LOG2E))
            total = jnp.sum(e_i, 0, keepdims=True) + jnp.sum(e_t, 0, keepdims=True)
            inv = 1.0 / total
            p_i = (e_i * inv).astype(jnp.bfloat16)
            p_t = (e_t * inv).astype(jnp.bfloat16)
            rows = slice(h * HEAD, (h + 1) * HEAD)
            parts.append(nn(vit[rows], p_i) + nn(vtt[rows], p_t))
            lse[0, h : h + 1, at : at + size] = top * (factor * LOG2E) + jnp.log2(total)
        dst[start : start + size, :] = jnp.concatenate(parts, 0).T.astype(jnp.bfloat16)
        at += size


def back_kernel(block, valid, qi, ki, vi, qt, kt, vt, gi, gt, lse, d_i, d_t, aki, avi, akt, avt):
    dqi, dki, dvi = (d_i.at[k] for k in range(3))
    dqt, dkt, dvt = (d_t.at[k] for k in range(3))
    factor = HEAD**-0.5
    low = lax.broadcasted_iota(jnp.int32, (1, 2 * HEAD), 1) < HEAD
    zero = jnp.zeros((), jnp.bfloat16)
    bias = pad_bias(qt.shape[0], block, valid)
    kit, ktt = ki[...].T, kt[...].T
    masks = [low, ~low]
    at = 0
    first = True
    for which, start, size in query_blocks(qi.shape[0], qt.shape[0]):
        q_ref, g_ref, d_ref = (qi, gi, dqi) if which == 0 else (qt, gt, dqt)
        q, g = q_ref[start : start + size, :], g_ref[start : start + size, :]
        parts = []
        for h in range(2):
            q_h, g_h = jnp.where(masks[h], q, zero), jnp.where(masks[h], g, zero)
            stat = lse[0, h : h + 1, at : at + size]
            p_i = jnp.exp2(nt(ki[...], q_h) * (factor * LOG2E) - stat)
            p_t = jnp.exp2((nt(kt[...], q_h) + bias) * (factor * LOG2E) - stat)
            e_i, e_t = nt(vi[...], g_h), nt(vt[...], g_h)
            delta = jnp.sum(e_i * p_i, 0, keepdims=True) + jnp.sum(e_t * p_t, 0, keepdims=True)
            s_i = (p_i * (e_i - delta)).astype(jnp.bfloat16)
            s_t = (p_t * (e_t - delta)).astype(jnp.bfloat16)
            v_i = nn(p_i.astype(jnp.bfloat16), g_h)
            v_t = nn(p_t.astype(jnp.bfloat16), g_h)
            k_i = nn(s_i, q_h)
            k_t = nn(s_t, q_h)
            if first:
                avi[...], avt[...], aki[...], akt[...] = v_i, v_t, k_i, k_t
                first = False
            else:
                avi[...] += v_i
                avt[...] += v_t
                aki[...] += k_i
                akt[...] += k_t
            rows = slice(h * HEAD, (h + 1) * HEAD)
            parts.append(nn(kit[rows], s_i) + nn(ktt[rows], s_t))
        d_ref[start : start + size, :] = (jnp.concatenate(parts, 0).T * factor).astype(jnp.bfloat16)
        at += size
    dki[...] = (aki[...] * factor).astype(jnp.bfloat16)
    dkt[...] = (akt[...] * factor).astype(jnp.bfloat16)
    dvi[...] = avi[...].astype(jnp.bfloat16)
    dvt[...] = avt[...].astype(jnp.bfloat16)


def kind_specs(rows):
    return [pl.BlockSpec((None, rows, 2 * HEAD), partial(lambda k, p: (k, 0, p), k)) for k in range(3)]


def attend(qkv_img, qkv_txt, block, valid):
    n_i, n_t, inner = qkv_img.shape[1], qkv_txt.shape[1], qkv_img.shape[2]
    pairs = inner // (2 * HEAD)
    col = lambda rows: pl.BlockSpec((rows, 2 * HEAD), lambda p: (0, p))
    return pl.pallas_call(
        partial(attend_kernel, block, valid),
        grid=(pairs,),
        in_specs=kind_specs(n_i) + kind_specs(n_t),
        out_specs=[col(n_i), col(n_t), pl.BlockSpec((1, 2, n_i + n_t), lambda p: (p, 0, 0))],
        out_shape=[
            jax.ShapeDtypeStruct((n_i, inner), jnp.bfloat16),
            jax.ShapeDtypeStruct((n_t, inner), jnp.bfloat16),
            jax.ShapeDtypeStruct((pairs, 2, n_i + n_t), jnp.float32),
        ],
        compiler_params=pltpu.CompilerParams(vmem_limit_bytes=40 << 20),
        cost_estimate=pl.CostEstimate(flops=1 << 34, bytes_accessed=1 << 23, transcendentals=0),
    )(*([qkv_img] * 3 + [qkv_txt] * 3))


def attend_back(qkv_img, qkv_txt, g_img, g_txt, lse, block, valid):
    n_i, n_t, inner = qkv_img.shape[1], qkv_txt.shape[1], qkv_img.shape[2]
    pairs = inner // (2 * HEAD)
    col = lambda rows: pl.BlockSpec((rows, 2 * HEAD), lambda p: (0, p))
    return pl.pallas_call(
        partial(back_kernel, block, valid),
        grid=(pairs,),
        in_specs=kind_specs(n_i)
        + kind_specs(n_t)
        + [col(n_i), col(n_t), pl.BlockSpec((1, 2, n_i + n_t), lambda p: (p, 0, 0))],
        out_specs=[pl.BlockSpec((3, rows, 2 * HEAD), lambda p: (0, 0, p)) for rows in (n_i, n_t)],
        out_shape=[jax.ShapeDtypeStruct((3, rows, inner), jnp.bfloat16) for rows in (n_i, n_t)],
        scratch_shapes=[pltpu.VMEM((n, 2 * HEAD), jnp.float32) for n in (n_i, n_i, n_t, n_t)],
        compiler_params=pltpu.CompilerParams(vmem_limit_bytes=40 << 20),
        cost_estimate=pl.CostEstimate(flops=1 << 35, bytes_accessed=1 << 24, transcendentals=0),
    )(*([qkv_img] * 3 + [qkv_txt] * 3 + [g_img, g_txt, lse]))


def tn(a, b):
    return lax.dot_general(a, b, (((0,), (0,)), ((), ())), preferred_element_type=jnp.float32)


def norm_forward(values):
    center = jnp.mean(values, -1, keepdims=True)
    spread = jnp.mean(jnp.square(values - center), -1, keepdims=True)
    rstd = lax.rsqrt(spread + norm_eps)
    return ((values - center) * rstd, rstd)


def norm_backward(grads, hats, rstd):
    first = jnp.mean(grads, -1, keepdims=True)
    second = jnp.mean(grads * hats, -1, keepdims=True)
    return rstd * (grads - first - hats * second)


def tile(n):
    return 512 if n % 512 == 0 else 256 if n % 256 == 0 else n


def dot_kind(a, w, flip):
    return nt(a, w) if flip else nn(a, w)


def gelu_parts(x):
    c, a = math.sqrt(2.0 / math.pi), 0.044715
    square = x * x
    t = jnp.tanh(c * (x + a * (x * square)))
    slope = 0.5 * (1.0 + t) + 0.5 * x * (1.0 - t * t) * (c * (1.0 + 3.0 * a * square))
    return 0.5 * x * (1.0 + t), slope


def up_kernel(flip, at, ai, w, ht, hi, st, si):
    for s, (a, h, slope) in enumerate(((at, ht, st), (ai, hi, si))):
        value, d = gelu_parts(dot_kind(a[...], w[s], flip))
        h[...] = value.astype(jnp.bfloat16)
        slope[...] = d


def scaled_kernel(flip, at, ai, w, st, si, ot, oi):
    for s, (a, o, slope) in enumerate(((at, ot, st), (ai, oi, si))):
        o[...] = (dot_kind(a[...], w[s], flip) * slope[...]).astype(jnp.bfloat16)


def plain_kernel(flip, at, ai, w, ot, oi):
    for s, (a, o) in enumerate(((at, ot), (ai, oi))):
        o[...] = dot_kind(a[...], w[s], flip).astype(jnp.bfloat16)


def qkv_kernel(at, ai, w, ot, oi):
    for s, (a, o) in enumerate(((at, ot), (ai, oi))):
        o[0] = nt(a[...], w[s, 0]).astype(jnp.bfloat16)


def halves_kernel(flip, at, ai, w, top, own):
    for s, a in ((1, ai), (0, at)):
        half = a.shape[-2] // 2
        start = 0 if s == 1 else ai.shape[-2] // 2
        if len(a.shape) == 3:
            total = nn(a[0], w[s, 0])
            for k in range(1, a.shape[0]):
                total = total + nn(a[k], w[s, k])
        else:
            total = dot_kind(a[...], w[s], flip)
        own[start : start + half, :] = total[:half]
        top[start : start + half, :] = total[half:].astype(jnp.bfloat16)


def over_columns(kernel, operands, w, flip, extra, outs, columns):
    step = tile(columns)
    whole = lambda v: pl.BlockSpec(v.shape, lambda n: (0,) * v.ndim)
    if w.ndim == 4:
        w_spec = pl.BlockSpec(w.shape[:3] + (step,), lambda n: (0, 0, 0, n))
    elif flip:
        w_spec = pl.BlockSpec((2, step, w.shape[2]), lambda n: (0, n, 0))
    else:
        w_spec = pl.BlockSpec((2, w.shape[1], step), lambda n: (0, 0, n))
    by_tile = lambda v: pl.BlockSpec((v.shape[0], step), lambda n: (0, n))
    return pl.pallas_call(
        kernel,
        grid=(columns // step,),
        in_specs=[whole(v) for v in operands] + [w_spec] + [by_tile(v) for v in extra],
        out_specs=[by_tile(v) for v in outs],
        out_shape=outs,
        compiler_params=pltpu.CompilerParams(vmem_limit_bytes=40 << 20),
        cost_estimate=pl.CostEstimate(flops=1 << 33, bytes_accessed=1 << 23, transcendentals=0),
    )(*operands, w, *extra)


def shaped(rows, columns, kind):
    return jax.ShapeDtypeStruct((rows, columns), kind)


def up_and_slope(at, ai, w):
    n = w.shape[2]
    kinds = [jnp.bfloat16, jnp.bfloat16, jnp.float32, jnp.float32]
    rows = [at.shape[0], ai.shape[0]] * 2
    outs = [shaped(r, n, k) for r, k in zip(rows, kinds)]
    return over_columns(partial(up_kernel, False), [at, ai], w, False, [], outs, n)


def scaled(at, ai, w, st, si):
    outs = [shaped(v.shape[0], w.shape[2], jnp.bfloat16) for v in (at, ai)]
    return over_columns(partial(scaled_kernel, False), [at, ai], w, False, [st, si], outs, w.shape[2])


def plain(at, ai, w):
    outs = [shaped(v.shape[0], w.shape[1], jnp.bfloat16) for v in (at, ai)]
    return over_columns(partial(plain_kernel, True), [at, ai], w, True, [], outs, w.shape[1])


def halves(at, ai, w, flip):
    columns = w.shape[1] if flip else w.shape[-1]
    rows = (at.shape[-2] + ai.shape[-2]) // 2
    outs = [shaped(rows, columns, jnp.bfloat16), shaped(rows, columns, jnp.float32)]
    return over_columns(partial(halves_kernel, flip), [at, ai], w, flip, [], outs, columns)


def project_qkv(at, ai, w):
    inner = w.shape[2]
    whole = lambda v: pl.BlockSpec(v.shape, lambda n: (0, 0))
    outs = [jax.ShapeDtypeStruct((3, v.shape[0], inner), jnp.bfloat16) for v in (at, ai)]
    return pl.pallas_call(
        qkv_kernel,
        grid=(3,),
        in_specs=[whole(at), whole(ai), pl.BlockSpec((2, 1) + w.shape[2:], lambda n: (0, n, 0, 0))],
        out_specs=[pl.BlockSpec((1,) + v.shape[1:], lambda n: (n, 0, 0)) for v in outs],
        out_shape=outs,
        compiler_params=pltpu.CompilerParams(vmem_limit_bytes=40 << 20),
        cost_estimate=pl.CostEstimate(flops=1 << 33, bytes_accessed=1 << 23, transcendentals=0),
    )(at, ai, w)


def outer_kernel(n, *refs):
    left, right, out = refs[: 2 * n], refs[2 * n : 4 * n], refs[4 * n]
    for s in range(2):
        total = None
        for j in range(n):
            a = left[s * n + j]
            a = a[0] if len(a.shape) == 3 else a[...]
            term = tn(a, right[s * n + j][...])
            total = term if total is None else total + term
        if len(out.shape) == 3:
            out[s] = total.astype(jnp.bfloat16)
            continue
        ranks = out.shape[1]
        part = HEAD // ranks
        for p in range(ranks):
            rows = [total[h + p * part : h + (p + 1) * part] for h in range(0, total.shape[0], HEAD)]
            out[s, p] = jnp.concatenate(rows, 0).astype(jnp.bfloat16)


def outer(left_t, left_i, right_t, right_i, ranks=None):
    n = len(left_t)
    left, right = left_t + left_i, right_t + right_i
    columns = right[0].shape[1]
    if left[0].ndim == 3:
        step, steps = left[0].shape[2], left[0].shape[0]
        l_spec = lambda v: pl.BlockSpec((1,) + v.shape[1:], lambda m: (m, 0, 0))
    else:
        width = left[0].shape[1]
        step = 512 if width % 512 == 0 else width if width < 512 else 256
        steps = width // step
        l_spec = lambda v: pl.BlockSpec((v.shape[0], step), lambda m: (0, m))
    return pl.pallas_call(
        partial(outer_kernel, n),
        grid=(steps,),
        in_specs=[l_spec(v) for v in left] + [pl.BlockSpec(v.shape, lambda m: (0, 0)) for v in right],
        out_specs=pl.BlockSpec((2, step, columns), lambda m: (0, m, 0))
        if ranks is None
        else pl.BlockSpec((2, ranks, step // ranks, columns), lambda m: (0, 0, m, 0)),
        out_shape=jax.ShapeDtypeStruct(
            (2, steps * step, columns) if ranks is None else (2, ranks, steps * step // ranks, columns),
            jnp.bfloat16,
        ),
        compiler_params=pltpu.CompilerParams(vmem_limit_bytes=52 << 20),
        cost_estimate=pl.CostEstimate(flops=1 << 34, bytes_accessed=1 << 24, transcendentals=0),
    )(*left, *right)


class Group:
    def __init__(self, size):
        self.size = size
        self.evens = [2 * k for k in range(size // 2)]
        self.odds = [2 * k + 1 for k in range(size // 2)]
        self.order = self.evens + self.odds

    def send(self, value, flip):
        return lax.ppermute(value, "tensor", [(t, t ^ flip) for t in range(self.size)])

    def gather(self, own):
        evens = [own] + [self.send(own, flip) for flip in self.evens[1:]]
        return evens + [self.send(value, 1) for value in evens]


MESH = pl.DeviceIdType.MESH


def flip_bits(index, flip, size):
    total, bit = 0, 1
    while bit < size:
        digit = lax.rem(lax.div(index, bit), 2)
        total = total + bit * ((1 - digit) if flip & bit else digit)
        bit *= 2
    return total


class Data:
    def __init__(self, size):
        self.size = size
        self.nx = math.isqrt(size // 2)
        self.nz = size // self.nx


def pass_kernel(*refs):
    pass


def gate(values, others):
    others = jax.tree.leaves(list(others))
    n = len(values)
    anywhere = pl.BlockSpec(memory_space=pl.ANY)
    return pl.pallas_call(
        pass_kernel,
        in_specs=[anywhere] * (n + len(others)),
        out_specs=[anywhere] * n,
        out_shape=[jax.ShapeDtypeStruct(v.shape, v.dtype) for v in values],
        input_output_aliases={i: i for i in range(n)},
        compiler_params=pltpu.CompilerParams(vmem_limit_bytes=1 << 20),
        cost_estimate=pl.CostEstimate(flops=1 << 10, bytes_accessed=1 << 10, transcendentals=0),
    )(*values, *others)


def after(value, *others):
    return gate([value], others)[0]


def greet(n_dp, size):
    me_d, me_t = lax.axis_index("dp"), lax.axis_index("tensor")
    barrier = pltpu.get_barrier_semaphore()
    for k in range(1, n_dp):
        pl.semaphore_signal(barrier, inc=1, device_id=(flip_bits(me_d, k, n_dp), me_t), device_id_type=MESH)
    for k in range(1, size):
        pl.semaphore_signal(barrier, inc=1, device_id=(me_d, flip_bits(me_t, k, size)), device_id_type=MESH)
    pl.semaphore_wait(barrier, n_dp + size - 2)


def to_data(n_dp, source, target, send, recv):
    me_d, me_t = lax.axis_index("dp"), lax.axis_index("tensor")
    copies = []
    for k in range(1, n_dp):
        peer = flip_bits(me_d, k, n_dp)
        copy = pltpu.make_async_remote_copy(
            src_ref=source(peer),
            dst_ref=target.at[me_d],
            send_sem=send.at[k - 1],
            recv_sem=recv.at[k - 1],
            device_id=(peer, me_t),
            device_id_type=MESH,
        )
        copy.start()
        copies.append(copy)
    return copies


def to_tensor(size, source, target, send, recv):
    me_d, me_t = lax.axis_index("dp"), lax.axis_index("tensor")
    copies = []
    for k in range(1, size):
        peer = flip_bits(me_t, k, size)
        copy = pltpu.make_async_remote_copy(
            src_ref=source(peer),
            dst_ref=target.at[me_t],
            send_sem=send.at[k - 1],
            recv_sem=recv.at[k - 1],
            device_id=(me_d, peer),
            device_id_type=MESH,
        )
        copy.start()
        copies.append(copy)
    return copies


def finish(copies):
    for copy in copies:
        copy.wait()


def mod_kernel(n_dp, size, cond, w, mod_out, act_out, conds, parts, got, own, sd1, rd1, sd2, rd2, st, rt):
    me_d, me_t = lax.axis_index("dp"), lax.axis_index("tensor")
    rows, part, columns = conds.shape[1], w.shape[1], w.shape[2] // 2
    greet(n_dp, size)
    copies = to_data(n_dp, lambda peer: cond.at[peer], conds, sd1, rd1)
    conds[me_d] = cond[me_d]
    finish(copies)
    value = conds[...].reshape(n_dp * rows, conds.shape[2])[:, :part]
    act = (value * jax.nn.sigmoid(value)).astype(jnp.bfloat16)
    act_out[...] = act
    place = lax.rem(lax.broadcasted_iota(jnp.int32, (n_dp * rows, 1), 0), rows)
    first = lax.rem(place, rows // 2) < rows // 4
    mixed = [
        jnp.where(first, nn(act, w[0, :, cut]), nn(act, w[1, :, cut]))
        for cut in (slice(0, columns), slice(columns, 2 * columns))
    ]
    mixed = jnp.where(place < rows // 2, mixed[0], mixed[1])
    parts[...] = mixed.reshape(n_dp, rows, columns)
    copies = to_data(n_dp, lambda peer: parts.at[peer], got, sd2, rd2)
    got[me_d] = parts[me_d]
    finish(copies)
    total = got[0]
    for p in range(1, n_dp):
        total = total + got[p]
    own[...] = total
    copies = to_tensor(size, lambda peer: own, mod_out, st, rt)
    mod_out[me_t] = total
    finish(copies)


def mod_forward(n_dp, size, cond, w_mod):
    slots, width = cond.shape
    part, columns = w_mod.shape[1:]
    rows, lanes = 4 * slots, -(-part // 128) * 128
    laid = cond.astype(jnp.float32).reshape(slots, n_dp, part).transpose(1, 0, 2)
    laid = jnp.concatenate([laid, laid, laid, laid], 1)
    laid = jnp.pad(laid, ((0, 0), (0, 0), (0, lanes - part)))
    dma = pltpu.SemaphoreType.DMA
    return pl.pallas_call(
        partial(mod_kernel, n_dp, size),
        in_specs=[pl.BlockSpec(memory_space=pltpu.VMEM)] * 2,
        out_specs=[pl.BlockSpec(memory_space=pltpu.VMEM)] * 2,
        out_shape=[
            jax.ShapeDtypeStruct((size, rows, columns // 2), jnp.float32),
            jax.ShapeDtypeStruct((n_dp * rows, part), jnp.bfloat16),
        ],
        scratch_shapes=[
            pltpu.VMEM((n_dp, rows, lanes), jnp.float32),
            pltpu.VMEM((n_dp, rows, columns // 2), jnp.float32),
            pltpu.VMEM((n_dp, rows, columns // 2), jnp.float32),
            pltpu.VMEM((rows, columns // 2), jnp.float32),
            dma((n_dp - 1,)), dma((n_dp - 1,)), dma((n_dp - 1,)), dma((n_dp - 1,)),
            dma((size - 1,)), dma((size - 1,)),
        ],
        compiler_params=pltpu.CompilerParams(
            collective_id=0, has_side_effects=True, vmem_limit_bytes=40 << 20
        ),
        cost_estimate=pl.CostEstimate(flops=1 << 33, bytes_accessed=1 << 21, transcendentals=0),
    )(laid, w_mod)


def mod_back_kernel(n_dp, size, terms, lost, act, w, grad, cond_out, loss_out, halves, sums, every, cparts, cgot, cfull,
                    lhalves, lsums, levery, st1, rt1, sd1, rd1, sd2, rd2, st2, rt2, st3, rt3, sd3, rd3):
    me_d, me_t = lax.axis_index("dp"), lax.axis_index("tensor")
    rows, columns = terms.shape[1:]
    part = w.shape[1]
    greet(n_dp, size)
    copies = to_tensor(size, lambda peer: terms.at[peer], halves, st1, rt1)
    copies += to_tensor(size, lambda peer: lost, lhalves, st3, rt3)
    halves[me_t] = terms[me_t]
    lhalves[me_t] = lost[...]
    finish(copies)
    total, loss = halves[0], lhalves[0]
    for t in range(1, size):
        total, loss = total + halves[t], loss + lhalves[t]
    sums[...] = total
    lsums[...] = loss
    copies = to_data(n_dp, lambda peer: sums, every, sd1, rd1)
    copies += to_data(n_dp, lambda peer: lsums, levery, sd3, rd3)
    every[me_d] = total
    levery[me_d] = loss
    finish(copies)
    loss = levery[0]
    for p in range(1, n_dp):
        loss = loss + levery[p]
    loss_out[...] = loss
    dmod = every[...].reshape(n_dp * rows, columns).astype(jnp.bfloat16)
    place = lax.rem(lax.broadcasted_iota(jnp.int32, (n_dp * rows, 1), 0), rows)
    quarter = rows // 4
    cuts = (slice(0, columns), slice(columns, 2 * columns))
    back = [nt(dmod, w[s, :, cut]) for cut in cuts for s in range(2)]
    mixed = back[0]
    for n in range(1, 4):
        mixed = jnp.where(place < n * quarter, mixed, back[n])
    cparts[:, :, :part] = mixed.reshape(n_dp, rows, part)
    copies = to_data(n_dp, lambda peer: cparts.at[peer], cgot, sd2, rd2)
    cgot[me_d] = cparts[me_d]
    for n in range(4):
        mask = (place >= n * quarter) & (place < (n + 1) * quarter)
        picked = jnp.where(mask, act[...], jnp.zeros((), jnp.bfloat16))
        grad[n % 2, :, cuts[n // 2]] = tn(picked, dmod)
    finish(copies)
    copies = to_tensor(size, lambda peer: cgot, cfull, st2, rt2)
    cfull[me_t] = cgot[...]
    finish(copies)
    full = cfull[0]
    for t in range(1, size):
        full = full + cfull[t]
    cond_out[...] = full


def mod_backward(n_dp, size, terms, lost, act, w_mod):
    rows, columns = terms.shape[1:]
    part = w_mod.shape[1]
    lanes = -(-part // 128) * 128
    dma = pltpu.SemaphoreType.DMA
    f32 = jnp.float32
    return pl.pallas_call(
        partial(mod_back_kernel, n_dp, size),
        in_specs=[pl.BlockSpec(memory_space=pltpu.VMEM)] * 4,
        out_specs=[pl.BlockSpec(memory_space=pltpu.VMEM)] * 3,
        out_shape=[
            jax.ShapeDtypeStruct(w_mod.shape, f32),
            jax.ShapeDtypeStruct((n_dp, rows, lanes), f32),
            jax.ShapeDtypeStruct((8, 128), f32),
        ],
        scratch_shapes=[
            pltpu.VMEM((size, rows, columns), f32),
            pltpu.VMEM((rows, columns), f32),
            pltpu.VMEM((n_dp, rows, columns), f32),
            pltpu.VMEM((n_dp, rows, lanes), f32),
            pltpu.VMEM((n_dp, rows, lanes), f32),
            pltpu.VMEM((size, n_dp, rows, lanes), f32),
            pltpu.VMEM((size, 8, 128), f32),
            pltpu.VMEM((8, 128), f32),
            pltpu.VMEM((n_dp, 8, 128), f32),
            dma((size - 1,)), dma((size - 1,)),
            dma((n_dp - 1,)), dma((n_dp - 1,)), dma((n_dp - 1,)), dma((n_dp - 1,)),
            dma((size - 1,)), dma((size - 1,)),
            dma((size - 1,)), dma((size - 1,)), dma((n_dp - 1,)), dma((n_dp - 1,)),
        ],
        compiler_params=pltpu.CompilerParams(
            collective_id=1, has_side_effects=True, vmem_limit_bytes=40 << 20
        ),
        cost_estimate=pl.CostEstimate(flops=1 << 33, bytes_accessed=1 << 21, transcendentals=0),
    )(terms, lost, act, w_mod)


def on_device(
    data,
    group,
    image,
    text,
    cond,
    teacher_image,
    teacher_text,
    grad_image,
    grad_text,
    live,
    w_mod,
    w_qkv,
    w_out,
    w_up,
    w_down,
):
    slots, width = cond.shape
    rows_i, rows_t = image.shape[1], text.shape[1]
    pad_t = -(-rows_t // 8) * 8
    size = group.size
    n_dp = data.size
    heads = w_qkv.shape[2]
    odd = heads % 2

    wide = jnp.concatenate([w_qkv, w_out[:, None]], 1)
    f_wide = lax.all_gather(wide, "dp", axis=3, tiled=True)
    f_up = lax.all_gather(w_up, "dp", axis=1, tiled=True)
    f_down = lax.all_gather(w_down, "dp", axis=1, tiled=True)
    if odd:
        f_wide = jnp.pad(f_wide, ((0, 0), (0, 0), (0, odd), (0, 0), (0, 0)))
    f_wide = f_wide.reshape(2, 4, -1, width)
    f_qkv, f_out = f_wide[:, :3], f_wide[:, 3]

    mod_all, act_all = mod_forward(n_dp, size, cond, w_mod)
    mods = jnp.stack(
        [
            jnp.stack(
                [
                    jnp.stack([mod_all[:, (h * 2 + s) * slots + j] for h in range(2)], 1).reshape(6, width)
                    for s in range(2)
                ]
            )
            for j in range(slots)
        ]
    )

    is_image = (lax.broadcasted_iota(jnp.int32, (rows_i + pad_t, 1), 0) < rows_i)
    is_real = (lax.broadcasted_iota(jnp.int32, (rows_i + pad_t, 1), 0) < rows_i + rows_t)

    def merged(img, txt, j):
        return jnp.concatenate([img[j], jnp.pad(txt[j], ((0, pad_t - rows_t), (0, 0)))], 0)

    def pick(j, span):
        return jnp.where(is_image, mods[j, 1, span][None], mods[j, 0, span][None])

    def token_sums(values):
        return jnp.stack([jnp.sum(values[rows_i:], 0), jnp.sum(values[:rows_i], 0)])

    def spread(blocks):
        return (
            jnp.concatenate([b[:rows_i] for b in blocks], 0),
            jnp.concatenate([b[rows_i:] for b in blocks], 0),
        )

    half_i = size // 2 * rows_i

    def scatter_begin(rows_txt, rows_img, w, flip):
        top, own = halves(rows_txt, rows_img, w, flip)
        got = group.send(top, 1)
        blocks = []
        for k in range(size // 2):
            cuts = (slice(k * rows_i, (k + 1) * rows_i), slice(half_i + k * pad_t, half_i + (k + 1) * pad_t))
            blocks.append(jnp.concatenate([own[cut] + got[cut].astype(jnp.float32) for cut in cuts], 0))
        blocks = [blocks[0]] + [block.astype(jnp.bfloat16) for block in blocks[1:]]
        return blocks, [group.send(blocks[k], 2 * k) for k in range(1, size // 2)]

    def scatter_end(started, *others):
        blocks, got = started
        total = blocks[0]
        for value in got:
            total = total + after(value, *others).astype(jnp.float32)
        return total

    def gather_begin(own):
        return [own], [group.send(own, flip) for flip in group.evens[1:]]

    def gather_end(started, *others):
        own, got = started
        evens = own + [after(value, *others) for value in got]
        odds = group.send(jnp.concatenate(evens, 0), 1)
        return spread(evens + [odds[k : k + rows_i + pad_t] for k in range(0, odds.shape[0], rows_i + pad_t)])

    count = 3.0 * (n_dp // 2) * size * (rows_i + rows_t)

    slot = [dict() for j in range(slots)]
    for j, v in enumerate(slot):
        v["x"] = merged(image, text, j).astype(jnp.float32)
        v["hat1"], v["rstd1"] = norm_forward(v["x"])
        h1 = (v["hat1"] * (1.0 + pick(j, 1)) + pick(j, 0)).astype(jnp.bfloat16)
        v["go"] = gather_begin(h1)
    for j, v in enumerate(slot):
        v["h1_i"], v["h1_t"] = gather_end(v["go"], slot[-1]["go"][0])
    for j, v in enumerate(slot):
        if j:
            v["h1_i"] = after(v["h1_i"], slot[j - 1]["att_i"])
        v["qkv_t"], v["qkv_i"] = project_qkv(v["h1_t"], v["h1_i"], f_qkv)
        v["att_i"], v["att_t"], v["lse"] = attend(v["qkv_i"], v["qkv_t"], pad_t, rows_t)
    for j, v in enumerate(slot):
        v["go"] = scatter_begin(v["att_t"], v["att_i"], f_out, False)
    for j, v in enumerate(slot):
        v["y"] = scatter_end(v["go"], slot[-1]["go"][0])
        v["mid"] = v["x"] + pick(j, 2) * v["y"]
        v["hat2"], v["rstd2"] = norm_forward(v["mid"])
        h2 = (v["hat2"] * (1.0 + pick(j, 4)) + pick(j, 3)).astype(jnp.bfloat16)
        v["go"] = gather_begin(h2)
    for j, v in enumerate(slot):
        v["h2_i"], v["h2_t"] = gather_end(v["go"], slot[-1]["go"][0])
    for j, v in enumerate(slot):
        if j:
            v["h2_i"] = after(v["h2_i"], slot[j - 1]["hid_i"])
        v["hid_t"], v["hid_i"], v["slope_t"], v["slope_i"] = up_and_slope(v["h2_t"], v["h2_i"], f_up)
    f_down = after(f_down, slot[-1]["hid_i"])
    for j, v in enumerate(slot):
        v["go"] = scatter_begin(v["hid_t"], v["hid_i"], f_down, True)
    for j, v in enumerate(slot):
        v["m"] = scatter_end(v["go"], slot[-1]["go"][0])
        out = v["mid"] + pick(j, 5) * v["m"]
        mask = jnp.where(is_real, live[j].astype(jnp.float32), 0.0)
        err = mask * (out - merged(teacher_image, teacher_text, j).astype(jnp.float32))
        v["loss"] = jnp.sum(err * err)
        v["cot"] = mask * merged(grad_image, grad_text, j).astype(jnp.float32) + 2.0 * err
        v["dgate2"] = token_sums(v["cot"] * v["m"])
        dm = (v["cot"] * pick(j, 5)).astype(jnp.bfloat16)
        v["go"] = gather_begin(dm)
    for j, v in enumerate(slot):
        v["dm_i"], v["dm_t"] = gather_end(v["go"], slot[-1]["go"][0])

    here = lax.axis_index("dp")

    both = lambda a, b, *ranks: outer(*([v[name + e] for v in slot] for name in (a, b) for e in ("_t", "_i")), *ranks)

    def reduced(grads):
        return lax.psum_scatter(grads.reshape(2, -1, grads.shape[-1]), "dp", scatter_dimension=1, tiled=True)

    g_down = both("dm", "hid")
    done_down = reduced(g_down)
    for j, v in enumerate(slot):
        v["dm_i"] = after(v["dm_i"], g_down if j == 0 else slot[j - 1]["dpre_i"])
        v["dpre_t"], v["dpre_i"] = scaled(v["dm_t"], v["dm_i"], f_down, v["slope_t"], v["slope_i"])
        v["go"] = scatter_begin(v["dpre_t"], v["dpre_i"], f_up, True)
    g_up = both("h2", "dpre")
    done_up = reduced(g_up)
    for j, v in enumerate(slot):
        v["dh2"] = scatter_end(v["go"], g_up)
        v["dshift2"] = token_sums(v["dh2"])
        v["dscale2"] = token_sums(v["dh2"] * v["hat2"])
        v["dmid"] = v["cot"] + norm_backward(v["dh2"] * (1.0 + pick(j, 4)), v["hat2"], v["rstd2"])
        v["dgate1"] = token_sums(v["dmid"] * v["y"])
        dy = (v["dmid"] * pick(j, 2)).astype(jnp.bfloat16)
        v["go"] = gather_begin(dy)
    for j, v in enumerate(slot):
        v["dy_i"], v["dy_t"] = gather_end(v["go"], slot[-1]["go"][0])
    g_out = both("att", "dy", n_dp)
    done_out = reduced(g_out)
    for j, v in enumerate(slot):
        v["dy_i"] = after(v["dy_i"], g_out, done_down) if j == 0 else after(v["dy_i"], slot[j - 1]["dqkv_i"])
        g_t, g_i = plain(v["dy_t"], v["dy_i"], f_out)
        v["dqkv_i"], v["dqkv_t"] = attend_back(v["qkv_i"], v["qkv_t"], g_i, g_t, v["lse"], pad_t, rows_t)
    g_qkv = both("dqkv", "h1", n_dp)
    done_qkv = reduced(g_qkv)
    for j, v in enumerate(slot):
        v["dqkv_i"] = after(v["dqkv_i"], g_qkv)
        v["go"] = scatter_begin(v["dqkv_t"], v["dqkv_i"], f_qkv, False)
    for j, v in enumerate(slot):
        v["dh1"] = scatter_end(v["go"], slot[-1]["go"][0])
    grad_i, grad_t, terms = [], [], []
    for j in range(slots):
        v = slot[j]
        dshift1 = token_sums(v["dh1"])
        dscale1 = token_sums(v["dh1"] * v["hat1"])
        back = v["dmid"] + norm_backward(v["dh1"] * (1.0 + pick(j, 1)), v["hat1"], v["rstd1"])
        grad_i.append(back[:rows_i])
        grad_t.append(back[rows_i : rows_i + rows_t])
        terms.append(
            jnp.stack([dshift1, dscale1, v["dgate1"], v["dshift2"], v["dscale2"], v["dgate2"]], 1)
        )
    lost = jnp.full((8, 128), sum(v["loss"] for v in slot))
    laid = jnp.stack(terms, 1).reshape(2 * slots, size, 2, -1).transpose(1, 2, 0, 3)
    laid = laid.reshape(size, 4 * slots, -1)
    laid = after(laid, done_up)
    done_mod, cond_rows, loss_rows = mod_backward(n_dp, size, laid, lost, act_all, w_mod)
    loss = loss_rows[0, 0] / (count * width)
    cond_rows = cond_rows[:, :, : w_mod.shape[1]]
    cond_total = jnp.sum(cond_rows.reshape(n_dp, 4, slots, -1), 1).transpose(1, 0, 2).reshape(slots, width)
    unused_value, silu_pull = jax.vjp(jax.nn.silu, cond.astype(jnp.float32))
    grad_cond = silu_pull(cond_total)[0]
    done_down = done_down.astype(jnp.float32)
    done_up = done_up.astype(jnp.float32)
    done_out = done_out.astype(jnp.float32).reshape(2, heads + odd, -1, width)
    done_qkv = done_qkv.astype(jnp.float32).reshape(2, 3, heads + odd, -1, width)
    if odd:
        done_qkv, done_out = done_qkv[:, :, :heads], done_out[:, :heads]
    return (
        loss,
        done_mod,
        done_qkv,
        done_out,
        done_up,
        done_down,
        jnp.stack(grad_i),
        jnp.stack(grad_t),
        grad_cond,
    )


def solution(mesh):
    return jax.shard_map(
        partial(on_device, Data(mesh.shape["dp"]), Group(mesh.shape["tensor"])),
        mesh=mesh,
        in_specs=(
            P("dp", "tensor", None),
            P("dp", "tensor", None),
            P("dp", None),
            P("dp", "tensor", None),
            P("dp", "tensor", None),
            P("dp", "tensor", None),
            P("dp", "tensor", None),
            P("dp"),
            P(None, "dp", "tensor"),
            P(None, None, "tensor", "dp", None),
            P(None, "tensor", "dp", None),
            P(None, "dp", "tensor"),
            P(None, "dp", "tensor"),
        ),
        out_specs=(
            P(),
            P(None, "dp", "tensor"),
            P(None, None, "tensor", "dp", None),
            P(None, "tensor", "dp", None),
            P(None, "dp", "tensor"),
            P(None, "dp", "tensor"),
            P("dp", "tensor", None),
            P("dp", "tensor", None),
            P("dp", None),
        ),
        check_vma=False,
    )
```

```python
import math
from functools import partial

import jax
import jax.numpy as jnp
from jax import lax
from jax.experimental import pallas as pl
from jax.experimental.pallas import tpu as pltpu
from jax.sharding import PartitionSpec as P

norm_eps = 1e-06

LOG2E = math.log2(math.e)
HEAD = 64


def nt(a, b):
    return lax.dot_general(a, b, (((1,), (1,)), ((), ())), preferred_element_type=jnp.float32)


def nn(a, b):
    return jnp.dot(a, b, preferred_element_type=jnp.float32)


def query_blocks(rows_img, rows_txt):
    step = 256 if rows_img % 256 == 0 else rows_img
    return [(0, s, step) for s in range(0, rows_img, step)] + [(1, 0, rows_txt)]


def pad_bias(rows, block, valid):
    place = lax.broadcasted_iota(jnp.int32, (rows, 1), 0)
    return jnp.where(lax.rem(place, block) < valid, 0.0, -1e30).astype(jnp.float32)


def attend_kernel(block, valid, qi, ki, vi, qt, kt, vt, oi, ot, lse):
    factor = HEAD**-0.5
    low = lax.broadcasted_iota(jnp.int32, (1, 2 * HEAD), 1) < HEAD
    zero = jnp.zeros((), jnp.bfloat16)
    bias = pad_bias(qt.shape[0], block, valid)
    vit, vtt = vi[...].T, vt[...].T
    keys = []
    for h in range(2):
        mask = low if h == 0 else ~low
        keys.append((jnp.where(mask, ki[...], zero), jnp.where(mask, kt[...], zero)))
    at = 0
    for which, start, size in query_blocks(qi.shape[0], qt.shape[0]):
        src, dst = (qi, oi) if which == 0 else (qt, ot)
        q = src[start : start + size, :]
        parts = []
        for h in range(2):
            s_i = nt(keys[h][0], q)
            s_t = nt(keys[h][1], q) + bias
            top = jnp.maximum(
                jnp.max(s_i, 0, keepdims=True), jnp.max(s_t, 0, keepdims=True)
            )
            e_i = jnp.exp2((s_i - top) * (factor * LOG2E))
            e_t = jnp.exp2((s_t - top) * (factor * LOG2E))
            total = jnp.sum(e_i, 0, keepdims=True) + jnp.sum(e_t, 0, keepdims=True)
            inv = 1.0 / total
            p_i = (e_i * inv).astype(jnp.bfloat16)
            p_t = (e_t * inv).astype(jnp.bfloat16)
            rows = slice(h * HEAD, (h + 1) * HEAD)
            parts.append(nn(vit[rows], p_i) + nn(vtt[rows], p_t))
            lse[0, h : h + 1, at : at + size] = top * (factor * LOG2E) + jnp.log2(total)
        dst[start : start + size, :] = jnp.concatenate(parts, 0).T.astype(jnp.bfloat16)
        at += size


def back_kernel(block, valid, qi, ki, vi, qt, kt, vt, gi, gt, lse, d_i, d_t, aki, avi, akt, avt):
    dqi, dki, dvi = (d_i.at[k] for k in range(3))
    dqt, dkt, dvt = (d_t.at[k] for k in range(3))
    factor = HEAD**-0.5
    low = lax.broadcasted_iota(jnp.int32, (1, 2 * HEAD), 1) < HEAD
    zero = jnp.zeros((), jnp.bfloat16)
    bias = pad_bias(qt.shape[0], block, valid)
    kit, ktt = ki[...].T, kt[...].T
    masks = [low, ~low]
    at = 0
    first = True
    for which, start, size in query_blocks(qi.shape[0], qt.shape[0]):
        q_ref, g_ref, d_ref = (qi, gi, dqi) if which == 0 else (qt, gt, dqt)
        q, g = q_ref[start : start + size, :], g_ref[start : start + size, :]
        parts = []
        for h in range(2):
            q_h, g_h = jnp.where(masks[h], q, zero), jnp.where(masks[h], g, zero)
            stat = lse[0, h : h + 1, at : at + size]
            p_i = jnp.exp2(nt(ki[...], q_h) * (factor * LOG2E) - stat)
            p_t = jnp.exp2((nt(kt[...], q_h) + bias) * (factor * LOG2E) - stat)
            e_i, e_t = nt(vi[...], g_h), nt(vt[...], g_h)
            delta = jnp.sum(e_i * p_i, 0, keepdims=True) + jnp.sum(e_t * p_t, 0, keepdims=True)
            s_i = (p_i * (e_i - delta)).astype(jnp.bfloat16)
            s_t = (p_t * (e_t - delta)).astype(jnp.bfloat16)
            v_i = nn(p_i.astype(jnp.bfloat16), g_h)
            v_t = nn(p_t.astype(jnp.bfloat16), g_h)
            k_i = nn(s_i, q_h)
            k_t = nn(s_t, q_h)
            if first:
                avi[...], avt[...], aki[...], akt[...] = v_i, v_t, k_i, k_t
                first = False
            else:
                avi[...] += v_i
                avt[...] += v_t
                aki[...] += k_i
                akt[...] += k_t
            rows = slice(h * HEAD, (h + 1) * HEAD)
            parts.append(nn(kit[rows], s_i) + nn(ktt[rows], s_t))
        d_ref[start : start + size, :] = (jnp.concatenate(parts, 0).T * factor).astype(jnp.bfloat16)
        at += size
    dki[...] = (aki[...] * factor).astype(jnp.bfloat16)
    dkt[...] = (akt[...] * factor).astype(jnp.bfloat16)
    dvi[...] = avi[...].astype(jnp.bfloat16)
    dvt[...] = avt[...].astype(jnp.bfloat16)


def kind_specs(rows):
    return [pl.BlockSpec((None, rows, 2 * HEAD), partial(lambda k, p: (k, 0, p), k)) for k in range(3)]


def attend(qkv_img, qkv_txt, block, valid):
    n_i, n_t, inner = qkv_img.shape[1], qkv_txt.shape[1], qkv_img.shape[2]
    pairs = inner // (2 * HEAD)
    col = lambda rows: pl.BlockSpec((rows, 2 * HEAD), lambda p: (0, p))
    return pl.pallas_call(
        partial(attend_kernel, block, valid),
        grid=(pairs,),
        in_specs=kind_specs(n_i) + kind_specs(n_t),
        out_specs=[col(n_i), col(n_t), pl.BlockSpec((1, 2, n_i + n_t), lambda p: (p, 0, 0))],
        out_shape=[
            jax.ShapeDtypeStruct((n_i, inner), jnp.bfloat16),
            jax.ShapeDtypeStruct((n_t, inner), jnp.bfloat16),
            jax.ShapeDtypeStruct((pairs, 2, n_i + n_t), jnp.float32),
        ],
        compiler_params=pltpu.CompilerParams(vmem_limit_bytes=40 << 20),
        cost_estimate=pl.CostEstimate(flops=1 << 34, bytes_accessed=1 << 23, transcendentals=0),
    )(*([qkv_img] * 3 + [qkv_txt] * 3))


def attend_back(qkv_img, qkv_txt, g_img, g_txt, lse, block, valid):
    n_i, n_t, inner = qkv_img.shape[1], qkv_txt.shape[1], qkv_img.shape[2]
    pairs = inner // (2 * HEAD)
    col = lambda rows: pl.BlockSpec((rows, 2 * HEAD), lambda p: (0, p))
    return pl.pallas_call(
        partial(back_kernel, block, valid),
        grid=(pairs,),
        in_specs=kind_specs(n_i)
        + kind_specs(n_t)
        + [col(n_i), col(n_t), pl.BlockSpec((1, 2, n_i + n_t), lambda p: (p, 0, 0))],
        out_specs=[pl.BlockSpec((3, rows, 2 * HEAD), lambda p: (0, 0, p)) for rows in (n_i, n_t)],
        out_shape=[jax.ShapeDtypeStruct((3, rows, inner), jnp.bfloat16) for rows in (n_i, n_t)],
        scratch_shapes=[pltpu.VMEM((n, 2 * HEAD), jnp.float32) for n in (n_i, n_i, n_t, n_t)],
        compiler_params=pltpu.CompilerParams(vmem_limit_bytes=40 << 20),
        cost_estimate=pl.CostEstimate(flops=1 << 35, bytes_accessed=1 << 24, transcendentals=0),
    )(*([qkv_img] * 3 + [qkv_txt] * 3 + [g_img, g_txt, lse]))


def tn(a, b):
    return lax.dot_general(a, b, (((0,), (0,)), ((), ())), preferred_element_type=jnp.float32)


def norm_forward(values):
    center = jnp.mean(values, -1, keepdims=True)
    spread = jnp.mean(jnp.square(values - center), -1, keepdims=True)
    rstd = lax.rsqrt(spread + norm_eps)
    return ((values - center) * rstd, rstd)


def norm_backward(grads, hats, rstd):
    first = jnp.mean(grads, -1, keepdims=True)
    second = jnp.mean(grads * hats, -1, keepdims=True)
    return rstd * (grads - first - hats * second)


def tile(n):
    return 512 if n % 512 == 0 else 256 if n % 256 == 0 else n


def dot_kind(a, w, flip):
    return nt(a, w) if flip else nn(a, w)


def gelu_parts(x):
    c, a = math.sqrt(2.0 / math.pi), 0.044715
    square = x * x
    t = jnp.tanh(c * (x + a * (x * square)))
    slope = 0.5 * (1.0 + t) + 0.5 * x * (1.0 - t * t) * (c * (1.0 + 3.0 * a * square))
    return 0.5 * x * (1.0 + t), slope


def up_kernel(flip, at, ai, w, ht, hi, st, si):
    for s, (a, h, slope) in enumerate(((at, ht, st), (ai, hi, si))):
        value, d = gelu_parts(dot_kind(a[...], w[s], flip))
        h[...] = value.astype(jnp.bfloat16)
        slope[...] = d


def scaled_kernel(flip, at, ai, w, st, si, ot, oi):
    for s, (a, o, slope) in enumerate(((at, ot, st), (ai, oi, si))):
        o[...] = (dot_kind(a[...], w[s], flip) * slope[...]).astype(jnp.bfloat16)


def plain_kernel(flip, at, ai, w, ot, oi):
    for s, (a, o) in enumerate(((at, ot), (ai, oi))):
        o[...] = dot_kind(a[...], w[s], flip).astype(jnp.bfloat16)


def qkv_kernel(at, ai, w, ot, oi):
    for s, (a, o) in enumerate(((at, ot), (ai, oi))):
        o[0] = nt(a[...], w[s, 0]).astype(jnp.bfloat16)


def halves_kernel(flip, at, ai, w, top, own):
    for s, a in ((1, ai), (0, at)):
        half = a.shape[-2] // 2
        start = 0 if s == 1 else ai.shape[-2] // 2
        if len(a.shape) == 3:
            total = nn(a[0], w[s, 0])
            for k in range(1, a.shape[0]):
                total = total + nn(a[k], w[s, k])
        else:
            total = dot_kind(a[...], w[s], flip)
        own[start : start + half, :] = total[:half]
        top[start : start + half, :] = total[half:].astype(jnp.bfloat16)


def over_columns(kernel, operands, w, flip, extra, outs, columns):
    step = tile(columns)
    whole = lambda v: pl.BlockSpec(v.shape, lambda n: (0,) * v.ndim)
    if w.ndim == 4:
        w_spec = pl.BlockSpec(w.shape[:3] + (step,), lambda n: (0, 0, 0, n))
    elif flip:
        w_spec = pl.BlockSpec((2, step, w.shape[2]), lambda n: (0, n, 0))
    else:
        w_spec = pl.BlockSpec((2, w.shape[1], step), lambda n: (0, 0, n))
    by_tile = lambda v: pl.BlockSpec((v.shape[0], step), lambda n: (0, n))
    return pl.pallas_call(
        kernel,
        grid=(columns // step,),
        in_specs=[whole(v) for v in operands] + [w_spec] + [by_tile(v) for v in extra],
        out_specs=[by_tile(v) for v in outs],
        out_shape=outs,
        compiler_params=pltpu.CompilerParams(vmem_limit_bytes=40 << 20),
        cost_estimate=pl.CostEstimate(flops=1 << 33, bytes_accessed=1 << 23, transcendentals=0),
    )(*operands, w, *extra)


def shaped(rows, columns, kind):
    return jax.ShapeDtypeStruct((rows, columns), kind)


def up_and_slope(at, ai, w):
    n = w.shape[2]
    kinds = [jnp.bfloat16, jnp.bfloat16, jnp.float32, jnp.float32]
    rows = [at.shape[0], ai.shape[0]] * 2
    outs = [shaped(r, n, k) for r, k in zip(rows, kinds)]
    return over_columns(partial(up_kernel, False), [at, ai], w, False, [], outs, n)


def scaled(at, ai, w, st, si):
    outs = [shaped(v.shape[0], w.shape[2], jnp.bfloat16) for v in (at, ai)]
    return over_columns(partial(scaled_kernel, False), [at, ai], w, False, [st, si], outs, w.shape[2])


def plain(at, ai, w):
    outs = [shaped(v.shape[0], w.shape[1], jnp.bfloat16) for v in (at, ai)]
    return over_columns(partial(plain_kernel, True), [at, ai], w, True, [], outs, w.shape[1])


def halves(at, ai, w, flip):
    columns = w.shape[1] if flip else w.shape[-1]
    rows = (at.shape[-2] + ai.shape[-2]) // 2
    outs = [shaped(rows, columns, jnp.bfloat16), shaped(rows, columns, jnp.float32)]
    return over_columns(partial(halves_kernel, flip), [at, ai], w, flip, [], outs, columns)


def project_qkv(at, ai, w):
    inner = w.shape[2]
    whole = lambda v: pl.BlockSpec(v.shape, lambda n: (0, 0))
    outs = [jax.ShapeDtypeStruct((3, v.shape[0], inner), jnp.bfloat16) for v in (at, ai)]
    return pl.pallas_call(
        qkv_kernel,
        grid=(3,),
        in_specs=[whole(at), whole(ai), pl.BlockSpec((2, 1) + w.shape[2:], lambda n: (0, n, 0, 0))],
        out_specs=[pl.BlockSpec((1,) + v.shape[1:], lambda n: (n, 0, 0)) for v in outs],
        out_shape=outs,
        compiler_params=pltpu.CompilerParams(vmem_limit_bytes=40 << 20),
        cost_estimate=pl.CostEstimate(flops=1 << 33, bytes_accessed=1 << 23, transcendentals=0),
    )(at, ai, w)


def outer_kernel(n, *refs):
    left, right, out = refs[: 2 * n], refs[2 * n : 4 * n], refs[-1]
    for s in range(2):
        total = None
        for j in range(n):
            a = left[s * n + j]
            a = a[0] if len(a.shape) == 3 else a[...]
            term = tn(a, right[s * n + j][...])
            total = term if total is None else total + term
        if len(out.shape) == 3:
            out[s] = total.astype(jnp.bfloat16)
            continue
        ranks = out.shape[1]
        part = HEAD // ranks
        for p in range(ranks):
            rows = [total[h + p * part : h + (p + 1) * part] for h in range(0, total.shape[0], HEAD)]
            out[s, p] = jnp.concatenate(rows, 0).astype(jnp.bfloat16)


def outer(left_t, left_i, right_t, right_i, ranks=None, into=None, kinds=1, first=0):
    n = len(left_t)
    left, right = left_t + left_i, right_t + right_i
    columns = right[0].shape[1]
    if left[0].ndim == 3:
        step, steps = left[0].shape[2], left[0].shape[0]
        l_spec = lambda v: pl.BlockSpec((1,) + v.shape[1:], lambda m: (m, 0, 0))
    else:
        width = left[0].shape[1]
        step = 512 if width % 512 == 0 else width if width < 512 else 256
        steps = width // step
        l_spec = lambda v: pl.BlockSpec((v.shape[0], step), lambda m: (0, m))
    if ranks is None:
        shape, block, place = (2, steps * step, columns), (2, step, columns), lambda m: (0, m, 0)
    else:
        part = step // ranks
        shape, block = (2, ranks, kinds * part, columns), (2, ranks, part, columns)
        place = lambda m: (0, 0, first + m, 0)
    held = [] if into is None else [into]
    return pl.pallas_call(
        partial(outer_kernel, n),
        grid=(steps,),
        in_specs=[l_spec(v) for v in left]
        + [pl.BlockSpec(v.shape, lambda m: (0, 0)) for v in right]
        + [pl.BlockSpec(memory_space=pl.ANY)] * len(held),
        out_specs=pl.BlockSpec(block, place),
        out_shape=jax.ShapeDtypeStruct(shape, jnp.bfloat16),
        input_output_aliases={4 * n: 0} if held else {},
        compiler_params=pltpu.CompilerParams(vmem_limit_bytes=52 << 20),
        cost_estimate=pl.CostEstimate(flops=1 << 34, bytes_accessed=1 << 24, transcendentals=0),
    )(*left, *right, *held)


class Group:
    def __init__(self, size):
        self.size = size
        self.evens = [2 * k for k in range(size // 2)]
        self.odds = [2 * k + 1 for k in range(size // 2)]
        self.order = self.evens + self.odds

    def send(self, value, flip):
        return lax.ppermute(value, "tensor", [(t, t ^ flip) for t in range(self.size)])

    def gather(self, own):
        evens = [own] + [self.send(own, flip) for flip in self.evens[1:]]
        return evens + [self.send(value, 1) for value in evens]


MESH = pl.DeviceIdType.MESH


def flip_bits(index, flip, size):
    total, bit = 0, 1
    while bit < size:
        digit = lax.rem(lax.div(index, bit), 2)
        total = total + bit * ((1 - digit) if flip & bit else digit)
        bit *= 2
    return total


class Data:
    def __init__(self, size):
        self.size = size
        self.nx = math.isqrt(size // 2)
        self.nz = size // self.nx


def pass_kernel(*refs):
    pass


def gate(values, others):
    others = jax.tree.leaves(list(others))
    n = len(values)
    anywhere = pl.BlockSpec(memory_space=pl.ANY)
    return pl.pallas_call(
        pass_kernel,
        in_specs=[anywhere] * (n + len(others)),
        out_specs=[anywhere] * n,
        out_shape=[jax.ShapeDtypeStruct(v.shape, v.dtype) for v in values],
        input_output_aliases={i: i for i in range(n)},
        compiler_params=pltpu.CompilerParams(vmem_limit_bytes=1 << 20),
        cost_estimate=pl.CostEstimate(flops=1 << 10, bytes_accessed=1 << 10, transcendentals=0),
    )(*values, *others)


def after(value, *others):
    return gate([value], others)[0]


def greet(n_dp, size):
    me_d, me_t = lax.axis_index("dp"), lax.axis_index("tensor")
    barrier = pltpu.get_barrier_semaphore()
    for k in range(1, n_dp):
        pl.semaphore_signal(barrier, inc=1, device_id=(flip_bits(me_d, k, n_dp), me_t), device_id_type=MESH)
    for k in range(1, size):
        pl.semaphore_signal(barrier, inc=1, device_id=(me_d, flip_bits(me_t, k, size)), device_id_type=MESH)
    pl.semaphore_wait(barrier, n_dp + size - 2)


def to_data(n_dp, source, target, send, recv):
    me_d, me_t = lax.axis_index("dp"), lax.axis_index("tensor")
    copies = []
    for k in range(1, n_dp):
        peer = flip_bits(me_d, k, n_dp)
        copy = pltpu.make_async_remote_copy(
            src_ref=source(peer),
            dst_ref=target.at[me_d],
            send_sem=send.at[k - 1],
            recv_sem=recv.at[k - 1],
            device_id=(peer, me_t),
            device_id_type=MESH,
        )
        copy.start()
        copies.append(copy)
    return copies


def to_tensor(size, source, target, send, recv):
    me_d, me_t = lax.axis_index("dp"), lax.axis_index("tensor")
    copies = []
    for k in range(1, size):
        peer = flip_bits(me_t, k, size)
        copy = pltpu.make_async_remote_copy(
            src_ref=source(peer),
            dst_ref=target.at[me_t],
            send_sem=send.at[k - 1],
            recv_sem=recv.at[k - 1],
            device_id=(me_d, peer),
            device_id_type=MESH,
        )
        copy.start()
        copies.append(copy)
    return copies


def finish(copies):
    for copy in copies:
        copy.wait()


def mod_kernel(n_dp, size, cond, w, mod_out, act_out, conds, parts, got, own, sd1, rd1, sd2, rd2, st, rt):
    me_d, me_t = lax.axis_index("dp"), lax.axis_index("tensor")
    rows, part, columns = conds.shape[1], w.shape[1], w.shape[2] // 2
    greet(n_dp, size)
    copies = to_data(n_dp, lambda peer: cond.at[peer], conds, sd1, rd1)
    conds[me_d] = cond[me_d]
    finish(copies)
    value = conds[...].reshape(n_dp * rows, conds.shape[2])[:, :part]
    act = (value * jax.nn.sigmoid(value)).astype(jnp.bfloat16)
    act_out[...] = act
    place = lax.rem(lax.broadcasted_iota(jnp.int32, (n_dp * rows, 1), 0), rows)
    first = lax.rem(place, rows // 2) < rows // 4
    mixed = [
        jnp.where(first, nn(act, w[0, :, cut]), nn(act, w[1, :, cut]))
        for cut in (slice(0, columns), slice(columns, 2 * columns))
    ]
    mixed = jnp.where(place < rows // 2, mixed[0], mixed[1])
    parts[...] = mixed.reshape(n_dp, rows, columns)
    copies = to_data(n_dp, lambda peer: parts.at[peer], got, sd2, rd2)
    got[me_d] = parts[me_d]
    finish(copies)
    total = got[0]
    for p in range(1, n_dp):
        total = total + got[p]
    own[...] = total
    copies = to_tensor(size, lambda peer: own, mod_out, st, rt)
    mod_out[me_t] = total
    finish(copies)


def mod_forward(n_dp, size, cond, w_mod):
    slots, width = cond.shape
    part, columns = w_mod.shape[1:]
    rows, lanes = 4 * slots, -(-part // 128) * 128
    laid = cond.astype(jnp.float32).reshape(slots, n_dp, part).transpose(1, 0, 2)
    laid = jnp.concatenate([laid, laid, laid, laid], 1)
    laid = jnp.pad(laid, ((0, 0), (0, 0), (0, lanes - part)))
    dma = pltpu.SemaphoreType.DMA
    return pl.pallas_call(
        partial(mod_kernel, n_dp, size),
        in_specs=[pl.BlockSpec(memory_space=pltpu.VMEM)] * 2,
        out_specs=[pl.BlockSpec(memory_space=pltpu.VMEM)] * 2,
        out_shape=[
            jax.ShapeDtypeStruct((size, rows, columns // 2), jnp.float32),
            jax.ShapeDtypeStruct((n_dp * rows, part), jnp.bfloat16),
        ],
        scratch_shapes=[
            pltpu.VMEM((n_dp, rows, lanes), jnp.float32),
            pltpu.VMEM((n_dp, rows, columns // 2), jnp.float32),
            pltpu.VMEM((n_dp, rows, columns // 2), jnp.float32),
            pltpu.VMEM((rows, columns // 2), jnp.float32),
            dma((n_dp - 1,)), dma((n_dp - 1,)), dma((n_dp - 1,)), dma((n_dp - 1,)),
            dma((size - 1,)), dma((size - 1,)),
        ],
        compiler_params=pltpu.CompilerParams(
            collective_id=0, has_side_effects=True, vmem_limit_bytes=40 << 20
        ),
        cost_estimate=pl.CostEstimate(flops=1 << 33, bytes_accessed=1 << 21, transcendentals=0),
    )(laid, w_mod)


def mod_back_kernel(n_dp, size, terms, lost, act, w, grad, cond_out, loss_out, halves, sums, every, cparts, cgot, cfull,
                    lhalves, lsums, levery, st1, rt1, sd1, rd1, sd2, rd2, st2, rt2, st3, rt3, sd3, rd3):
    me_d, me_t = lax.axis_index("dp"), lax.axis_index("tensor")
    rows, columns = terms.shape[1:]
    part = w.shape[1]
    greet(n_dp, size)
    copies = to_tensor(size, lambda peer: terms.at[peer], halves, st1, rt1)
    copies += to_tensor(size, lambda peer: lost, lhalves, st3, rt3)
    halves[me_t] = terms[me_t]
    lhalves[me_t] = lost[...]
    finish(copies)
    total, loss = halves[0], lhalves[0]
    for t in range(1, size):
        total, loss = total + halves[t], loss + lhalves[t]
    sums[...] = total
    lsums[...] = loss
    copies = to_data(n_dp, lambda peer: sums, every, sd1, rd1)
    copies += to_data(n_dp, lambda peer: lsums, levery, sd3, rd3)
    every[me_d] = total
    levery[me_d] = loss
    finish(copies)
    loss = levery[0]
    for p in range(1, n_dp):
        loss = loss + levery[p]
    loss_out[...] = loss
    dmod = every[...].reshape(n_dp * rows, columns).astype(jnp.bfloat16)
    place = lax.rem(lax.broadcasted_iota(jnp.int32, (n_dp * rows, 1), 0), rows)
    quarter = rows // 4
    cuts = (slice(0, columns), slice(columns, 2 * columns))
    back = [nt(dmod, w[s, :, cut]) for cut in cuts for s in range(2)]
    mixed = back[0]
    for n in range(1, 4):
        mixed = jnp.where(place < n * quarter, mixed, back[n])
    cparts[:, :, :part] = mixed.reshape(n_dp, rows, part)
    copies = to_data(n_dp, lambda peer: cparts.at[peer], cgot, sd2, rd2)
    cgot[me_d] = cparts[me_d]
    for n in range(4):
        mask = (place >= n * quarter) & (place < (n + 1) * quarter)
        picked = jnp.where(mask, act[...], jnp.zeros((), jnp.bfloat16))
        grad[n % 2, :, cuts[n // 2]] = tn(picked, dmod)
    finish(copies)
    copies = to_tensor(size, lambda peer: cgot, cfull, st2, rt2)
    cfull[me_t] = cgot[...]
    finish(copies)
    full = cfull[0]
    for t in range(1, size):
        full = full + cfull[t]
    cond_out[...] = full


def mod_backward(n_dp, size, terms, lost, act, w_mod):
    rows, columns = terms.shape[1:]
    part = w_mod.shape[1]
    lanes = -(-part // 128) * 128
    dma = pltpu.SemaphoreType.DMA
    f32 = jnp.float32
    return pl.pallas_call(
        partial(mod_back_kernel, n_dp, size),
        in_specs=[pl.BlockSpec(memory_space=pltpu.VMEM)] * 4,
        out_specs=[pl.BlockSpec(memory_space=pltpu.VMEM)] * 3,
        out_shape=[
            jax.ShapeDtypeStruct(w_mod.shape, f32),
            jax.ShapeDtypeStruct((n_dp, rows, lanes), f32),
            jax.ShapeDtypeStruct((8, 128), f32),
        ],
        scratch_shapes=[
            pltpu.VMEM((size, rows, columns), f32),
            pltpu.VMEM((rows, columns), f32),
            pltpu.VMEM((n_dp, rows, columns), f32),
            pltpu.VMEM((n_dp, rows, lanes), f32),
            pltpu.VMEM((n_dp, rows, lanes), f32),
            pltpu.VMEM((size, n_dp, rows, lanes), f32),
            pltpu.VMEM((size, 8, 128), f32),
            pltpu.VMEM((8, 128), f32),
            pltpu.VMEM((n_dp, 8, 128), f32),
            dma((size - 1,)), dma((size - 1,)),
            dma((n_dp - 1,)), dma((n_dp - 1,)), dma((n_dp - 1,)), dma((n_dp - 1,)),
            dma((size - 1,)), dma((size - 1,)),
            dma((size - 1,)), dma((size - 1,)), dma((n_dp - 1,)), dma((n_dp - 1,)),
        ],
        compiler_params=pltpu.CompilerParams(
            collective_id=1, has_side_effects=True, vmem_limit_bytes=40 << 20
        ),
        cost_estimate=pl.CostEstimate(flops=1 << 33, bytes_accessed=1 << 21, transcendentals=0),
    )(terms, lost, act, w_mod)


def on_device(
    data,
    group,
    image,
    text,
    cond,
    teacher_image,
    teacher_text,
    grad_image,
    grad_text,
    live,
    w_mod,
    w_qkv,
    w_out,
    w_up,
    w_down,
):
    slots, width = cond.shape
    rows_i, rows_t = image.shape[1], text.shape[1]
    pad_t = -(-rows_t // 8) * 8
    size = group.size
    n_dp = data.size
    heads = w_qkv.shape[2]
    odd = heads % 2

    wide = jnp.concatenate([w_qkv, w_out[:, None]], 1)
    f_wide = lax.all_gather(wide, "dp", axis=3, tiled=True)
    f_up = lax.all_gather(w_up, "dp", axis=1, tiled=True)
    f_down = lax.all_gather(w_down, "dp", axis=1, tiled=True)
    if odd:
        f_wide = jnp.pad(f_wide, ((0, 0), (0, 0), (0, odd), (0, 0), (0, 0)))
    f_wide = f_wide.reshape(2, 4, -1, width)
    f_qkv, f_out = f_wide[:, :3], f_wide[:, 3]

    mod_all, act_all = mod_forward(n_dp, size, cond, w_mod)
    mods = jnp.stack(
        [
            jnp.stack(
                [
                    jnp.stack([mod_all[:, (h * 2 + s) * slots + j] for h in range(2)], 1).reshape(6, width)
                    for s in range(2)
                ]
            )
            for j in range(slots)
        ]
    )

    is_image = (lax.broadcasted_iota(jnp.int32, (rows_i + pad_t, 1), 0) < rows_i)
    is_real = (lax.broadcasted_iota(jnp.int32, (rows_i + pad_t, 1), 0) < rows_i + rows_t)

    def merged(img, txt, j):
        return jnp.concatenate([img[j], jnp.pad(txt[j], ((0, pad_t - rows_t), (0, 0)))], 0)

    def pick(j, span):
        return jnp.where(is_image, mods[j, 1, span][None], mods[j, 0, span][None])

    def token_sums(values):
        return jnp.stack([jnp.sum(values[rows_i:], 0), jnp.sum(values[:rows_i], 0)])

    def spread(blocks):
        return (
            jnp.concatenate([b[:rows_i] for b in blocks], 0),
            jnp.concatenate([b[rows_i:] for b in blocks], 0),
        )

    half_i = size // 2 * rows_i

    def scatter_begin(rows_txt, rows_img, w, flip):
        top, own = halves(rows_txt, rows_img, w, flip)
        got = group.send(top, 1)
        blocks = []
        for k in range(size // 2):
            cuts = (slice(k * rows_i, (k + 1) * rows_i), slice(half_i + k * pad_t, half_i + (k + 1) * pad_t))
            blocks.append(jnp.concatenate([own[cut] + got[cut].astype(jnp.float32) for cut in cuts], 0))
        blocks = [blocks[0]] + [block.astype(jnp.bfloat16) for block in blocks[1:]]
        return blocks, [group.send(blocks[k], 2 * k) for k in range(1, size // 2)]

    def scatter_end(started, *others):
        blocks, got = started
        total = blocks[0]
        for value in got:
            total = total + after(value, *others).astype(jnp.float32)
        return total

    def gather_begin(own):
        return [own], [group.send(own, flip) for flip in group.evens[1:]]

    def gather_end(started, *others):
        own, got = started
        evens = own + [after(value, *others) for value in got]
        odds = group.send(jnp.concatenate(evens, 0), 1)
        return spread(evens + [odds[k : k + rows_i + pad_t] for k in range(0, odds.shape[0], rows_i + pad_t)])

    count = 3.0 * (n_dp // 2) * size * (rows_i + rows_t)

    slot = [dict() for j in range(slots)]
    for j, v in enumerate(slot):
        v["x"] = merged(image, text, j).astype(jnp.float32)
        v["hat1"], v["rstd1"] = norm_forward(v["x"])
        h1 = (v["hat1"] * (1.0 + pick(j, 1)) + pick(j, 0)).astype(jnp.bfloat16)
        v["go"] = gather_begin(h1)
    for j, v in enumerate(slot):
        v["h1_i"], v["h1_t"] = gather_end(v["go"], slot[-1]["go"][0])
    for j, v in enumerate(slot):
        if j:
            v["h1_i"] = after(v["h1_i"], slot[j - 1]["att_i"])
        v["qkv_t"], v["qkv_i"] = project_qkv(v["h1_t"], v["h1_i"], f_qkv)
        v["att_i"], v["att_t"], v["lse"] = attend(v["qkv_i"], v["qkv_t"], pad_t, rows_t)
    for j, v in enumerate(slot):
        v["go"] = scatter_begin(v["att_t"], v["att_i"], f_out, False)
    for j, v in enumerate(slot):
        v["y"] = scatter_end(v["go"], slot[-1]["go"][0])
        v["mid"] = v["x"] + pick(j, 2) * v["y"]
        v["hat2"], v["rstd2"] = norm_forward(v["mid"])
        h2 = (v["hat2"] * (1.0 + pick(j, 4)) + pick(j, 3)).astype(jnp.bfloat16)
        v["go"] = gather_begin(h2)
    for j, v in enumerate(slot):
        v["h2_i"], v["h2_t"] = gather_end(v["go"], slot[-1]["go"][0])
    for j, v in enumerate(slot):
        if j:
            v["h2_i"] = after(v["h2_i"], slot[j - 1]["hid_i"])
        v["hid_t"], v["hid_i"], v["slope_t"], v["slope_i"] = up_and_slope(v["h2_t"], v["h2_i"], f_up)
    f_down = after(f_down, slot[-1]["hid_i"])
    for j, v in enumerate(slot):
        if j:
            v["hid_t"] = after(v["hid_t"], *slot[j - 1]["go"][0])
        v["go"] = scatter_begin(v["hid_t"], v["hid_i"], f_down, True)
    for j, v in enumerate(slot):
        v["m"] = scatter_end(v["go"], slot[j - 1]["go"][0])
        out = v["mid"] + pick(j, 5) * v["m"]
        mask = jnp.where(is_real, live[j].astype(jnp.float32), 0.0)
        err = mask * (out - merged(teacher_image, teacher_text, j).astype(jnp.float32))
        v["loss"] = jnp.sum(err * err)
        v["cot"] = mask * merged(grad_image, grad_text, j).astype(jnp.float32) + 2.0 * err
        v["dgate2"] = token_sums(v["cot"] * v["m"])
        dm = (v["cot"] * pick(j, 5)).astype(jnp.bfloat16)
        v["go"] = gather_begin(dm)
    for j, v in enumerate(slot):
        v["dm_i"], v["dm_t"] = gather_end(v["go"], slot[-1]["go"][0])

    here = lax.axis_index("dp")

    both = lambda a, b, *dealt: outer(*([v[name + e] for v in slot] for name in (a, b) for e in ("_t", "_i")), *dealt)

    def reduced(grads):
        return lax.psum_scatter(grads.reshape(2, -1, grads.shape[-1]), "dp", scatter_dimension=1, tiled=True)

    g_down = both("dm", "hid")
    done_down = reduced(g_down)
    for j, v in enumerate(slot):
        v["dm_i"] = after(v["dm_i"], g_down if j == 0 else slot[j - 1]["go"][0])
        v["dpre_t"], v["dpre_i"] = scaled(v["dm_t"], v["dm_i"], f_down, v["slope_t"], v["slope_i"])
        v["go"] = scatter_begin(v["dpre_t"], v["dpre_i"], f_up, True)
    g_up = both("h2", "dpre")
    done_up = reduced(g_up)
    for j, v in enumerate(slot):
        v["dh2"] = scatter_end(v["go"], g_up, slot[j - 1]["go"][0])
        v["dshift2"] = token_sums(v["dh2"])
        v["dscale2"] = token_sums(v["dh2"] * v["hat2"])
        v["dmid"] = v["cot"] + norm_backward(v["dh2"] * (1.0 + pick(j, 4)), v["hat2"], v["rstd2"])
        v["dgate1"] = token_sums(v["dmid"] * v["y"])
        dy = (v["dmid"] * pick(j, 2)).astype(jnp.bfloat16)
        v["go"] = gather_begin(dy)
    for j, v in enumerate(slot):
        v["dy_i"], v["dy_t"] = gather_end(v["go"], slot[-1]["go"][0])
    slot[-1]["dy_i"] = after(slot[-1]["dy_i"], done_down)
    g_out = both("att", "dy", n_dp, None, 4, 3)
    for j, v in enumerate(slot):
        v["dy_i"] = after(v["dy_i"], g_out) if j == 0 else after(v["dy_i"], slot[j - 1]["dqkv_i"])
        g_t, g_i = plain(v["dy_t"], v["dy_i"], f_out)
        v["dqkv_i"], v["dqkv_t"] = attend_back(v["qkv_i"], v["qkv_t"], g_i, g_t, v["lse"], pad_t, rows_t)
    g_wide = both("dqkv", "h1", n_dp, g_out, 4, 0)
    done_wide = reduced(g_wide)
    for j, v in enumerate(slot):
        v["dqkv_i"] = after(v["dqkv_i"], g_wide)
        v["go"] = scatter_begin(v["dqkv_t"], v["dqkv_i"], f_qkv, False)
    for j, v in enumerate(slot):
        v["dh1"] = scatter_end(v["go"], slot[-1]["go"][0])
    grad_i, grad_t, terms = [], [], []
    for j in range(slots):
        v = slot[j]
        dshift1 = token_sums(v["dh1"])
        dscale1 = token_sums(v["dh1"] * v["hat1"])
        back = v["dmid"] + norm_backward(v["dh1"] * (1.0 + pick(j, 1)), v["hat1"], v["rstd1"])
        grad_i.append(back[:rows_i])
        grad_t.append(back[rows_i : rows_i + rows_t])
        terms.append(
            jnp.stack([dshift1, dscale1, v["dgate1"], v["dshift2"], v["dscale2"], v["dgate2"]], 1)
        )
    lost = jnp.full((8, 128), sum(v["loss"] for v in slot))
    laid = jnp.stack(terms, 1).reshape(2 * slots, size, 2, -1).transpose(1, 2, 0, 3)
    laid = laid.reshape(size, 4 * slots, -1)
    laid = after(laid, done_up)
    done_mod, cond_rows, loss_rows = mod_backward(n_dp, size, laid, lost, act_all, w_mod)
    loss = loss_rows[0, 0] / (count * width)
    cond_rows = cond_rows[:, :, : w_mod.shape[1]]
    cond_total = jnp.sum(cond_rows.reshape(n_dp, 4, slots, -1), 1).transpose(1, 0, 2).reshape(slots, width)
    unused_value, silu_pull = jax.vjp(jax.nn.silu, cond.astype(jnp.float32))
    grad_cond = silu_pull(cond_total)[0]
    done_down = done_down.astype(jnp.float32)
    done_up = done_up.astype(jnp.float32)
    done_wide = done_wide.astype(jnp.float32).reshape(2, 4, heads + odd, -1, width)
    done_qkv, done_out = done_wide[:, :3], done_wide[:, 3]
    if odd:
        done_qkv, done_out = done_qkv[:, :, :heads], done_out[:, :heads]
    return (
        loss,
        done_mod,
        done_qkv,
        done_out,
        done_up,
        done_down,
        jnp.stack(grad_i),
        jnp.stack(grad_t),
        grad_cond,
    )


def solution(mesh):
    return jax.shard_map(
        partial(on_device, Data(mesh.shape["dp"]), Group(mesh.shape["tensor"])),
        mesh=mesh,
        in_specs=(
            P("dp", "tensor", None),
            P("dp", "tensor", None),
            P("dp", None),
            P("dp", "tensor", None),
            P("dp", "tensor", None),
            P("dp", "tensor", None),
            P("dp", "tensor", None),
            P("dp"),
            P(None, "dp", "tensor"),
            P(None, None, "tensor", "dp", None),
            P(None, "tensor", "dp", None),
            P(None, "dp", "tensor"),
            P(None, "dp", "tensor"),
        ),
        out_specs=(
            P(),
            P(None, "dp", "tensor"),
            P(None, None, "tensor", "dp", None),
            P(None, "tensor", "dp", None),
            P(None, "dp", "tensor"),
            P(None, "dp", "tensor"),
            P("dp", "tensor", None),
            P("dp", "tensor", None),
            P("dp", None),
        ),
        check_vma=False,
    )
```

```python
import math
from functools import partial

import jax
import jax.numpy as jnp
from jax import lax
from jax.experimental import pallas as pl
from jax.experimental.pallas import tpu as pltpu
from jax.sharding import PartitionSpec as P

norm_eps = 1e-06

LOG2E = math.log2(math.e)
HEAD = 64


def nt(a, b):
    return lax.dot_general(a, b, (((1,), (1,)), ((), ())), preferred_element_type=jnp.float32)


def nn(a, b):
    return jnp.dot(a, b, preferred_element_type=jnp.float32)


def query_blocks(rows_img, rows_txt):
    step = 256 if rows_img % 256 == 0 else rows_img
    return [(0, s, step) for s in range(0, rows_img, step)] + [(1, 0, rows_txt)]


def pad_bias(rows, block, valid):
    place = lax.broadcasted_iota(jnp.int32, (rows, 1), 0)
    return jnp.where(lax.rem(place, block) < valid, 0.0, -1e30).astype(jnp.float32)


def attend_kernel(block, valid, qi, ki, vi, qt, kt, vt, oi, ot, lse):
    factor = HEAD**-0.5
    low = lax.broadcasted_iota(jnp.int32, (1, 2 * HEAD), 1) < HEAD
    zero = jnp.zeros((), jnp.bfloat16)
    bias = pad_bias(qt.shape[0], block, valid)
    vit, vtt = vi[...].T, vt[...].T
    keys = []
    for h in range(2):
        mask = low if h == 0 else ~low
        keys.append((jnp.where(mask, ki[...], zero), jnp.where(mask, kt[...], zero)))
    at = 0
    for which, start, size in query_blocks(qi.shape[0], qt.shape[0]):
        src, dst = (qi, oi) if which == 0 else (qt, ot)
        q = src[start : start + size, :]
        parts = []
        for h in range(2):
            s_i = nt(keys[h][0], q)
            s_t = nt(keys[h][1], q) + bias
            top = jnp.maximum(
                jnp.max(s_i, 0, keepdims=True), jnp.max(s_t, 0, keepdims=True)
            )
            e_i = jnp.exp2((s_i - top) * (factor * LOG2E))
            e_t = jnp.exp2((s_t - top) * (factor * LOG2E))
            total = jnp.sum(e_i, 0, keepdims=True) + jnp.sum(e_t, 0, keepdims=True)
            inv = 1.0 / total
            p_i = (e_i * inv).astype(jnp.bfloat16)
            p_t = (e_t * inv).astype(jnp.bfloat16)
            rows = slice(h * HEAD, (h + 1) * HEAD)
            parts.append(nn(vit[rows], p_i) + nn(vtt[rows], p_t))
            lse[0, h : h + 1, at : at + size] = top * (factor * LOG2E) + jnp.log2(total)
        dst[start : start + size, :] = jnp.concatenate(parts, 0).T.astype(jnp.bfloat16)
        at += size


def back_kernel(block, valid, qi, ki, vi, qt, kt, vt, gi, gt, lse, d_i, d_t, aki, avi, akt, avt):
    dqi, dki, dvi = (d_i.at[k] for k in range(3))
    dqt, dkt, dvt = (d_t.at[k] for k in range(3))
    factor = HEAD**-0.5
    low = lax.broadcasted_iota(jnp.int32, (1, 2 * HEAD), 1) < HEAD
    zero = jnp.zeros((), jnp.bfloat16)
    bias = pad_bias(qt.shape[0], block, valid)
    kit, ktt = ki[...].T, kt[...].T
    masks = [low, ~low]
    at = 0
    first = True
    for which, start, size in query_blocks(qi.shape[0], qt.shape[0]):
        q_ref, g_ref, d_ref = (qi, gi, dqi) if which == 0 else (qt, gt, dqt)
        q, g = q_ref[start : start + size, :], g_ref[start : start + size, :]
        parts = []
        for h in range(2):
            q_h, g_h = jnp.where(masks[h], q, zero), jnp.where(masks[h], g, zero)
            stat = lse[0, h : h + 1, at : at + size]
            p_i = jnp.exp2(nt(ki[...], q_h) * (factor * LOG2E) - stat)
            p_t = jnp.exp2((nt(kt[...], q_h) + bias) * (factor * LOG2E) - stat)
            e_i, e_t = nt(vi[...], g_h), nt(vt[...], g_h)
            delta = jnp.sum(e_i * p_i, 0, keepdims=True) + jnp.sum(e_t * p_t, 0, keepdims=True)
            s_i = (p_i * (e_i - delta)).astype(jnp.bfloat16)
            s_t = (p_t * (e_t - delta)).astype(jnp.bfloat16)
            v_i = nn(p_i.astype(jnp.bfloat16), g_h)
            v_t = nn(p_t.astype(jnp.bfloat16), g_h)
            k_i = nn(s_i, q_h)
            k_t = nn(s_t, q_h)
            if first:
                avi[...], avt[...], aki[...], akt[...] = v_i, v_t, k_i, k_t
                first = False
            else:
                avi[...] += v_i
                avt[...] += v_t
                aki[...] += k_i
                akt[...] += k_t
            rows = slice(h * HEAD, (h + 1) * HEAD)
            parts.append(nn(kit[rows], s_i) + nn(ktt[rows], s_t))
        d_ref[start : start + size, :] = (jnp.concatenate(parts, 0).T * factor).astype(jnp.bfloat16)
        at += size
    dki[...] = (aki[...] * factor).astype(jnp.bfloat16)
    dkt[...] = (akt[...] * factor).astype(jnp.bfloat16)
    dvi[...] = avi[...].astype(jnp.bfloat16)
    dvt[...] = avt[...].astype(jnp.bfloat16)


def kind_specs(rows):
    return [pl.BlockSpec((None, rows, 2 * HEAD), partial(lambda k, p: (k, 0, p), k)) for k in range(3)]


def attend(qkv_img, qkv_txt, block, valid):
    n_i, n_t, inner = qkv_img.shape[1], qkv_txt.shape[1], qkv_img.shape[2]
    pairs = inner // (2 * HEAD)
    col = lambda rows: pl.BlockSpec((rows, 2 * HEAD), lambda p: (0, p))
    return pl.pallas_call(
        partial(attend_kernel, block, valid),
        grid=(pairs,),
        in_specs=kind_specs(n_i) + kind_specs(n_t),
        out_specs=[col(n_i), col(n_t), pl.BlockSpec((1, 2, n_i + n_t), lambda p: (p, 0, 0))],
        out_shape=[
            jax.ShapeDtypeStruct((n_i, inner), jnp.bfloat16),
            jax.ShapeDtypeStruct((n_t, inner), jnp.bfloat16),
            jax.ShapeDtypeStruct((pairs, 2, n_i + n_t), jnp.float32),
        ],
        compiler_params=pltpu.CompilerParams(vmem_limit_bytes=40 << 20),
        cost_estimate=pl.CostEstimate(flops=1 << 34, bytes_accessed=1 << 23, transcendentals=0),
    )(*([qkv_img] * 3 + [qkv_txt] * 3))


def attend_back(qkv_img, qkv_txt, g_img, g_txt, lse, block, valid):
    n_i, n_t, inner = qkv_img.shape[1], qkv_txt.shape[1], qkv_img.shape[2]
    pairs = inner // (2 * HEAD)
    col = lambda rows: pl.BlockSpec((rows, 2 * HEAD), lambda p: (0, p))
    return pl.pallas_call(
        partial(back_kernel, block, valid),
        grid=(pairs,),
        in_specs=kind_specs(n_i)
        + kind_specs(n_t)
        + [col(n_i), col(n_t), pl.BlockSpec((1, 2, n_i + n_t), lambda p: (p, 0, 0))],
        out_specs=[pl.BlockSpec((3, rows, 2 * HEAD), lambda p: (0, 0, p)) for rows in (n_i, n_t)],
        out_shape=[jax.ShapeDtypeStruct((3, rows, inner), jnp.bfloat16) for rows in (n_i, n_t)],
        scratch_shapes=[pltpu.VMEM((n, 2 * HEAD), jnp.float32) for n in (n_i, n_i, n_t, n_t)],
        compiler_params=pltpu.CompilerParams(vmem_limit_bytes=40 << 20),
        cost_estimate=pl.CostEstimate(flops=1 << 35, bytes_accessed=1 << 24, transcendentals=0),
    )(*([qkv_img] * 3 + [qkv_txt] * 3 + [g_img, g_txt, lse]))


def tn(a, b):
    return lax.dot_general(a, b, (((0,), (0,)), ((), ())), preferred_element_type=jnp.float32)


def norm_forward(values):
    center = jnp.mean(values, -1, keepdims=True)
    spread = jnp.mean(jnp.square(values - center), -1, keepdims=True)
    rstd = lax.rsqrt(spread + norm_eps)
    return ((values - center) * rstd, rstd)


def norm_backward(grads, hats, rstd):
    first = jnp.mean(grads, -1, keepdims=True)
    second = jnp.mean(grads * hats, -1, keepdims=True)
    return rstd * (grads - first - hats * second)


def tile(n):
    return 512 if n % 512 == 0 else 256 if n % 256 == 0 else n


def dot_kind(a, w, flip):
    return nt(a, w) if flip else nn(a, w)


def gelu_parts(x):
    c, a = math.sqrt(2.0 / math.pi), 0.044715
    square = x * x
    t = jnp.tanh(c * (x + a * (x * square)))
    slope = 0.5 * (1.0 + t) + 0.5 * x * (1.0 - t * t) * (c * (1.0 + 3.0 * a * square))
    return 0.5 * x * (1.0 + t), slope


def up_kernel(flip, at, ai, w, ht, hi, st, si):
    for s, (a, h, slope) in enumerate(((at, ht, st), (ai, hi, si))):
        value, d = gelu_parts(dot_kind(a[...], w[s], flip))
        h[...] = value.astype(jnp.bfloat16)
        slope[...] = d


def scaled_kernel(flip, at, ai, w, st, si, ot, oi):
    for s, (a, o, slope) in enumerate(((at, ot, st), (ai, oi, si))):
        o[...] = (dot_kind(a[...], w[s], flip) * slope[...]).astype(jnp.bfloat16)


def plain_kernel(flip, at, ai, w, ot, oi):
    for s, (a, o) in enumerate(((at, ot), (ai, oi))):
        o[...] = dot_kind(a[...], w[s], flip).astype(jnp.bfloat16)


def qkv_kernel(at, ai, w, ot, oi):
    for s, (a, o) in enumerate(((at, ot), (ai, oi))):
        o[0] = nt(a[...], w[s, 0]).astype(jnp.bfloat16)


def halves_kernel(flip, at, ai, w, top, own):
    for s, a in ((1, ai), (0, at)):
        half = a.shape[-2] // 2
        start = 0 if s == 1 else ai.shape[-2] // 2
        if len(a.shape) == 3:
            total = nn(a[0], w[s, 0])
            for k in range(1, a.shape[0]):
                total = total + nn(a[k], w[s, k])
        else:
            total = dot_kind(a[...], w[s], flip)
        own[start : start + half, :] = total[:half]
        top[start : start + half, :] = total[half:].astype(jnp.bfloat16)


def over_columns(kernel, operands, w, flip, extra, outs, columns):
    step = tile(columns)
    whole = lambda v: pl.BlockSpec(v.shape, lambda n: (0,) * v.ndim)
    if w.ndim == 4:
        w_spec = pl.BlockSpec(w.shape[:3] + (step,), lambda n: (0, 0, 0, n))
    elif flip:
        w_spec = pl.BlockSpec((2, step, w.shape[2]), lambda n: (0, n, 0))
    else:
        w_spec = pl.BlockSpec((2, w.shape[1], step), lambda n: (0, 0, n))
    by_tile = lambda v: pl.BlockSpec((v.shape[0], step), lambda n: (0, n))
    return pl.pallas_call(
        kernel,
        grid=(columns // step,),
        in_specs=[whole(v) for v in operands] + [w_spec] + [by_tile(v) for v in extra],
        out_specs=[by_tile(v) for v in outs],
        out_shape=outs,
        compiler_params=pltpu.CompilerParams(vmem_limit_bytes=40 << 20),
        cost_estimate=pl.CostEstimate(flops=1 << 33, bytes_accessed=1 << 23, transcendentals=0),
    )(*operands, w, *extra)


def shaped(rows, columns, kind):
    return jax.ShapeDtypeStruct((rows, columns), kind)


def up_and_slope(at, ai, w):
    n = w.shape[2]
    kinds = [jnp.bfloat16, jnp.bfloat16, jnp.float32, jnp.float32]
    rows = [at.shape[0], ai.shape[0]] * 2
    outs = [shaped(r, n, k) for r, k in zip(rows, kinds)]
    return over_columns(partial(up_kernel, False), [at, ai], w, False, [], outs, n)


def scaled(at, ai, w, st, si):
    outs = [shaped(v.shape[0], w.shape[2], jnp.bfloat16) for v in (at, ai)]
    return over_columns(partial(scaled_kernel, False), [at, ai], w, False, [st, si], outs, w.shape[2])


def plain(at, ai, w):
    outs = [shaped(v.shape[0], w.shape[1], jnp.bfloat16) for v in (at, ai)]
    return over_columns(partial(plain_kernel, True), [at, ai], w, True, [], outs, w.shape[1])


def halves(at, ai, w, flip):
    columns = w.shape[1] if flip else w.shape[-1]
    rows = (at.shape[-2] + ai.shape[-2]) // 2
    outs = [shaped(rows, columns, jnp.bfloat16), shaped(rows, columns, jnp.float32)]
    return over_columns(partial(halves_kernel, flip), [at, ai], w, flip, [], outs, columns)


def project_qkv(at, ai, w):
    inner = w.shape[2]
    whole = lambda v: pl.BlockSpec(v.shape, lambda n: (0, 0))
    outs = [jax.ShapeDtypeStruct((3, v.shape[0], inner), jnp.bfloat16) for v in (at, ai)]
    return pl.pallas_call(
        qkv_kernel,
        grid=(3,),
        in_specs=[whole(at), whole(ai), pl.BlockSpec((2, 1) + w.shape[2:], lambda n: (0, n, 0, 0))],
        out_specs=[pl.BlockSpec((1,) + v.shape[1:], lambda n: (n, 0, 0)) for v in outs],
        out_shape=outs,
        compiler_params=pltpu.CompilerParams(vmem_limit_bytes=40 << 20),
        cost_estimate=pl.CostEstimate(flops=1 << 33, bytes_accessed=1 << 23, transcendentals=0),
    )(at, ai, w)


def outer_kernel(n, *refs):
    left, right, out = refs[: 2 * n], refs[2 * n : 4 * n], refs[-1]
    for s in range(2):
        total = None
        for j in range(n):
            a = left[s * n + j]
            a = a[0] if len(a.shape) == 3 else a[...]
            term = tn(a, right[s * n + j][...])
            total = term if total is None else total + term
        if len(out.shape) == 3:
            out[s] = total.astype(jnp.bfloat16)
            continue
        ranks = out.shape[1]
        part = HEAD // ranks
        for p in range(ranks):
            rows = [total[h + p * part : h + (p + 1) * part] for h in range(0, total.shape[0], HEAD)]
            out[s, p] = jnp.concatenate(rows, 0).astype(jnp.bfloat16)


def outer(left_t, left_i, right_t, right_i, ranks=None, into=None, kinds=1, first=0):
    n = len(left_t)
    left, right = left_t + left_i, right_t + right_i
    columns = right[0].shape[1]
    if left[0].ndim == 3:
        step, steps = left[0].shape[2], left[0].shape[0]
        l_spec = lambda v: pl.BlockSpec((1,) + v.shape[1:], lambda m: (m, 0, 0))
    else:
        width = left[0].shape[1]
        step = 512 if width % 512 == 0 else width if width < 512 else 256
        steps = width // step
        l_spec = lambda v: pl.BlockSpec((v.shape[0], step), lambda m: (0, m))
    if ranks is None:
        shape, block, place = (2, steps * step, columns), (2, step, columns), lambda m: (0, m, 0)
    else:
        part = step // ranks
        shape, block = (2, ranks, kinds * part, columns), (2, ranks, part, columns)
        place = lambda m: (0, 0, first + m, 0)
    held = [] if into is None else [into]
    return pl.pallas_call(
        partial(outer_kernel, n),
        grid=(steps,),
        in_specs=[l_spec(v) for v in left]
        + [pl.BlockSpec(v.shape, lambda m: (0, 0)) for v in right]
        + [pl.BlockSpec(memory_space=pl.ANY)] * len(held),
        out_specs=pl.BlockSpec(block, place),
        out_shape=jax.ShapeDtypeStruct(shape, jnp.bfloat16),
        input_output_aliases={4 * n: 0} if held else {},
        compiler_params=pltpu.CompilerParams(vmem_limit_bytes=52 << 20),
        cost_estimate=pl.CostEstimate(flops=1 << 34, bytes_accessed=1 << 24, transcendentals=0),
    )(*left, *right, *held)


class Group:
    def __init__(self, size):
        self.size = size
        self.evens = [2 * k for k in range(size // 2)]
        self.odds = [2 * k + 1 for k in range(size // 2)]
        self.order = self.evens + self.odds

    def send(self, value, flip):
        return lax.ppermute(value, "tensor", [(t, t ^ flip) for t in range(self.size)])

    def gather(self, own):
        evens = [own] + [self.send(own, flip) for flip in self.evens[1:]]
        return evens + [self.send(value, 1) for value in evens]


MESH = pl.DeviceIdType.MESH


def flip_bits(index, flip, size):
    total, bit = 0, 1
    while bit < size:
        digit = lax.rem(lax.div(index, bit), 2)
        total = total + bit * ((1 - digit) if flip & bit else digit)
        bit *= 2
    return total


class Data:
    def __init__(self, size):
        self.size = size
        self.nx = math.isqrt(size // 2)
        self.nz = size // self.nx

    def send(self, value, flip):
        return lax.ppermute(value, "dp", [(p, p ^ flip) for p in range(self.size)])

    def across(self, partial_of):
        here = lax.axis_index("dp")
        rank = lambda zk, xk: flip_bits(here, zk * self.nx + xk, self.size)
        sent = lambda xk: jnp.stack([partial_of(rank(zk, xk)) for zk in range(self.nz)])
        own = [partial_of(rank(zk, 0)) for zk in range(self.nz)]
        return own, [self.send(sent(xk), xk) for xk in range(1, self.nx)]

    def along(self, own, got):
        totals = []
        for zk in range(self.nz):
            total = own[zk].astype(jnp.float32)
            for value in got:
                total = total + value[zk].astype(jnp.float32)
            totals.append(total)
        return totals[0], [self.send(totals[zk].astype(jnp.bfloat16), zk * self.nx) for zk in range(1, self.nz)]


def pass_kernel(*refs):
    pass


def gate(values, others):
    others = jax.tree.leaves(list(others))
    n = len(values)
    anywhere = pl.BlockSpec(memory_space=pl.ANY)
    return pl.pallas_call(
        pass_kernel,
        in_specs=[anywhere] * (n + len(others)),
        out_specs=[anywhere] * n,
        out_shape=[jax.ShapeDtypeStruct(v.shape, v.dtype) for v in values],
        input_output_aliases={i: i for i in range(n)},
        compiler_params=pltpu.CompilerParams(vmem_limit_bytes=1 << 20),
        cost_estimate=pl.CostEstimate(flops=1 << 10, bytes_accessed=1 << 10, transcendentals=0),
    )(*values, *others)


def after(value, *others):
    return gate([value], others)[0]


def greet(n_dp, size):
    me_d, me_t = lax.axis_index("dp"), lax.axis_index("tensor")
    barrier = pltpu.get_barrier_semaphore()
    for k in range(1, n_dp):
        pl.semaphore_signal(barrier, inc=1, device_id=(flip_bits(me_d, k, n_dp), me_t), device_id_type=MESH)
    for k in range(1, size):
        pl.semaphore_signal(barrier, inc=1, device_id=(me_d, flip_bits(me_t, k, size)), device_id_type=MESH)
    pl.semaphore_wait(barrier, n_dp + size - 2)


def to_data(n_dp, source, target, send, recv):
    me_d, me_t = lax.axis_index("dp"), lax.axis_index("tensor")
    copies = []
    for k in range(1, n_dp):
        peer = flip_bits(me_d, k, n_dp)
        copy = pltpu.make_async_remote_copy(
            src_ref=source(peer),
            dst_ref=target.at[me_d],
            send_sem=send.at[k - 1],
            recv_sem=recv.at[k - 1],
            device_id=(peer, me_t),
            device_id_type=MESH,
        )
        copy.start()
        copies.append(copy)
    return copies


def to_tensor(size, source, target, send, recv):
    me_d, me_t = lax.axis_index("dp"), lax.axis_index("tensor")
    copies = []
    for k in range(1, size):
        peer = flip_bits(me_t, k, size)
        copy = pltpu.make_async_remote_copy(
            src_ref=source(peer),
            dst_ref=target.at[me_t],
            send_sem=send.at[k - 1],
            recv_sem=recv.at[k - 1],
            device_id=(me_d, peer),
            device_id_type=MESH,
        )
        copy.start()
        copies.append(copy)
    return copies


def finish(copies):
    for copy in copies:
        copy.wait()


def mod_kernel(n_dp, size, cond, w, mod_out, act_out, conds, parts, got, own, sd1, rd1, sd2, rd2, st, rt):
    me_d, me_t = lax.axis_index("dp"), lax.axis_index("tensor")
    rows, part, columns = conds.shape[1], w.shape[1], w.shape[2] // 2
    greet(n_dp, size)
    copies = to_data(n_dp, lambda peer: cond.at[peer], conds, sd1, rd1)
    conds[me_d] = cond[me_d]
    finish(copies)
    value = conds[...].reshape(n_dp * rows, conds.shape[2])[:, :part]
    act = (value * jax.nn.sigmoid(value)).astype(jnp.bfloat16)
    act_out[...] = act
    place = lax.rem(lax.broadcasted_iota(jnp.int32, (n_dp * rows, 1), 0), rows)
    first = lax.rem(place, rows // 2) < rows // 4
    mixed = [
        jnp.where(first, nn(act, w[0, :, cut]), nn(act, w[1, :, cut]))
        for cut in (slice(0, columns), slice(columns, 2 * columns))
    ]
    mixed = jnp.where(place < rows // 2, mixed[0], mixed[1])
    parts[...] = mixed.reshape(n_dp, rows, columns)
    copies = to_data(n_dp, lambda peer: parts.at[peer], got, sd2, rd2)
    got[me_d] = parts[me_d]
    finish(copies)
    total = got[0]
    for p in range(1, n_dp):
        total = total + got[p]
    own[...] = total
    copies = to_tensor(size, lambda peer: own, mod_out, st, rt)
    mod_out[me_t] = total
    finish(copies)


def mod_forward(n_dp, size, cond, w_mod):
    slots, width = cond.shape
    part, columns = w_mod.shape[1:]
    rows, lanes = 4 * slots, -(-part // 128) * 128
    laid = cond.astype(jnp.float32).reshape(slots, n_dp, part).transpose(1, 0, 2)
    laid = jnp.concatenate([laid, laid, laid, laid], 1)
    laid = jnp.pad(laid, ((0, 0), (0, 0), (0, lanes - part)))
    dma = pltpu.SemaphoreType.DMA
    return pl.pallas_call(
        partial(mod_kernel, n_dp, size),
        in_specs=[pl.BlockSpec(memory_space=pltpu.VMEM)] * 2,
        out_specs=[pl.BlockSpec(memory_space=pltpu.VMEM)] * 2,
        out_shape=[
            jax.ShapeDtypeStruct((size, rows, columns // 2), jnp.float32),
            jax.ShapeDtypeStruct((n_dp * rows, part), jnp.bfloat16),
        ],
        scratch_shapes=[
            pltpu.VMEM((n_dp, rows, lanes), jnp.float32),
            pltpu.VMEM((n_dp, rows, columns // 2), jnp.float32),
            pltpu.VMEM((n_dp, rows, columns // 2), jnp.float32),
            pltpu.VMEM((rows, columns // 2), jnp.float32),
            dma((n_dp - 1,)), dma((n_dp - 1,)), dma((n_dp - 1,)), dma((n_dp - 1,)),
            dma((size - 1,)), dma((size - 1,)),
        ],
        compiler_params=pltpu.CompilerParams(
            collective_id=0, has_side_effects=True, vmem_limit_bytes=40 << 20
        ),
        cost_estimate=pl.CostEstimate(flops=1 << 33, bytes_accessed=1 << 21, transcendentals=0),
    )(laid, w_mod)


def mod_back_kernel(n_dp, size, terms, lost, act, w, grad, cond_out, loss_out, halves, sums, every, cparts, cgot, cfull,
                    lhalves, lsums, levery, st1, rt1, sd1, rd1, sd2, rd2, st2, rt2, st3, rt3, sd3, rd3):
    me_d, me_t = lax.axis_index("dp"), lax.axis_index("tensor")
    rows, columns = terms.shape[1:]
    part = w.shape[1]
    greet(n_dp, size)
    copies = to_tensor(size, lambda peer: terms.at[peer], halves, st1, rt1)
    copies += to_tensor(size, lambda peer: lost, lhalves, st3, rt3)
    halves[me_t] = terms[me_t]
    lhalves[me_t] = lost[...]
    finish(copies)
    total, loss = halves[0], lhalves[0]
    for t in range(1, size):
        total, loss = total + halves[t], loss + lhalves[t]
    sums[...] = total
    lsums[...] = loss
    copies = to_data(n_dp, lambda peer: sums, every, sd1, rd1)
    copies += to_data(n_dp, lambda peer: lsums, levery, sd3, rd3)
    every[me_d] = total
    levery[me_d] = loss
    finish(copies)
    loss = levery[0]
    for p in range(1, n_dp):
        loss = loss + levery[p]
    loss_out[...] = loss
    dmod = every[...].reshape(n_dp * rows, columns).astype(jnp.bfloat16)
    place = lax.rem(lax.broadcasted_iota(jnp.int32, (n_dp * rows, 1), 0), rows)
    quarter = rows // 4
    cuts = (slice(0, columns), slice(columns, 2 * columns))
    back = [nt(dmod, w[s, :, cut]) for cut in cuts for s in range(2)]
    mixed = back[0]
    for n in range(1, 4):
        mixed = jnp.where(place < n * quarter, mixed, back[n])
    cparts[:, :, :part] = mixed.reshape(n_dp, rows, part)
    copies = to_data(n_dp, lambda peer: cparts.at[peer], cgot, sd2, rd2)
    cgot[me_d] = cparts[me_d]
    for n in range(4):
        mask = (place >= n * quarter) & (place < (n + 1) * quarter)
        picked = jnp.where(mask, act[...], jnp.zeros((), jnp.bfloat16))
        grad[n % 2, :, cuts[n // 2]] = tn(picked, dmod)
    finish(copies)
    copies = to_tensor(size, lambda peer: cgot, cfull, st2, rt2)
    cfull[me_t] = cgot[...]
    finish(copies)
    full = cfull[0]
    for t in range(1, size):
        full = full + cfull[t]
    cond_out[...] = full


def mod_backward(n_dp, size, terms, lost, act, w_mod):
    rows, columns = terms.shape[1:]
    part = w_mod.shape[1]
    lanes = -(-part // 128) * 128
    dma = pltpu.SemaphoreType.DMA
    f32 = jnp.float32
    return pl.pallas_call(
        partial(mod_back_kernel, n_dp, size),
        in_specs=[pl.BlockSpec(memory_space=pltpu.VMEM)] * 4,
        out_specs=[pl.BlockSpec(memory_space=pltpu.VMEM)] * 3,
        out_shape=[
            jax.ShapeDtypeStruct(w_mod.shape, f32),
            jax.ShapeDtypeStruct((n_dp, rows, lanes), f32),
            jax.ShapeDtypeStruct((8, 128), f32),
        ],
        scratch_shapes=[
            pltpu.VMEM((size, rows, columns), f32),
            pltpu.VMEM((rows, columns), f32),
            pltpu.VMEM((n_dp, rows, columns), f32),
            pltpu.VMEM((n_dp, rows, lanes), f32),
            pltpu.VMEM((n_dp, rows, lanes), f32),
            pltpu.VMEM((size, n_dp, rows, lanes), f32),
            pltpu.VMEM((size, 8, 128), f32),
            pltpu.VMEM((8, 128), f32),
            pltpu.VMEM((n_dp, 8, 128), f32),
            dma((size - 1,)), dma((size - 1,)),
            dma((n_dp - 1,)), dma((n_dp - 1,)), dma((n_dp - 1,)), dma((n_dp - 1,)),
            dma((size - 1,)), dma((size - 1,)),
            dma((size - 1,)), dma((size - 1,)), dma((n_dp - 1,)), dma((n_dp - 1,)),
        ],
        compiler_params=pltpu.CompilerParams(
            collective_id=1, has_side_effects=True, vmem_limit_bytes=40 << 20
        ),
        cost_estimate=pl.CostEstimate(flops=1 << 33, bytes_accessed=1 << 21, transcendentals=0),
    )(terms, lost, act, w_mod)


def on_device(
    data,
    group,
    image,
    text,
    cond,
    teacher_image,
    teacher_text,
    grad_image,
    grad_text,
    live,
    w_mod,
    w_qkv,
    w_out,
    w_up,
    w_down,
):
    slots, width = cond.shape
    rows_i, rows_t = image.shape[1], text.shape[1]
    pad_t = -(-rows_t // 8) * 8
    size = group.size
    n_dp = data.size
    heads = w_qkv.shape[2]
    odd = heads % 2

    wide = jnp.concatenate([w_qkv, w_out[:, None]], 1)
    f_wide = lax.all_gather(wide, "dp", axis=3, tiled=True)
    f_up = lax.all_gather(w_up, "dp", axis=1, tiled=True)
    f_down = lax.all_gather(w_down, "dp", axis=1, tiled=True)
    if odd:
        f_wide = jnp.pad(f_wide, ((0, 0), (0, 0), (0, odd), (0, 0), (0, 0)))
    f_wide = f_wide.reshape(2, 4, -1, width)
    f_qkv, f_out = f_wide[:, :3], f_wide[:, 3]

    mod_all, act_all = mod_forward(n_dp, size, cond, w_mod)
    mods = jnp.stack(
        [
            jnp.stack(
                [
                    jnp.stack([mod_all[:, (h * 2 + s) * slots + j] for h in range(2)], 1).reshape(6, width)
                    for s in range(2)
                ]
            )
            for j in range(slots)
        ]
    )

    is_image = (lax.broadcasted_iota(jnp.int32, (rows_i + pad_t, 1), 0) < rows_i)
    is_real = (lax.broadcasted_iota(jnp.int32, (rows_i + pad_t, 1), 0) < rows_i + rows_t)

    def merged(img, txt, j):
        return jnp.concatenate([img[j], jnp.pad(txt[j], ((0, pad_t - rows_t), (0, 0)))], 0)

    def pick(j, span):
        return jnp.where(is_image, mods[j, 1, span][None], mods[j, 0, span][None])

    def token_sums(values):
        return jnp.stack([jnp.sum(values[rows_i:], 0), jnp.sum(values[:rows_i], 0)])

    def spread(blocks):
        return (
            jnp.concatenate([b[:rows_i] for b in blocks], 0),
            jnp.concatenate([b[rows_i:] for b in blocks], 0),
        )

    half_i = size // 2 * rows_i

    def scatter_begin(rows_txt, rows_img, w, flip):
        top, own = halves(rows_txt, rows_img, w, flip)
        got = group.send(top, 1)
        blocks = []
        for k in range(size // 2):
            cuts = (slice(k * rows_i, (k + 1) * rows_i), slice(half_i + k * pad_t, half_i + (k + 1) * pad_t))
            blocks.append(jnp.concatenate([own[cut] + got[cut].astype(jnp.float32) for cut in cuts], 0))
        blocks = [blocks[0]] + [block.astype(jnp.bfloat16) for block in blocks[1:]]
        return blocks, [group.send(blocks[k], 2 * k) for k in range(1, size // 2)]

    def scatter_end(started, *others):
        blocks, got = started
        total = blocks[0]
        for value in got:
            total = total + after(value, *others).astype(jnp.float32)
        return total

    def gather_begin(own):
        return [own], [group.send(own, flip) for flip in group.evens[1:]]

    def gather_end(started, *others):
        own, got = started
        evens = own + [after(value, *others) for value in got]
        odds = group.send(jnp.concatenate(evens, 0), 1)
        return spread(evens + [odds[k : k + rows_i + pad_t] for k in range(0, odds.shape[0], rows_i + pad_t)])

    count = 3.0 * (n_dp // 2) * size * (rows_i + rows_t)

    slot = [dict() for j in range(slots)]
    for j, v in enumerate(slot):
        v["x"] = merged(image, text, j).astype(jnp.float32)
        v["hat1"], v["rstd1"] = norm_forward(v["x"])
        h1 = (v["hat1"] * (1.0 + pick(j, 1)) + pick(j, 0)).astype(jnp.bfloat16)
        v["go"] = gather_begin(h1)
    for j, v in enumerate(slot):
        v["h1_i"], v["h1_t"] = gather_end(v["go"], slot[-1]["go"][0])
    for j, v in enumerate(slot):
        if j:
            v["h1_i"] = after(v["h1_i"], slot[j - 1]["att_i"])
        v["qkv_t"], v["qkv_i"] = project_qkv(v["h1_t"], v["h1_i"], f_qkv)
        v["att_i"], v["att_t"], v["lse"] = attend(v["qkv_i"], v["qkv_t"], pad_t, rows_t)
    for j, v in enumerate(slot):
        v["go"] = scatter_begin(v["att_t"], v["att_i"], f_out, False)
    for j, v in enumerate(slot):
        v["y"] = scatter_end(v["go"], slot[-1]["go"][0])
        v["mid"] = v["x"] + pick(j, 2) * v["y"]
        v["hat2"], v["rstd2"] = norm_forward(v["mid"])
        h2 = (v["hat2"] * (1.0 + pick(j, 4)) + pick(j, 3)).astype(jnp.bfloat16)
        v["go"] = gather_begin(h2)
    for j, v in enumerate(slot):
        v["h2_i"], v["h2_t"] = gather_end(v["go"], slot[-1]["go"][0])
    for j, v in enumerate(slot):
        if j:
            v["h2_i"] = after(v["h2_i"], slot[j - 1]["hid_i"])
        v["hid_t"], v["hid_i"], v["slope_t"], v["slope_i"] = up_and_slope(v["h2_t"], v["h2_i"], f_up)
    f_down = after(f_down, slot[-1]["hid_i"])
    for j, v in enumerate(slot):
        if j:
            v["hid_t"] = after(v["hid_t"], *slot[j - 1]["go"][0])
        v["go"] = scatter_begin(v["hid_t"], v["hid_i"], f_down, True)
    for j, v in enumerate(slot):
        v["m"] = scatter_end(v["go"], slot[j - 1]["go"][0])
        out = v["mid"] + pick(j, 5) * v["m"]
        mask = jnp.where(is_real, live[j].astype(jnp.float32), 0.0)
        err = mask * (out - merged(teacher_image, teacher_text, j).astype(jnp.float32))
        v["loss"] = jnp.sum(err * err)
        v["cot"] = mask * merged(grad_image, grad_text, j).astype(jnp.float32) + 2.0 * err
        v["dgate2"] = token_sums(v["cot"] * v["m"])
        dm = (v["cot"] * pick(j, 5)).astype(jnp.bfloat16)
        v["go"] = gather_begin(dm)
    for j, v in enumerate(slot):
        v["dm_i"], v["dm_t"] = gather_end(v["go"], slot[-1]["go"][0])

    here = lax.axis_index("dp")

    both = lambda a, b, *dealt: outer(*([v[name + e] for v in slot] for name in (a, b) for e in ("_t", "_i")), *dealt)

    def reduced(grads):
        return lax.psum_scatter(grads.reshape(2, -1, grads.shape[-1]), "dp", scatter_dimension=1, tiled=True)

    g_down = both("dm", "hid")
    done_down = reduced(g_down)
    for j, v in enumerate(slot):
        v["dm_i"] = after(v["dm_i"], g_down if j == 0 else slot[j - 1]["go"][0])
        v["dpre_t"], v["dpre_i"] = scaled(v["dm_t"], v["dm_i"], f_down, v["slope_t"], v["slope_i"])
        v["go"] = scatter_begin(v["dpre_t"], v["dpre_i"], f_up, True)
    g_up = both("h2", "dpre")
    done_up = reduced(g_up)
    for j, v in enumerate(slot):
        v["dh2"] = scatter_end(v["go"], g_up, slot[j - 1]["go"][0])
        v["dshift2"] = token_sums(v["dh2"])
        v["dscale2"] = token_sums(v["dh2"] * v["hat2"])
        v["dmid"] = v["cot"] + norm_backward(v["dh2"] * (1.0 + pick(j, 4)), v["hat2"], v["rstd2"])
        v["dgate1"] = token_sums(v["dmid"] * v["y"])
        dy = (v["dmid"] * pick(j, 2)).astype(jnp.bfloat16)
        v["go"] = gather_begin(dy)
    for j, v in enumerate(slot):
        v["dy_i"], v["dy_t"] = gather_end(v["go"], slot[-1]["go"][0])
    slot[-1]["dy_i"] = after(slot[-1]["dy_i"], done_down)
    g_out = both("att", "dy", n_dp)
    out_own, out_got = data.across(lambda rank: lax.dynamic_index_in_dim(g_out, rank, 1, keepdims=False))
    for j, v in enumerate(slot):
        v["dy_i"] = after(v["dy_i"], g_out) if j == 0 else after(v["dy_i"], slot[j - 1]["dqkv_i"])
        g_t, g_i = plain(v["dy_t"], v["dy_i"], f_out)
        v["dqkv_i"], v["dqkv_t"] = attend_back(v["qkv_i"], v["qkv_t"], g_i, g_t, v["lse"], pad_t, rows_t)
        if j == 0:
            out_got = [after(value, v["dqkv_i"]) for value in out_got]
    g_wide = both("dqkv", "h1", n_dp, None, 3, 0)
    done_qkv = reduced(g_wide)
    out_total, out_got = data.along(out_own, out_got)
    for j, v in enumerate(slot):
        v["dqkv_i"] = after(v["dqkv_i"], g_wide)
        v["go"] = scatter_begin(v["dqkv_t"], v["dqkv_i"], f_qkv, False)
    for j, v in enumerate(slot):
        v["dh1"] = scatter_end(v["go"], slot[-1]["go"][0])
    grad_i, grad_t, terms = [], [], []
    for j in range(slots):
        v = slot[j]
        dshift1 = token_sums(v["dh1"])
        dscale1 = token_sums(v["dh1"] * v["hat1"])
        back = v["dmid"] + norm_backward(v["dh1"] * (1.0 + pick(j, 1)), v["hat1"], v["rstd1"])
        grad_i.append(back[:rows_i])
        grad_t.append(back[rows_i : rows_i + rows_t])
        terms.append(
            jnp.stack([dshift1, dscale1, v["dgate1"], v["dshift2"], v["dscale2"], v["dgate2"]], 1)
        )
    lost = jnp.full((8, 128), sum(v["loss"] for v in slot))
    laid = jnp.stack(terms, 1).reshape(2 * slots, size, 2, -1).transpose(1, 2, 0, 3)
    laid = laid.reshape(size, 4 * slots, -1)
    laid = after(laid, done_up)
    done_mod, cond_rows, loss_rows = mod_backward(n_dp, size, laid, lost, act_all, w_mod)
    loss = loss_rows[0, 0] / (count * width)
    cond_rows = cond_rows[:, :, : w_mod.shape[1]]
    cond_total = jnp.sum(cond_rows.reshape(n_dp, 4, slots, -1), 1).transpose(1, 0, 2).reshape(slots, width)
    unused_value, silu_pull = jax.vjp(jax.nn.silu, cond.astype(jnp.float32))
    grad_cond = silu_pull(cond_total)[0]
    done_down = done_down.astype(jnp.float32)
    done_up = done_up.astype(jnp.float32)
    done_qkv = done_qkv.astype(jnp.float32).reshape(2, 3, heads + odd, -1, width)
    done_out = out_total + sum(after(value, slot[-1]["go"][0]).astype(jnp.float32) for value in out_got)
    done_out = done_out.reshape(2, heads + odd, -1, width)
    if odd:
        done_qkv, done_out = done_qkv[:, :, :heads], done_out[:, :heads]
    return (
        loss,
        done_mod,
        done_qkv,
        done_out,
        done_up,
        done_down,
        jnp.stack(grad_i),
        jnp.stack(grad_t),
        grad_cond,
    )


def solution(mesh):
    return jax.shard_map(
        partial(on_device, Data(mesh.shape["dp"]), Group(mesh.shape["tensor"])),
        mesh=mesh,
        in_specs=(
            P("dp", "tensor", None),
            P("dp", "tensor", None),
            P("dp", None),
            P("dp", "tensor", None),
            P("dp", "tensor", None),
            P("dp", "tensor", None),
            P("dp", "tensor", None),
            P("dp"),
            P(None, "dp", "tensor"),
            P(None, None, "tensor", "dp", None),
            P(None, "tensor", "dp", None),
            P(None, "dp", "tensor"),
            P(None, "dp", "tensor"),
        ),
        out_specs=(
            P(),
            P(None, "dp", "tensor"),
            P(None, None, "tensor", "dp", None),
            P(None, "tensor", "dp", None),
            P(None, "dp", "tensor"),
            P(None, "dp", "tensor"),
            P("dp", "tensor", None),
            P("dp", "tensor", None),
            P("dp", None),
        ),
        check_vma=False,
    )
```

```python
import math
from functools import partial

import jax
import jax.numpy as jnp
from jax import lax
from jax.experimental import pallas as pl
from jax.experimental.pallas import tpu as pltpu
from jax.sharding import PartitionSpec as P

norm_eps = 1e-06

LOG2E = math.log2(math.e)
HEAD = 64


def nt(a, b):
    return lax.dot_general(a, b, (((1,), (1,)), ((), ())), preferred_element_type=jnp.float32)


def nn(a, b):
    return jnp.dot(a, b, preferred_element_type=jnp.float32)


def query_blocks(rows_img, rows_txt):
    step = 256 if rows_img % 256 == 0 else rows_img
    return [(0, s, step) for s in range(0, rows_img, step)] + [(1, 0, rows_txt)]


def pad_bias(rows, block, valid):
    place = lax.broadcasted_iota(jnp.int32, (rows, 1), 0)
    return jnp.where(lax.rem(place, block) < valid, 0.0, -1e30).astype(jnp.float32)


def attend_kernel(block, valid, qi, ki, vi, qt, kt, vt, oi, ot, lse):
    factor = HEAD**-0.5
    low = lax.broadcasted_iota(jnp.int32, (1, 2 * HEAD), 1) < HEAD
    zero = jnp.zeros((), jnp.bfloat16)
    bias = pad_bias(qt.shape[0], block, valid)
    vit, vtt = vi[...].T, vt[...].T
    keys = []
    for h in range(2):
        mask = low if h == 0 else ~low
        keys.append((jnp.where(mask, ki[...], zero), jnp.where(mask, kt[...], zero)))
    at = 0
    for which, start, size in query_blocks(qi.shape[0], qt.shape[0]):
        src, dst = (qi, oi) if which == 0 else (qt, ot)
        q = src[start : start + size, :]
        parts = []
        for h in range(2):
            s_i = nt(keys[h][0], q)
            s_t = nt(keys[h][1], q) + bias
            top = jnp.maximum(
                jnp.max(s_i, 0, keepdims=True), jnp.max(s_t, 0, keepdims=True)
            )
            e_i = jnp.exp2((s_i - top) * (factor * LOG2E))
            e_t = jnp.exp2((s_t - top) * (factor * LOG2E))
            total = jnp.sum(e_i, 0, keepdims=True) + jnp.sum(e_t, 0, keepdims=True)
            inv = 1.0 / total
            p_i = (e_i * inv).astype(jnp.bfloat16)
            p_t = (e_t * inv).astype(jnp.bfloat16)
            rows = slice(h * HEAD, (h + 1) * HEAD)
            parts.append(nn(vit[rows], p_i) + nn(vtt[rows], p_t))
            lse[0, h : h + 1, at : at + size] = top * (factor * LOG2E) + jnp.log2(total)
        dst[start : start + size, :] = jnp.concatenate(parts, 0).T.astype(jnp.bfloat16)
        at += size


def back_kernel(block, valid, qi, ki, vi, qt, kt, vt, gi, gt, lse, d_i, d_t, aki, avi, akt, avt):
    dqi, dki, dvi = (d_i.at[k] for k in range(3))
    dqt, dkt, dvt = (d_t.at[k] for k in range(3))
    factor = HEAD**-0.5
    low = lax.broadcasted_iota(jnp.int32, (1, 2 * HEAD), 1) < HEAD
    zero = jnp.zeros((), jnp.bfloat16)
    bias = pad_bias(qt.shape[0], block, valid)
    kit, ktt = ki[...].T, kt[...].T
    masks = [low, ~low]
    at = 0
    first = True
    for which, start, size in query_blocks(qi.shape[0], qt.shape[0]):
        q_ref, g_ref, d_ref = (qi, gi, dqi) if which == 0 else (qt, gt, dqt)
        q, g = q_ref[start : start + size, :], g_ref[start : start + size, :]
        parts = []
        for h in range(2):
            q_h, g_h = jnp.where(masks[h], q, zero), jnp.where(masks[h], g, zero)
            stat = lse[0, h : h + 1, at : at + size]
            p_i = jnp.exp2(nt(ki[...], q_h) * (factor * LOG2E) - stat)
            p_t = jnp.exp2((nt(kt[...], q_h) + bias) * (factor * LOG2E) - stat)
            e_i, e_t = nt(vi[...], g_h), nt(vt[...], g_h)
            delta = jnp.sum(e_i * p_i, 0, keepdims=True) + jnp.sum(e_t * p_t, 0, keepdims=True)
            s_i = (p_i * (e_i - delta)).astype(jnp.bfloat16)
            s_t = (p_t * (e_t - delta)).astype(jnp.bfloat16)
            v_i = nn(p_i.astype(jnp.bfloat16), g_h)
            v_t = nn(p_t.astype(jnp.bfloat16), g_h)
            k_i = nn(s_i, q_h)
            k_t = nn(s_t, q_h)
            if first:
                avi[...], avt[...], aki[...], akt[...] = v_i, v_t, k_i, k_t
                first = False
            else:
                avi[...] += v_i
                avt[...] += v_t
                aki[...] += k_i
                akt[...] += k_t
            rows = slice(h * HEAD, (h + 1) * HEAD)
            parts.append(nn(kit[rows], s_i) + nn(ktt[rows], s_t))
        d_ref[start : start + size, :] = (jnp.concatenate(parts, 0).T * factor).astype(jnp.bfloat16)
        at += size
    dki[...] = (aki[...] * factor).astype(jnp.bfloat16)
    dkt[...] = (akt[...] * factor).astype(jnp.bfloat16)
    dvi[...] = avi[...].astype(jnp.bfloat16)
    dvt[...] = avt[...].astype(jnp.bfloat16)


def kind_specs(rows):
    return [pl.BlockSpec((None, rows, 2 * HEAD), partial(lambda k, p: (k, 0, p), k)) for k in range(3)]


def attend(qkv_img, qkv_txt, block, valid):
    n_i, n_t, inner = qkv_img.shape[1], qkv_txt.shape[1], qkv_img.shape[2]
    pairs = inner // (2 * HEAD)
    col = lambda rows: pl.BlockSpec((rows, 2 * HEAD), lambda p: (0, p))
    return pl.pallas_call(
        partial(attend_kernel, block, valid),
        grid=(pairs,),
        in_specs=kind_specs(n_i) + kind_specs(n_t),
        out_specs=[col(n_i), col(n_t), pl.BlockSpec((1, 2, n_i + n_t), lambda p: (p, 0, 0))],
        out_shape=[
            jax.ShapeDtypeStruct((n_i, inner), jnp.bfloat16),
            jax.ShapeDtypeStruct((n_t, inner), jnp.bfloat16),
            jax.ShapeDtypeStruct((pairs, 2, n_i + n_t), jnp.float32),
        ],
        compiler_params=pltpu.CompilerParams(vmem_limit_bytes=40 << 20),
        cost_estimate=pl.CostEstimate(flops=1 << 34, bytes_accessed=1 << 23, transcendentals=0),
    )(*([qkv_img] * 3 + [qkv_txt] * 3))


def attend_back(qkv_img, qkv_txt, g_img, g_txt, lse, block, valid):
    n_i, n_t, inner = qkv_img.shape[1], qkv_txt.shape[1], qkv_img.shape[2]
    pairs = inner // (2 * HEAD)
    col = lambda rows: pl.BlockSpec((rows, 2 * HEAD), lambda p: (0, p))
    return pl.pallas_call(
        partial(back_kernel, block, valid),
        grid=(pairs,),
        in_specs=kind_specs(n_i)
        + kind_specs(n_t)
        + [col(n_i), col(n_t), pl.BlockSpec((1, 2, n_i + n_t), lambda p: (p, 0, 0))],
        out_specs=[pl.BlockSpec((3, rows, 2 * HEAD), lambda p: (0, 0, p)) for rows in (n_i, n_t)],
        out_shape=[jax.ShapeDtypeStruct((3, rows, inner), jnp.bfloat16) for rows in (n_i, n_t)],
        scratch_shapes=[pltpu.VMEM((n, 2 * HEAD), jnp.float32) for n in (n_i, n_i, n_t, n_t)],
        compiler_params=pltpu.CompilerParams(vmem_limit_bytes=40 << 20),
        cost_estimate=pl.CostEstimate(flops=1 << 35, bytes_accessed=1 << 24, transcendentals=0),
    )(*([qkv_img] * 3 + [qkv_txt] * 3 + [g_img, g_txt, lse]))


def tn(a, b):
    return lax.dot_general(a, b, (((0,), (0,)), ((), ())), preferred_element_type=jnp.float32)


def norm_forward(values):
    center = jnp.mean(values, -1, keepdims=True)
    spread = jnp.mean(jnp.square(values - center), -1, keepdims=True)
    rstd = lax.rsqrt(spread + norm_eps)
    return ((values - center) * rstd, rstd)


def norm_backward(grads, hats, rstd):
    first = jnp.mean(grads, -1, keepdims=True)
    second = jnp.mean(grads * hats, -1, keepdims=True)
    return rstd * (grads - first - hats * second)


def tile(n):
    return 512 if n % 512 == 0 else 256 if n % 256 == 0 else n


def dot_kind(a, w, flip):
    return nt(a, w) if flip else nn(a, w)


def gelu_parts(x):
    c, a = math.sqrt(2.0 / math.pi), 0.044715
    square = x * x
    t = jnp.tanh(c * (x + a * (x * square)))
    slope = 0.5 * (1.0 + t) + 0.5 * x * (1.0 - t * t) * (c * (1.0 + 3.0 * a * square))
    return 0.5 * x * (1.0 + t), slope


def up_kernel(flip, at, ai, w, ht, hi, st, si):
    for s, (a, h, slope) in enumerate(((at, ht, st), (ai, hi, si))):
        value, d = gelu_parts(dot_kind(a[...], w[s], flip))
        h[...] = value.astype(jnp.bfloat16)
        slope[...] = d


def scaled_kernel(flip, at, ai, w, st, si, ot, oi):
    for s, (a, o, slope) in enumerate(((at, ot, st), (ai, oi, si))):
        o[...] = (dot_kind(a[...], w[s], flip) * slope[...]).astype(jnp.bfloat16)


def plain_kernel(flip, at, ai, w, ot, oi):
    for s, (a, o) in enumerate(((at, ot), (ai, oi))):
        o[...] = dot_kind(a[...], w[s], flip).astype(jnp.bfloat16)


def qkv_kernel(at, ai, w, ot, oi):
    for s, (a, o) in enumerate(((at, ot), (ai, oi))):
        o[0] = nt(a[...], w[s, 0]).astype(jnp.bfloat16)


def halves_kernel(flip, at, ai, w, top, own):
    for s, a in ((1, ai), (0, at)):
        half = a.shape[-2] // 2
        start = 0 if s == 1 else ai.shape[-2] // 2
        if len(a.shape) == 3:
            total = nn(a[0], w[s, 0])
            for k in range(1, a.shape[0]):
                total = total + nn(a[k], w[s, k])
        else:
            total = dot_kind(a[...], w[s], flip)
        own[start : start + half, :] = total[:half]
        top[start : start + half, :] = total[half:].astype(jnp.bfloat16)


def over_columns(kernel, operands, w, flip, extra, outs, columns):
    step = tile(columns)
    whole = lambda v: pl.BlockSpec(v.shape, lambda n: (0,) * v.ndim)
    if w.ndim == 4:
        w_spec = pl.BlockSpec(w.shape[:3] + (step,), lambda n: (0, 0, 0, n))
    elif flip:
        w_spec = pl.BlockSpec((2, step, w.shape[2]), lambda n: (0, n, 0))
    else:
        w_spec = pl.BlockSpec((2, w.shape[1], step), lambda n: (0, 0, n))
    by_tile = lambda v: pl.BlockSpec((v.shape[0], step), lambda n: (0, n))
    return pl.pallas_call(
        kernel,
        grid=(columns // step,),
        in_specs=[whole(v) for v in operands] + [w_spec] + [by_tile(v) for v in extra],
        out_specs=[by_tile(v) for v in outs],
        out_shape=outs,
        compiler_params=pltpu.CompilerParams(vmem_limit_bytes=40 << 20),
        cost_estimate=pl.CostEstimate(flops=1 << 33, bytes_accessed=1 << 23, transcendentals=0),
    )(*operands, w, *extra)


def shaped(rows, columns, kind):
    return jax.ShapeDtypeStruct((rows, columns), kind)


def up_and_slope(at, ai, w):
    n = w.shape[2]
    kinds = [jnp.bfloat16, jnp.bfloat16, jnp.float32, jnp.float32]
    rows = [at.shape[0], ai.shape[0]] * 2
    outs = [shaped(r, n, k) for r, k in zip(rows, kinds)]
    return over_columns(partial(up_kernel, False), [at, ai], w, False, [], outs, n)


def scaled(at, ai, w, st, si):
    outs = [shaped(v.shape[0], w.shape[2], jnp.bfloat16) for v in (at, ai)]
    return over_columns(partial(scaled_kernel, False), [at, ai], w, False, [st, si], outs, w.shape[2])


def plain(at, ai, w):
    outs = [shaped(v.shape[0], w.shape[1], jnp.bfloat16) for v in (at, ai)]
    return over_columns(partial(plain_kernel, True), [at, ai], w, True, [], outs, w.shape[1])


def halves(at, ai, w, flip):
    columns = w.shape[1] if flip else w.shape[-1]
    rows = (at.shape[-2] + ai.shape[-2]) // 2
    outs = [shaped(rows, columns, jnp.bfloat16), shaped(rows, columns, jnp.float32)]
    return over_columns(partial(halves_kernel, flip), [at, ai], w, flip, [], outs, columns)


def project_qkv(at, ai, w):
    inner = w.shape[2]
    whole = lambda v: pl.BlockSpec(v.shape, lambda n: (0, 0))
    outs = [jax.ShapeDtypeStruct((3, v.shape[0], inner), jnp.bfloat16) for v in (at, ai)]
    return pl.pallas_call(
        qkv_kernel,
        grid=(3,),
        in_specs=[whole(at), whole(ai), pl.BlockSpec((2, 1) + w.shape[2:], lambda n: (0, n, 0, 0))],
        out_specs=[pl.BlockSpec((1,) + v.shape[1:], lambda n: (n, 0, 0)) for v in outs],
        out_shape=outs,
        compiler_params=pltpu.CompilerParams(vmem_limit_bytes=40 << 20),
        cost_estimate=pl.CostEstimate(flops=1 << 33, bytes_accessed=1 << 23, transcendentals=0),
    )(at, ai, w)


def outer_kernel(n, *refs):
    left, right, out = refs[: 2 * n], refs[2 * n : 4 * n], refs[-1]
    for s in range(2):
        total = None
        for j in range(n):
            a = left[s * n + j]
            a = a[0] if len(a.shape) == 3 else a[...]
            term = tn(a, right[s * n + j][...])
            total = term if total is None else total + term
        if len(out.shape) == 3:
            out[s] = total.astype(jnp.bfloat16)
            continue
        ranks = out.shape[1]
        part = HEAD // ranks
        for p in range(ranks):
            rows = [total[h + p * part : h + (p + 1) * part] for h in range(0, total.shape[0], HEAD)]
            out[s, p] = jnp.concatenate(rows, 0).astype(jnp.bfloat16)


def outer(left_t, left_i, right_t, right_i, ranks=None, into=None, kinds=1, first=0):
    n = len(left_t)
    left, right = left_t + left_i, right_t + right_i
    columns = right[0].shape[1]
    if left[0].ndim == 3:
        step, steps = left[0].shape[2], left[0].shape[0]
        l_spec = lambda v: pl.BlockSpec((1,) + v.shape[1:], lambda m: (m, 0, 0))
    else:
        width = left[0].shape[1]
        step = 512 if width % 512 == 0 else width if width < 512 else 256
        steps = width // step
        l_spec = lambda v: pl.BlockSpec((v.shape[0], step), lambda m: (0, m))
    if ranks is None:
        shape, block, place = (2, steps * step, columns), (2, step, columns), lambda m: (0, m, 0)
    else:
        part = step // ranks
        shape, block = (2, ranks, kinds * part, columns), (2, ranks, part, columns)
        place = lambda m: (0, 0, first + m, 0)
    held = [] if into is None else [into]
    return pl.pallas_call(
        partial(outer_kernel, n),
        grid=(steps,),
        in_specs=[l_spec(v) for v in left]
        + [pl.BlockSpec(v.shape, lambda m: (0, 0)) for v in right]
        + [pl.BlockSpec(memory_space=pl.ANY)] * len(held),
        out_specs=pl.BlockSpec(block, place),
        out_shape=jax.ShapeDtypeStruct(shape, jnp.bfloat16),
        input_output_aliases={4 * n: 0} if held else {},
        compiler_params=pltpu.CompilerParams(vmem_limit_bytes=52 << 20),
        cost_estimate=pl.CostEstimate(flops=1 << 34, bytes_accessed=1 << 24, transcendentals=0),
    )(*left, *right, *held)


class Group:
    def __init__(self, size):
        self.size = size
        self.evens = [2 * k for k in range(size // 2)]
        self.odds = [2 * k + 1 for k in range(size // 2)]
        self.order = self.evens + self.odds

    def send(self, value, flip):
        return lax.ppermute(value, "tensor", [(t, t ^ flip) for t in range(self.size)])

    def gather(self, own):
        evens = [own] + [self.send(own, flip) for flip in self.evens[1:]]
        return evens + [self.send(value, 1) for value in evens]


MESH = pl.DeviceIdType.MESH


def flip_bits(index, flip, size):
    total, bit = 0, 1
    while bit < size:
        digit = lax.rem(lax.div(index, bit), 2)
        total = total + bit * ((1 - digit) if flip & bit else digit)
        bit *= 2
    return total


class Data:
    def __init__(self, size):
        self.size = size
        self.nx = math.isqrt(size // 2)
        self.nz = size // self.nx

    def send(self, value, flip):
        return lax.ppermute(value, "dp", [(p, p ^ flip) for p in range(self.size)])

    def across(self, partial_of):
        here = lax.axis_index("dp")
        rank = lambda zk, xk: flip_bits(here, zk * self.nx + xk, self.size)
        sent = lambda xk: jnp.stack([partial_of(rank(zk, xk)) for zk in range(self.nz)])
        own = [partial_of(rank(zk, 0)) for zk in range(self.nz)]
        return own, [self.send(sent(xk), xk) for xk in range(1, self.nx)]

    def along(self, own, got):
        totals = []
        for zk in range(self.nz):
            total = own[zk].astype(jnp.float32)
            for value in got:
                total = total + value[zk].astype(jnp.float32)
            totals.append(total)
        return totals[0], [self.send(totals[zk].astype(jnp.bfloat16), zk * self.nx) for zk in range(1, self.nz)]


def pass_kernel(*refs):
    pass


def gate(values, others):
    others = jax.tree.leaves(list(others))
    n = len(values)
    anywhere = pl.BlockSpec(memory_space=pl.ANY)
    return pl.pallas_call(
        pass_kernel,
        in_specs=[anywhere] * (n + len(others)),
        out_specs=[anywhere] * n,
        out_shape=[jax.ShapeDtypeStruct(v.shape, v.dtype) for v in values],
        input_output_aliases={i: i for i in range(n)},
        compiler_params=pltpu.CompilerParams(vmem_limit_bytes=1 << 20),
        cost_estimate=pl.CostEstimate(flops=1 << 10, bytes_accessed=1 << 10, transcendentals=0),
    )(*values, *others)


def after(value, *others):
    return gate([value], others)[0]


def greet(n_dp, size):
    me_d, me_t = lax.axis_index("dp"), lax.axis_index("tensor")
    barrier = pltpu.get_barrier_semaphore()
    for k in range(1, n_dp):
        pl.semaphore_signal(barrier, inc=1, device_id=(flip_bits(me_d, k, n_dp), me_t), device_id_type=MESH)
    for k in range(1, size):
        pl.semaphore_signal(barrier, inc=1, device_id=(me_d, flip_bits(me_t, k, size)), device_id_type=MESH)
    pl.semaphore_wait(barrier, n_dp + size - 2)


def to_data(n_dp, source, target, send, recv):
    me_d, me_t = lax.axis_index("dp"), lax.axis_index("tensor")
    copies = []
    for k in range(1, n_dp):
        peer = flip_bits(me_d, k, n_dp)
        copy = pltpu.make_async_remote_copy(
            src_ref=source(peer),
            dst_ref=target.at[me_d],
            send_sem=send.at[k - 1],
            recv_sem=recv.at[k - 1],
            device_id=(peer, me_t),
            device_id_type=MESH,
        )
        copy.start()
        copies.append(copy)
    return copies


def to_tensor(size, source, target, send, recv):
    me_d, me_t = lax.axis_index("dp"), lax.axis_index("tensor")
    copies = []
    for k in range(1, size):
        peer = flip_bits(me_t, k, size)
        copy = pltpu.make_async_remote_copy(
            src_ref=source(peer),
            dst_ref=target.at[me_t],
            send_sem=send.at[k - 1],
            recv_sem=recv.at[k - 1],
            device_id=(me_d, peer),
            device_id_type=MESH,
        )
        copy.start()
        copies.append(copy)
    return copies


def finish(copies):
    for copy in copies:
        copy.wait()


def mod_kernel(n_dp, size, cond, w, mod_out, act_out, conds, parts, got, own, sd1, rd1, sd2, rd2, st, rt):
    me_d, me_t = lax.axis_index("dp"), lax.axis_index("tensor")
    rows, part, columns = conds.shape[1], w.shape[1], w.shape[2] // 2
    greet(n_dp, size)
    copies = to_data(n_dp, lambda peer: cond.at[peer], conds, sd1, rd1)
    conds[me_d] = cond[me_d]
    finish(copies)
    value = conds[...].reshape(n_dp * rows, conds.shape[2])[:, :part]
    act = (value * jax.nn.sigmoid(value)).astype(jnp.bfloat16)
    act_out[...] = act
    place = lax.rem(lax.broadcasted_iota(jnp.int32, (n_dp * rows, 1), 0), rows)
    first = lax.rem(place, rows // 2) < rows // 4
    mixed = [
        jnp.where(first, nn(act, w[0, :, cut]), nn(act, w[1, :, cut]))
        for cut in (slice(0, columns), slice(columns, 2 * columns))
    ]
    mixed = jnp.where(place < rows // 2, mixed[0], mixed[1])
    parts[...] = mixed.reshape(n_dp, rows, columns)
    copies = to_data(n_dp, lambda peer: parts.at[peer], got, sd2, rd2)
    got[me_d] = parts[me_d]
    finish(copies)
    total = got[0]
    for p in range(1, n_dp):
        total = total + got[p]
    own[...] = total
    copies = to_tensor(size, lambda peer: own, mod_out, st, rt)
    mod_out[me_t] = total
    finish(copies)


def mod_forward(n_dp, size, cond, w_mod):
    slots, width = cond.shape
    part, columns = w_mod.shape[1:]
    rows, lanes = 4 * slots, -(-part // 128) * 128
    laid = cond.astype(jnp.float32).reshape(slots, n_dp, part).transpose(1, 0, 2)
    laid = jnp.concatenate([laid, laid, laid, laid], 1)
    laid = jnp.pad(laid, ((0, 0), (0, 0), (0, lanes - part)))
    dma = pltpu.SemaphoreType.DMA
    return pl.pallas_call(
        partial(mod_kernel, n_dp, size),
        in_specs=[pl.BlockSpec(memory_space=pltpu.VMEM)] * 2,
        out_specs=[pl.BlockSpec(memory_space=pltpu.VMEM)] * 2,
        out_shape=[
            jax.ShapeDtypeStruct((size, rows, columns // 2), jnp.float32),
            jax.ShapeDtypeStruct((n_dp * rows, part), jnp.bfloat16),
        ],
        scratch_shapes=[
            pltpu.VMEM((n_dp, rows, lanes), jnp.float32),
            pltpu.VMEM((n_dp, rows, columns // 2), jnp.float32),
            pltpu.VMEM((n_dp, rows, columns // 2), jnp.float32),
            pltpu.VMEM((rows, columns // 2), jnp.float32),
            dma((n_dp - 1,)), dma((n_dp - 1,)), dma((n_dp - 1,)), dma((n_dp - 1,)),
            dma((size - 1,)), dma((size - 1,)),
        ],
        compiler_params=pltpu.CompilerParams(
            collective_id=0, has_side_effects=True, vmem_limit_bytes=40 << 20
        ),
        cost_estimate=pl.CostEstimate(flops=1 << 33, bytes_accessed=1 << 21, transcendentals=0),
    )(laid, w_mod)


def mod_back_kernel(n_dp, size, terms, lost, act, w, grad, cond_out, loss_out, halves, sums, every, cparts, cgot, cfull,
                    lhalves, lsums, levery, st1, rt1, sd1, rd1, sd2, rd2, st2, rt2, st3, rt3, sd3, rd3):
    me_d, me_t = lax.axis_index("dp"), lax.axis_index("tensor")
    rows, columns = terms.shape[1:]
    part = w.shape[1]
    greet(n_dp, size)
    copies = to_tensor(size, lambda peer: terms.at[peer], halves, st1, rt1)
    copies += to_tensor(size, lambda peer: lost, lhalves, st3, rt3)
    halves[me_t] = terms[me_t]
    lhalves[me_t] = lost[...]
    finish(copies)
    total, loss = halves[0], lhalves[0]
    for t in range(1, size):
        total, loss = total + halves[t], loss + lhalves[t]
    sums[...] = total
    lsums[...] = loss
    copies = to_data(n_dp, lambda peer: sums, every, sd1, rd1)
    copies += to_data(n_dp, lambda peer: lsums, levery, sd3, rd3)
    every[me_d] = total
    levery[me_d] = loss
    finish(copies)
    loss = levery[0]
    for p in range(1, n_dp):
        loss = loss + levery[p]
    loss_out[...] = loss
    dmod = every[...].reshape(n_dp * rows, columns).astype(jnp.bfloat16)
    place = lax.rem(lax.broadcasted_iota(jnp.int32, (n_dp * rows, 1), 0), rows)
    quarter = rows // 4
    cuts = (slice(0, columns), slice(columns, 2 * columns))
    back = [nt(dmod, w[s, :, cut]) for cut in cuts for s in range(2)]
    mixed = back[0]
    for n in range(1, 4):
        mixed = jnp.where(place < n * quarter, mixed, back[n])
    cparts[:, :, :part] = mixed.reshape(n_dp, rows, part)
    copies = to_data(n_dp, lambda peer: cparts.at[peer], cgot, sd2, rd2)
    cgot[me_d] = cparts[me_d]
    for n in range(4):
        mask = (place >= n * quarter) & (place < (n + 1) * quarter)
        picked = jnp.where(mask, act[...], jnp.zeros((), jnp.bfloat16))
        grad[n % 2, :, cuts[n // 2]] = tn(picked, dmod)
    finish(copies)
    copies = to_tensor(size, lambda peer: cgot, cfull, st2, rt2)
    cfull[me_t] = cgot[...]
    finish(copies)
    full = cfull[0]
    for t in range(1, size):
        full = full + cfull[t]
    cond_out[...] = full


def mod_backward(n_dp, size, terms, lost, act, w_mod):
    rows, columns = terms.shape[1:]
    part = w_mod.shape[1]
    lanes = -(-part // 128) * 128
    dma = pltpu.SemaphoreType.DMA
    f32 = jnp.float32
    return pl.pallas_call(
        partial(mod_back_kernel, n_dp, size),
        in_specs=[pl.BlockSpec(memory_space=pltpu.VMEM)] * 4,
        out_specs=[pl.BlockSpec(memory_space=pltpu.VMEM)] * 3,
        out_shape=[
            jax.ShapeDtypeStruct(w_mod.shape, f32),
            jax.ShapeDtypeStruct((n_dp, rows, lanes), f32),
            jax.ShapeDtypeStruct((8, 128), f32),
        ],
        scratch_shapes=[
            pltpu.VMEM((size, rows, columns), f32),
            pltpu.VMEM((rows, columns), f32),
            pltpu.VMEM((n_dp, rows, columns), f32),
            pltpu.VMEM((n_dp, rows, lanes), f32),
            pltpu.VMEM((n_dp, rows, lanes), f32),
            pltpu.VMEM((size, n_dp, rows, lanes), f32),
            pltpu.VMEM((size, 8, 128), f32),
            pltpu.VMEM((8, 128), f32),
            pltpu.VMEM((n_dp, 8, 128), f32),
            dma((size - 1,)), dma((size - 1,)),
            dma((n_dp - 1,)), dma((n_dp - 1,)), dma((n_dp - 1,)), dma((n_dp - 1,)),
            dma((size - 1,)), dma((size - 1,)),
            dma((size - 1,)), dma((size - 1,)), dma((n_dp - 1,)), dma((n_dp - 1,)),
        ],
        compiler_params=pltpu.CompilerParams(
            collective_id=1, has_side_effects=True, vmem_limit_bytes=40 << 20
        ),
        cost_estimate=pl.CostEstimate(flops=1 << 33, bytes_accessed=1 << 21, transcendentals=0),
    )(terms, lost, act, w_mod)


def on_device(
    data,
    group,
    image,
    text,
    cond,
    teacher_image,
    teacher_text,
    grad_image,
    grad_text,
    live,
    w_mod,
    w_qkv,
    w_out,
    w_up,
    w_down,
):
    slots, width = cond.shape
    rows_i, rows_t = image.shape[1], text.shape[1]
    pad_t = -(-rows_t // 8) * 8
    size = group.size
    n_dp = data.size
    heads = w_qkv.shape[2]
    odd = heads % 2

    wide = jnp.concatenate([w_qkv, w_out[:, None]], 1)
    f_wide = lax.all_gather(wide, "dp", axis=3, tiled=True)
    f_up = lax.all_gather(w_up, "dp", axis=1, tiled=True)
    f_down = lax.all_gather(w_down, "dp", axis=1, tiled=True)
    if odd:
        f_wide = jnp.pad(f_wide, ((0, 0), (0, 0), (0, odd), (0, 0), (0, 0)))
    f_wide = f_wide.reshape(2, 4, -1, width)
    f_qkv, f_out = f_wide[:, :3], f_wide[:, 3]

    mod_all, act_all = mod_forward(n_dp, size, cond, w_mod)
    mods = jnp.stack(
        [
            jnp.stack(
                [
                    jnp.stack([mod_all[:, (h * 2 + s) * slots + j] for h in range(2)], 1).reshape(6, width)
                    for s in range(2)
                ]
            )
            for j in range(slots)
        ]
    )

    is_image = (lax.broadcasted_iota(jnp.int32, (rows_i + pad_t, 1), 0) < rows_i)
    is_real = (lax.broadcasted_iota(jnp.int32, (rows_i + pad_t, 1), 0) < rows_i + rows_t)

    def merged(img, txt, j):
        return jnp.concatenate([img[j], jnp.pad(txt[j], ((0, pad_t - rows_t), (0, 0)))], 0)

    def pick(j, span):
        return jnp.where(is_image, mods[j, 1, span][None], mods[j, 0, span][None])

    def token_sums(values):
        return jnp.stack([jnp.sum(values[rows_i:], 0), jnp.sum(values[:rows_i], 0)])

    def spread(blocks):
        return (
            jnp.concatenate([b[:rows_i] for b in blocks], 0),
            jnp.concatenate([b[rows_i:] for b in blocks], 0),
        )

    half_i = size // 2 * rows_i

    def scatter_begin(rows_txt, rows_img, w, flip):
        top, own = halves(rows_txt, rows_img, w, flip)
        got = group.send(top, 1)
        blocks = []
        for k in range(size // 2):
            cuts = (slice(k * rows_i, (k + 1) * rows_i), slice(half_i + k * pad_t, half_i + (k + 1) * pad_t))
            blocks.append(jnp.concatenate([own[cut] + got[cut].astype(jnp.float32) for cut in cuts], 0))
        blocks = [blocks[0]] + [block.astype(jnp.bfloat16) for block in blocks[1:]]
        return blocks, [group.send(blocks[k], 2 * k) for k in range(1, size // 2)]

    def scatter_end(started, *others):
        blocks, got = started
        total = blocks[0]
        for value in got:
            total = total + after(value, *others).astype(jnp.float32)
        return total

    def gather_begin(own):
        return [own], [group.send(own, flip) for flip in group.evens[1:]]

    def gather_end(started, *others):
        own, got = started
        evens = own + [after(value, *others) for value in got]
        odds = group.send(jnp.concatenate(evens, 0), 1)
        return spread(evens + [odds[k : k + rows_i + pad_t] for k in range(0, odds.shape[0], rows_i + pad_t)])

    count = 3.0 * (n_dp // 2) * size * (rows_i + rows_t)

    slot = [dict() for j in range(slots)]
    for j, v in enumerate(slot):
        v["x"] = merged(image, text, j).astype(jnp.float32)
        v["hat1"], v["rstd1"] = norm_forward(v["x"])
        h1 = (v["hat1"] * (1.0 + pick(j, 1)) + pick(j, 0)).astype(jnp.bfloat16)
        v["go"] = gather_begin(h1)
    for j, v in enumerate(slot):
        v["h1_i"], v["h1_t"] = gather_end(v["go"], slot[-1]["go"][0])
    for j, v in enumerate(slot):
        if j:
            v["h1_i"] = after(v["h1_i"], slot[j - 1]["att_i"])
        v["qkv_t"], v["qkv_i"] = project_qkv(v["h1_t"], v["h1_i"], f_qkv)
        v["att_i"], v["att_t"], v["lse"] = attend(v["qkv_i"], v["qkv_t"], pad_t, rows_t)
    for j, v in enumerate(slot):
        v["go"] = scatter_begin(v["att_t"], v["att_i"], f_out, False)
    for j, v in enumerate(slot):
        v["y"] = scatter_end(v["go"], slot[-1]["go"][0])
        v["mid"] = v["x"] + pick(j, 2) * v["y"]
        v["hat2"], v["rstd2"] = norm_forward(v["mid"])
        h2 = (v["hat2"] * (1.0 + pick(j, 4)) + pick(j, 3)).astype(jnp.bfloat16)
        v["go"] = gather_begin(h2)
    for j, v in enumerate(slot):
        v["h2_i"], v["h2_t"] = gather_end(v["go"], slot[-1]["go"][0])
    for j, v in enumerate(slot):
        if j:
            v["h2_i"] = after(v["h2_i"], slot[j - 1]["hid_i"])
        v["hid_t"], v["hid_i"], v["slope_t"], v["slope_i"] = up_and_slope(v["h2_t"], v["h2_i"], f_up)
    f_down = after(f_down, slot[-1]["hid_i"])
    for j, v in enumerate(slot):
        v["go"] = scatter_begin(v["hid_t"], v["hid_i"], f_down, True)
    for j, v in enumerate(slot):
        v["m"] = scatter_end(v["go"], slot[j - 1]["go"][0])
        out = v["mid"] + pick(j, 5) * v["m"]
        mask = jnp.where(is_real, live[j].astype(jnp.float32), 0.0)
        err = mask * (out - merged(teacher_image, teacher_text, j).astype(jnp.float32))
        v["loss"] = jnp.sum(err * err)
        v["cot"] = mask * merged(grad_image, grad_text, j).astype(jnp.float32) + 2.0 * err
        v["dgate2"] = token_sums(v["cot"] * v["m"])
        dm = (v["cot"] * pick(j, 5)).astype(jnp.bfloat16)
        v["go"] = gather_begin(dm)
    for j, v in enumerate(slot):
        v["dm_i"], v["dm_t"] = gather_end(v["go"], slot[-1]["go"][0])

    here = lax.axis_index("dp")

    both = lambda a, b, *dealt: outer(*([v[name + e] for v in slot] for name in (a, b) for e in ("_t", "_i")), *dealt)

    def reduced(grads):
        return lax.psum_scatter(grads.reshape(2, -1, grads.shape[-1]), "dp", scatter_dimension=1, tiled=True)

    g_down = both("dm", "hid")
    done_down = reduced(g_down)
    for j, v in enumerate(slot):
        v["dm_i"] = after(v["dm_i"], g_down if j == 0 else slot[j - 1]["go"][0])
        v["dpre_t"], v["dpre_i"] = scaled(v["dm_t"], v["dm_i"], f_down, v["slope_t"], v["slope_i"])
        v["go"] = scatter_begin(v["dpre_t"], v["dpre_i"], f_up, True)
    g_up = both("h2", "dpre")
    done_up = reduced(g_up)
    for j, v in enumerate(slot):
        v["dh2"] = scatter_end(v["go"], g_up, slot[j - 1]["go"][0])
        v["dshift2"] = token_sums(v["dh2"])
        v["dscale2"] = token_sums(v["dh2"] * v["hat2"])
        v["dmid"] = v["cot"] + norm_backward(v["dh2"] * (1.0 + pick(j, 4)), v["hat2"], v["rstd2"])
        v["dgate1"] = token_sums(v["dmid"] * v["y"])
        dy = (v["dmid"] * pick(j, 2)).astype(jnp.bfloat16)
        v["go"] = gather_begin(dy)
    for j, v in enumerate(slot):
        v["dy_i"], v["dy_t"] = gather_end(v["go"], slot[-1]["go"][0])
    slot[-1]["dy_i"] = after(slot[-1]["dy_i"], done_down)
    g_out = both("att", "dy", n_dp)
    out_own, out_got = data.across(lambda rank: lax.dynamic_index_in_dim(g_out, rank, 1, keepdims=False))
    for j, v in enumerate(slot):
        v["dy_i"] = after(v["dy_i"], g_out) if j == 0 else after(v["dy_i"], slot[j - 1]["dqkv_i"])
        g_t, g_i = plain(v["dy_t"], v["dy_i"], f_out)
        v["dqkv_i"], v["dqkv_t"] = attend_back(v["qkv_i"], v["qkv_t"], g_i, g_t, v["lse"], pad_t, rows_t)
        if j == 0:
            out_got = [after(value, v["dqkv_i"]) for value in out_got]
    g_wide = both("dqkv", "h1", n_dp, None, 3, 0)
    done_qkv = reduced(g_wide)
    out_total, out_got = data.along(out_own, out_got)
    for j, v in enumerate(slot):
        v["dqkv_i"] = after(v["dqkv_i"], g_wide)
        v["go"] = scatter_begin(v["dqkv_t"], v["dqkv_i"], f_qkv, False)
    for j, v in enumerate(slot):
        v["dh1"] = scatter_end(v["go"], slot[-1]["go"][0])
    grad_i, grad_t, terms = [], [], []
    for j in range(slots):
        v = slot[j]
        dshift1 = token_sums(v["dh1"])
        dscale1 = token_sums(v["dh1"] * v["hat1"])
        back = v["dmid"] + norm_backward(v["dh1"] * (1.0 + pick(j, 1)), v["hat1"], v["rstd1"])
        grad_i.append(back[:rows_i])
        grad_t.append(back[rows_i : rows_i + rows_t])
        terms.append(
            jnp.stack([dshift1, dscale1, v["dgate1"], v["dshift2"], v["dscale2"], v["dgate2"]], 1)
        )
    lost = jnp.full((8, 128), sum(v["loss"] for v in slot))
    laid = jnp.stack(terms, 1).reshape(2 * slots, size, 2, -1).transpose(1, 2, 0, 3)
    laid = laid.reshape(size, 4 * slots, -1)
    laid = after(laid, done_up)
    done_mod, cond_rows, loss_rows = mod_backward(n_dp, size, laid, lost, act_all, w_mod)
    loss = loss_rows[0, 0] / (count * width)
    cond_rows = cond_rows[:, :, : w_mod.shape[1]]
    cond_total = jnp.sum(cond_rows.reshape(n_dp, 4, slots, -1), 1).transpose(1, 0, 2).reshape(slots, width)
    unused_value, silu_pull = jax.vjp(jax.nn.silu, cond.astype(jnp.float32))
    grad_cond = silu_pull(cond_total)[0]
    done_down = done_down.astype(jnp.float32)
    done_up = done_up.astype(jnp.float32)
    done_qkv = done_qkv.astype(jnp.float32).reshape(2, 3, heads + odd, -1, width)
    done_out = out_total + sum(after(value, slot[-1]["go"][0]).astype(jnp.float32) for value in out_got)
    done_out = done_out.reshape(2, heads + odd, -1, width)
    if odd:
        done_qkv, done_out = done_qkv[:, :, :heads], done_out[:, :heads]
    return (
        loss,
        done_mod,
        done_qkv,
        done_out,
        done_up,
        done_down,
        jnp.stack(grad_i),
        jnp.stack(grad_t),
        grad_cond,
    )


def solution(mesh):
    return jax.shard_map(
        partial(on_device, Data(mesh.shape["dp"]), Group(mesh.shape["tensor"])),
        mesh=mesh,
        in_specs=(
            P("dp", "tensor", None),
            P("dp", "tensor", None),
            P("dp", None),
            P("dp", "tensor", None),
            P("dp", "tensor", None),
            P("dp", "tensor", None),
            P("dp", "tensor", None),
            P("dp"),
            P(None, "dp", "tensor"),
            P(None, None, "tensor", "dp", None),
            P(None, "tensor", "dp", None),
            P(None, "dp", "tensor"),
            P(None, "dp", "tensor"),
        ),
        out_specs=(
            P(),
            P(None, "dp", "tensor"),
            P(None, None, "tensor", "dp", None),
            P(None, "tensor", "dp", None),
            P(None, "dp", "tensor"),
            P(None, "dp", "tensor"),
            P("dp", "tensor", None),
            P("dp", "tensor", None),
            P("dp", None),
        ),
        check_vma=False,
    )
```
